32 devices in a mesh: aa: 4 (over y, core), ba: 8 (over z, x).
Axes of the slice: x: 2, y: 2, z: 4, core: 2. Of those that a mesh axis runs over, the one named last changes fastest.
Arguments:
- grid_nodes: bfloat16 [32768, 512], P(('aa', 'ba')), may hold values from -6 to 6
- mesh_nodes: bfloat16 [6144, 512], P(('aa', 'ba')), may hold values from -6 to 6
- owned_nodes: int32 [32], P(('aa', 'ba')), may hold values from 96 to 192, as said below
- grid_rim: int32 [32, 8, 128], P(('aa', 'ba')), may hold values from 0 to 1023
- mesh_rim: int32 [32, 8, 16], P(('aa', 'ba')), may hold values from 0 to 95
- long_send: int32 [32, 32, 8], P(('aa', 'ba')), may hold values from 0 to 15
- g2m_edges: int32 [32, 2, 3072], P(('aa', 'ba')), may hold values from 0 to 2047, as said below
- short_edges: int32 [32, 2, 1536], P(('aa', 'ba')), may hold values from 0 to 319, as said below
- long_edges: int32 [32, 2, 1536], P(('aa', 'ba')), may hold values from 0 to 447, as said below
- m2g_edges: int32 [32, 3, 1024], P(('aa', 'ba')), may hold values from 0 to 319, as said below
- edge_first: bfloat16 [4, 2, 512, 512], replicated, may hold values from -0.1875 to 0.1875
- edge_second: bfloat16 [4, 512, 512], replicated, may hold values from -0.25 to 0.25
- edge_bias: float32 [4, 512], replicated, may hold values from -3 to 3
- edge_gain: float32 [4, 512], replicated, may hold values from 0.5 to 2
- node_first: bfloat16 [4, 2, 512, 512], replicated, may hold values from -0.1875 to 0.1875
- node_second: bfloat16 [4, 512, 512], replicated, may hold values from -0.25 to 0.25
- node_bias: float32 [4, 512], replicated, may hold values from -3 to 3
- node_gain: float32 [4, 512], replicated, may hold values from 0.5 to 2
Outputs:
- grid_out: bfloat16 [32768, 512], P(('aa', 'ba'))
- mesh_out: bfloat16 [6144, 512], P(('aa', 'ba'))
The draws below stay inside these ranges and needn't reach their ends.
Inputs may be any that keep to these rules, and one draw needn't show every extreme that they name: `owned_nodes`: some device owns 192 nodes in every draw. `g2m_edges`: row 0 holds senders, row 1 receivers. On device d the first 16 * owned_nodes[d] slots are used, with receivers below owned_nodes[d]; the others have receiver 192. Senders at or above 1024 never name a direction with a_k = -1 on band i = 0 or a_k = 1 on band i = 3. `short_edges`: row 0 holds senders, row 1 receivers. On device d the first 8 * owned_nodes[d] slots are used, with receivers below owned_nodes[d]; the others have receiver 192. Senders below 192 are below owned_nodes[d]; senders at or above 192 never name a direction with a_k = -1 on band 0 or a_k = 1 on band 4 - 1. `long_edges`: row 0 holds senders, row 1 receivers. On device d the first 8 * owned_nodes[d] slots are used, with receivers below owned_nodes[d]; the others have receiver 192. Senders below 192 are below owned_nodes[d]. `m2g_edges`: senders below 192 are below owned_nodes[d]; senders at or above 192 never name a direction with a_k = -1 on band 0 or a_k = 1 on band 4 - 1.
All inputs are finite; a program needn't handle non-finite values.
Results may differ from the reference program's by a relative error of at most 0.013.
Values may be sent and summed in bfloat16 or wider, within the bound.
No kernel may reach another device: no remote copies, remote signals or barrier semaphores. Data moves between devices by JAX's collectives and lax.ppermute only.
A program may use at most 128 MiB of HBM per device.

```python
import math
import jax
import jax.numpy as jnp
from jax import lax

D = 512
G_DEV = 1024
M_DEV = 192
GB = 128
HB = 16
KL = 8
CS = 16
G2M_PER = 16
SHORT_PER = 8
LONG_PER = 8
GRID = 32768
MESH_SLOTS = 6144
N_AA = 4
N_BA = 8
DEVICES = 32


def owned_counts(key):
    base = jax.random.fold_in(key, 7001)
    devices = N_AA * N_BA
    counts = jax.random.randint(jax.random.fold_in(base, 1), (devices,), M_DEV // 2, M_DEV + 1)
    busiest = jax.random.randint(jax.random.fold_in(base, 2), (), 0, devices)
    counts = jnp.where(jnp.arange(devices) == busiest, M_DEV, counts)
    return counts.astype(jnp.int32)


def rim_senders(key, shape, local_high, local_count, block_depth):
    devices = N_AA * N_BA
    row_first = (jnp.arange(devices, dtype=jnp.int32) // N_BA).reshape((devices,) + (1,) * (len(shape) - 1))
    choose = jax.random.randint(jax.random.fold_in(key, 1), shape, 0, 2) == 0
    local_rows = jax.random.randint(jax.random.fold_in(key, 2), shape, 0, local_high)
    direction = jax.random.randint(jax.random.fold_in(key, 3), shape, 0, 8)
    direction = jnp.where((row_first == 0) & (direction < 3), direction + 3, direction)
    direction = jnp.where((row_first == N_AA - 1) & (direction >= 5), direction - 3, direction)
    position = jax.random.randint(jax.random.fold_in(key, 4), shape, 0, block_depth)
    return jnp.where(choose, local_rows, local_count + direction * block_depth + position).astype(jnp.int32)


def edge_targets(key, salted, per_slot):
    counts = owned_counts(key)
    devices = N_AA * N_BA
    slot_count = per_slot * M_DEV
    alive = jnp.arange(slot_count)[None, :] < counts[:, None] * per_slot
    chosen = jax.random.randint(salted, (devices, slot_count), 0, counts[:, None])
    return jnp.where(alive, chosen, M_DEV).astype(jnp.int32)


def draw_owned_nodes(key, part):
    return owned_counts(key)


def draw_g2m_edges(key, part):
    devices = N_AA * N_BA
    senders = rim_senders(jax.random.fold_in(key, 11), (devices, G2M_PER * M_DEV), G_DEV, G_DEV, GB)
    targets = edge_targets(key, jax.random.fold_in(key, 12), G2M_PER)
    return jnp.stack([senders, targets], 1)


def draw_short_edges(key, part):
    devices = N_AA * N_BA
    counts = owned_counts(key)
    senders = rim_senders(jax.random.fold_in(key, 21), (devices, SHORT_PER * M_DEV), counts[:, None], M_DEV, HB)
    targets = edge_targets(key, jax.random.fold_in(key, 22), SHORT_PER)
    return jnp.stack([senders, targets], 1)


def draw_long_edges(key, part):
    devices = N_AA * N_BA
    counts = owned_counts(key)
    shape = (devices, LONG_PER * M_DEV)
    choose = jax.random.randint(jax.random.fold_in(key, 31), shape, 0, 4) == 0
    local_rows = jax.random.randint(jax.random.fold_in(key, 32), shape, 0, counts[:, None])
    remote = M_DEV + jax.random.randint(jax.random.fold_in(key, 33), shape, 0, devices * KL)
    senders = jnp.where(choose, local_rows, remote).astype(jnp.int32)
    targets = edge_targets(key, jax.random.fold_in(key, 34), LONG_PER)
    return jnp.stack([senders, targets], 1)


def draw_m2g_edges(key, part):
    devices = N_AA * N_BA
    counts = owned_counts(key)
    return rim_senders(jax.random.fold_in(key, 41), (devices, 3, G_DEV), counts[:, None, None], M_DEV, HB)


def draw_grid_nodes(key, part):
    second_key = jax.random.fold_in(key, 52)
    values = jnp.clip(jax.random.normal(second_key, (GRID, D)), -6.0, 6.0)
    return values.astype(jnp.bfloat16)


def set_ends(values, key, low, top_value):
    longest = values.shape.index(max(values.shape))
    spots = []
    for shift in (0, 1):
        where = [jax.random.randint(jax.random.fold_in(key, axis), (), 0, length) for axis, length in enumerate(values.shape)]
        where[longest] = (where[longest] + shift) % values.shape[longest]
        spots.append(tuple(where))
    return values.at[spots[0]].set(low).at[spots[1]].set(top_value)


def block_levels(rng, extent, pieces, smallest, largest):
    factor_of = 1.0
    for dim, shards_of in pieces:
        heights = jax.random.uniform(jax.random.fold_in(jax.random.fold_in(rng, 6), dim), (shards_of,), jnp.float32, smallest / len(pieces), largest / len(pieces))
        factor_of = factor_of * jnp.repeat(jnp.exp(heights), extent[dim] // shards_of).reshape((-1,) + (1,) * (len(extent) - 1 - dim))
    return factor_of


def gaussian(stream_key, extent, scale, most, split=(), kind=jnp.bfloat16):
    values = jax.random.normal(stream_key, extent, jnp.float32) * scale
    if len(split) > 0:
        values = block_levels(stream_key, extent, split, -0.22, 0.18) * values
    return jnp.clip(values, min=-most, max=most).astype(kind)


def setup_inputs(seed: int = 0) -> dict:
    seeds = jax.random.split(jax.random.key(seed), 19)
    grid_nodes = draw_grid_nodes(jax.random.fold_in(seeds[18], 71), 0)
    mesh_nodes = gaussian(seeds[1], (MESH_SLOTS, D), 1.0, 6.0, ((0, 32),))
    owned_nodes = draw_owned_nodes(jax.random.fold_in(seeds[18], 71), 0)
    grid_rim = set_ends(jax.random.randint(seeds[3], (DEVICES, 8, GB), 0, G_DEV), jax.random.fold_in(seeds[3], 1), 0, G_DEV - 1).astype(jnp.int32)
    mesh_rim = set_ends(jax.random.randint(seeds[4], (DEVICES, 8, HB), 0, M_DEV // 2), jax.random.fold_in(seeds[4], 1), 0, (M_DEV // 2) - 1).astype(jnp.int32)
    long_send = set_ends(jax.random.randint(seeds[5], (DEVICES, DEVICES, KL), 0, CS), jax.random.fold_in(seeds[5], 1), 0, CS - 1).astype(jnp.int32)
    g2m_edges = draw_g2m_edges(jax.random.fold_in(seeds[18], 71), 0)
    short_edges = draw_short_edges(jax.random.fold_in(seeds[18], 71), 0)
    long_edges = draw_long_edges(jax.random.fold_in(seeds[18], 71), 0)
    m2g_edges = draw_m2g_edges(jax.random.fold_in(seeds[18], 71), 0)
    edge_first = gaussian(seeds[10], (4, 2, D, D), (2 * D) ** -0.5, 0.1875)
    edge_second = gaussian(seeds[11], (4, D, D), D ** -0.5, 0.25)
    edge_bias = gaussian(seeds[12], (4, D), 0.5, 3.0, (), jnp.float32)
    edge_gain = jnp.clip(jnp.exp(jax.random.uniform(seeds[13], (4, D), jnp.float32, math.log(0.5), math.log(2.0))), 0.5, 2.0)
    node_first = gaussian(seeds[14], (4, 2, D, D), (2 * D) ** -0.5, 0.1875)
    node_second = gaussian(seeds[15], (4, D, D), D ** -0.5, 0.25)
    node_bias = gaussian(seeds[16], (4, D), 0.5, 3.0, (), jnp.float32)
    node_gain = jnp.clip(jnp.exp(jax.random.uniform(seeds[17], (4, D), jnp.float32, math.log(0.5), math.log(2.0))), 0.5, 2.0)
    return {"grid_nodes": grid_nodes, "mesh_nodes": mesh_nodes, "owned_nodes": owned_nodes, "grid_rim": grid_rim, "mesh_rim": mesh_rim, "long_send": long_send, "g2m_edges": g2m_edges, "short_edges": short_edges, "long_edges": long_edges, "m2g_edges": m2g_edges, "edge_first": edge_first, "edge_second": edge_second, "edge_bias": edge_bias, "edge_gain": edge_gain, "node_first": node_first, "node_second": node_second, "node_bias": node_bias, "node_gain": node_gain}


EPSILON = 1e-05
ALONG_FIRST = (-1, -1, -1, 0, 0, 1, 1, 1)
ALONG_SECOND = (-1, 0, 1, -1, 1, -1, 0, 1)

def layer_norm(values, norm_gain):
    average = lax.optimization_barrier(jnp.mean(values, axis=-1, keepdims=True))
    centred = values - average
    spread = lax.optimization_barrier(jnp.mean(centred * centred, axis=-1, keepdims=True))
    return centred * lax.rsqrt(spread + EPSILON) * norm_gain

def messages(source_table, senders, target_proj, biases, second, norm_gain):
    gathered = source_table[senders]
    hidden = jax.nn.silu(gathered.astype(jnp.float32) + target_proj + biases).astype(jnp.bfloat16)
    flat_hidden = hidden.reshape(-1, hidden.shape[-1])
    result = jnp.dot(flat_hidden, second, preferred_element_type=jnp.float32)
    return layer_norm(result, norm_gain).astype(jnp.bfloat16).reshape(hidden.shape)

def node_update(node_rows, totals, first_layer, biases, second, norm_gain):
    summed_input = jnp.dot(node_rows, first_layer[0], preferred_element_type=jnp.float32)
    summed_input = summed_input + jnp.dot(totals.astype(jnp.bfloat16), first_layer[1], preferred_element_type=jnp.float32) + biases
    hidden = jax.nn.silu(summed_input).astype(jnp.bfloat16)
    result = jnp.dot(hidden, second, preferred_element_type=jnp.float32)
    return (node_rows.astype(jnp.float32) + layer_norm(result, norm_gain)).astype(jnp.bfloat16)

def halo_global(senders, rim_rows, local_count):
    devices = N_AA * N_BA
    block_depth = rim_rows.shape[2]
    shape_full = (devices,) + (1,) * (senders.ndim - 1)
    device_ids = jnp.arange(devices, dtype=jnp.int32).reshape(shape_full)
    row_first = device_ids // N_BA
    row_second = device_ids % N_BA
    is_local = senders < local_count
    offset = jnp.maximum(senders - local_count, 0)
    direction = offset // block_depth
    position = offset % block_depth
    step_first = jnp.array(ALONG_FIRST, dtype=jnp.int32)[direction]
    step_second = jnp.array(ALONG_SECOND, dtype=jnp.int32)[direction]
    peer_ids = (row_first + step_first) % N_AA * N_BA + (row_second + step_second) % N_BA
    remote = rim_rows[peer_ids, 7 - direction, position]
    return jnp.where(is_local, device_ids * local_count + senders, peer_ids * local_count + remote).astype(jnp.int32)

def long_global(senders, long_send):
    devices = N_AA * N_BA
    blocks = long_send.shape[2]
    device_ids = jnp.arange(devices, dtype=jnp.int32).reshape(devices, 1)
    offset = jnp.maximum(senders - M_DEV, 0)
    peer_ids = offset // blocks
    position = offset % blocks
    remote = long_send[peer_ids, device_ids, position]
    return jnp.where(senders < M_DEV, device_ids * M_DEV + senders, peer_ids * M_DEV + remote).astype(jnp.int32)

def mesh_section(source_table, node_rows, senders, targets, section_index, weights):
    edge_first, edge_second, edge_bias, edge_gain, node_first, node_second, node_bias, node_gain = weights
    devices = N_AA * N_BA
    target_proj = jnp.dot(node_rows, edge_first[section_index, 1], preferred_element_type=jnp.float32)
    target_proj = target_proj.reshape(devices, M_DEV, D)

    def one_device(inputs):
        sender_ids, target_ids, proj_rows = inputs
        picked = proj_rows[jnp.minimum(target_ids, M_DEV - 1)]
        message_rows = messages(source_table, sender_ids, picked, edge_bias[section_index], edge_second[section_index], edge_gain[section_index])
        summed = jax.ops.segment_sum(message_rows.astype(jnp.float32), target_ids, num_segments=M_DEV + 1)
        return summed[:M_DEV]
    totals = lax.map(one_device, (senders, targets, target_proj)).reshape(-1, D)
    return node_update(node_rows, totals, node_first[section_index], node_bias[section_index], node_second[section_index], node_gain[section_index])

def reference(grid_nodes, mesh_nodes, owned_nodes, grid_rim, mesh_rim, long_send, g2m_edges, short_edges, long_edges, m2g_edges, edge_first, edge_second, edge_bias, edge_gain, node_first, node_second, node_bias, node_gain):
    weights = (edge_first, edge_second, edge_bias, edge_gain, node_first, node_second, node_bias, node_gain)
    devices = N_AA * N_BA
    grid_proj = jnp.dot(grid_nodes, edge_first[0, 0], preferred_element_type=jnp.float32).astype(jnp.bfloat16)
    senders = halo_global(g2m_edges[:, 0], grid_rim, G_DEV)
    mesh_one = mesh_section(grid_proj, mesh_nodes, senders, g2m_edges[:, 1], 0, weights)
    short_proj = jnp.dot(mesh_one, edge_first[1, 0], preferred_element_type=jnp.float32).astype(jnp.bfloat16)
    senders = halo_global(short_edges[:, 0], mesh_rim, M_DEV)
    mesh_two = mesh_section(short_proj, mesh_one, senders, short_edges[:, 1], 1, weights)
    long_proj = jnp.dot(mesh_two, edge_first[2, 0], preferred_element_type=jnp.float32).astype(jnp.bfloat16)
    senders = long_global(long_edges[:, 0], long_send)
    mesh_three = mesh_section(long_proj, mesh_two, senders, long_edges[:, 1], 2, weights)
    decode_proj = jnp.dot(mesh_three, edge_first[3, 0], preferred_element_type=jnp.float32).astype(jnp.bfloat16)
    senders = halo_global(m2g_edges, mesh_rim, M_DEV)
    target_proj = jnp.dot(grid_nodes, edge_first[3, 1], preferred_element_type=jnp.float32).reshape(devices, G_DEV, D)

    def one_tile(inputs):
        sender_ids, proj_rows = inputs
        message_rows = messages(decode_proj, sender_ids, proj_rows[None], edge_bias[3], edge_second[3], edge_gain[3])
        return lax.optimization_barrier(jnp.sum(message_rows.astype(jnp.float32), axis=0))
    totals = lax.map(one_tile, (senders, target_proj)).reshape(-1, D)
    grid_out = node_update(grid_nodes, totals, node_first[3], node_bias[3], node_second[3], node_gain[3])
    alive_rows = (jnp.arange(M_DEV, dtype=jnp.int32)[None, :] < owned_nodes[:, None]).reshape(-1, 1)
    mesh_out = jnp.where(alive_rows, mesh_three, jnp.zeros_like(mesh_three))
    return (grid_out, mesh_out)
```

```python
import functools

import jax
import jax.numpy as jnp
from jax import lax
from jax.experimental import pallas as pl
from jax.experimental.pallas import tpu as pltpu
from jax.sharding import PartitionSpec as P

EPSILON = 1e-05
AXES = ("aa", "ba")
LANES = 128
BF16 = jnp.bfloat16
F32 = jnp.float32
LIMIT = pltpu.CompilerParams(vmem_limit_bytes=48 * 1024 * 1024)

UP_LISTS = (7, 5, 6)
DOWN_LISTS = (2, 0, 1)
RIGHT_LIST = 4
LEFT_LIST = 3
SEND_ORDER = UP_LISTS + DOWN_LISTS + (RIGHT_LIST, LEFT_LIST)


def dot(left, right):
    return jnp.dot(left, right, preferred_element_type=F32)


def round_up(value, unit):
    return -(-value // unit) * unit


def column(row):
    tall = jnp.broadcast_to(row, (LANES, row.shape[1]))
    return jnp.transpose(tall).astype(jnp.int16)


def one_hot(ids, width, base=0):
    lane = lax.broadcasted_iota(jnp.int16, ids.shape, 1)
    parts = [
        jnp.where(ids == lane + jnp.int16(base + start), BF16(1), BF16(0))
        for start in range(0, width, LANES)
    ]
    return parts[0] if len(parts) == 1 else jnp.concatenate(parts, 1)


def silu(value):
    half = 0.5 * value
    return half + half * jnp.tanh(half)


def normed(value, gain):
    average = jnp.mean(value, axis=-1, keepdims=True)
    centred = value - average
    spread = jnp.mean(centred * centred, axis=-1, keepdims=True)
    return centred * lax.rsqrt(spread + EPSILON) * gain


def whole(shape):
    return pl.BlockSpec(shape, lambda *_: (0,) * len(shape))


def layer(section, part, width):
    if part is None:
        return pl.BlockSpec((1, width, width), lambda *_: (section, 0, 0))
    return pl.BlockSpec((1, 1, width, width), lambda *_: (section, part, 0, 0))


def cost(macs, moved):
    return pl.CostEstimate(flops=2 * macs, bytes_accessed=moved, transcendentals=0)


def pick_kernel(rows_ref, rim_ref, up_ref, down_ref, right_ref, left_ref):
    count = rows_ref.shape[0]
    lists = rim_ref[0]
    for place, chosen in enumerate(SEND_ORDER):
        picked = one_hot(column(lists[chosen : chosen + 1]), count)
        block = dot(picked, rows_ref[...]).astype(BF16)
        if place < 3:
            up_ref[place] = block
        elif place < 6:
            down_ref[place - 3] = block
        elif place == 6:
            right_ref[0] = block
        else:
            left_ref[0] = block


def send_shapes(depth, width):
    return [jax.ShapeDtypeStruct((n, depth, width), BF16) for n in (3, 3, 1, 1)]


def pick_grid(rows, rim):
    count, width = rows.shape
    depth = rim.shape[2]
    return pl.pallas_call(
        pick_kernel,
        out_shape=send_shapes(depth, width),
        compiler_params=LIMIT,
        cost_estimate=cost(8 * depth * count * width, 2 * (count + 8 * depth) * width),
        name="pick_grid",
    )(rows, rim)


def fill(ref, value):
    rows = value.shape[0]
    ref[:rows] = value
    if ref.shape[0] > rows:
        ref[rows:] = jnp.zeros((ref.shape[0] - rows, ref.shape[1]), ref.dtype)


def local_kernel(
    section, project, source_ref, mesh_ref, edges_ref, first_s, first_r, bias_ref, out_ref, table, target
):
    @pl.when(pl.program_id(0) == 0)
    def _():
        source = source_ref[...]
        if project:
            source = dot(source, first_s[0, 0]).astype(BF16)
        fill(table, source)
        receiver = dot(mesh_ref[...], first_r[0, 0]) + bias_ref[section : section + 1]
        fill(target, receiver.astype(BF16))

    block = out_ref.shape[0]
    sub = math_block(block, 256)
    for start in range(0, block, sub):
        senders = column(edges_ref[0, 0:1, start : start + sub])
        targets = column(edges_ref[0, 1:2, start : start + sub])
        out_ref[start : start + sub] = dot(one_hot(senders, table.shape[0]), table[...]) + dot(
            one_hot(targets, target.shape[0]), target[...]
        )


def math_block(total, most):
    block = most
    while total % block:
        block -= LANES
    return block


def local_part(source, mesh_rows, edges, weights, section, project):
    total = edges.shape[2]
    width = source.shape[1]
    block = math_block(total, 512)
    count, slots = source.shape[0], mesh_rows.shape[0]
    first = weights["edge_first"]
    return pl.pallas_call(
        functools.partial(local_kernel, section, project),
        grid=(total // block,),
        in_specs=[
            whole(source.shape),
            whole(mesh_rows.shape),
            pl.BlockSpec((1, 2, block), lambda i: (0, 0, i)),
            layer(section, 0, width),
            layer(section, 1, width),
            whole(weights["edge_bias"].shape),
        ],
        out_specs=pl.BlockSpec((block, width), lambda i: (i, 0)),
        out_shape=jax.ShapeDtypeStruct((total, width), F32),
        scratch_shapes=[
            pltpu.VMEM((round_up(count, LANES), width), BF16),
            pltpu.VMEM((round_up(slots, LANES), width), BF16),
        ],
        compiler_params=LIMIT,
        cost_estimate=cost(total * (count + 256) * width, total * width * 4),
        name="local_part",
    )(source, mesh_rows, edges, first, first, weights["edge_bias"])


def place_remote(table, remote, places, weight):
    for ref, slots in zip(remote, places):
        depth = ref.shape[1]
        for index, slot in enumerate(slots):
            rows = ref[index]
            if weight is not None:
                rows = dot(rows, weight).astype(BF16)
            table[slot * depth : (slot + 1) * depth] = rows


def round_kernel(section, project, places, last, split, *refs):
    refs = list(refs)
    pre_ref, edges_ref, mesh_ref = refs[:3]
    remote = refs[3 : 3 + len(places)]
    (
        first_ref, second_ref, gain_ref, node0_ref, node1_ref, node2_ref, node_bias_ref, node_gain_ref,
        next_ref, lists_ref, owned_ref,
    ) = refs[3 + len(places) : 14 + len(places)]
    rest = refs[14 + len(places) :]
    mesh_out, proj_out = rest[:2]
    table, total = rest[-2:]
    sends = rest[2:-2]
    if last:
        masked_out, sends = sends[0], sends[1:]
    step = pl.program_id(0)
    slots = mesh_ref.shape[0]
    base = split

    @pl.when(step == 0)
    def _():
        place_remote(table, remote, places, first_ref[0, 0] if project else None)
        total[...] = jnp.zeros_like(total)

    block = pre_ref.shape[0]
    sub = math_block(block, 256)
    for start in range(0, block, sub):
        senders = column(edges_ref[0, 0:1, start : start + sub])
        pre = pre_ref[start : start + sub] + dot(one_hot(senders, table.shape[0], base), table[...])
        hidden = silu(pre).astype(BF16)
        message = normed(dot(hidden, second_ref[0]), gain_ref[section : section + 1]).astype(BF16)
        targets = edges_ref[0, 1:2, start : start + sub]
        member = lax.broadcasted_iota(jnp.int32, (slots, sub), 0) == targets
        total[...] += dot(member.astype(BF16), message)

    @pl.when(step == pl.num_programs(0) - 1)
    def _():
        rows = mesh_ref[...]
        inner = dot(rows, node0_ref[0, 0]) + dot(total[...].astype(BF16), node1_ref[0, 0])
        hidden = silu(inner + node_bias_ref[section : section + 1]).astype(BF16)
        update = normed(dot(hidden, node2_ref[0]), node_gain_ref[section : section + 1])
        fresh = (rows.astype(F32) + update).astype(BF16)
        mesh_out[...] = fresh
        if last:
            alive = lax.broadcasted_iota(jnp.int32, fresh.shape, 0) < owned_ref[0]
            masked_out[...] = jnp.where(alive, fresh, jnp.zeros_like(fresh))
        fill(proj_out, dot(fresh, next_ref[0, 0]).astype(BF16))
        listed = lists_ref.shape[1]
        size = math_block(listed, 256)
        made = []
        for start in range(0, listed, size):
            picked = one_hot(column(lists_ref[0:1, start : start + size]), proj_out.shape[0])
            made.append(dot(picked, proj_out[...]).astype(BF16))
        made = made[0] if len(made) == 1 else jnp.concatenate(made, 0)
        place = 0
        for ref in sends:
            if len(ref.shape) == 2:
                ref[...] = made
                continue
            depth = ref.shape[1]
            for index in range(ref.shape[0]):
                ref[index] = made[place : place + depth]
                place += depth


def round_part(pre, edges, mesh_rows, remote, places, weights, section, project, lists, owned, sends, split):
    total, width = pre.shape
    slots = mesh_rows.shape[0]
    last = section == 2
    block = math_block(total, 512)
    table_rows = sum(r.shape[0] * r.shape[1] for r in remote)
    padded = round_up(slots, LANES)
    out_shape = [
        jax.ShapeDtypeStruct((slots, width), BF16),
        jax.ShapeDtypeStruct((padded, width), BF16),
    ]
    if last:
        out_shape.append(jax.ShapeDtypeStruct((slots, width), BF16))
    out_shape += sends
    vectors = weights["edge_bias"].shape
    return pl.pallas_call(
        functools.partial(round_kernel, section, project, places, last, split),
        grid=(total // block,),
        in_specs=[
            pl.BlockSpec((block, width), lambda i: (i, 0)),
            pl.BlockSpec((1, 2, block), lambda i: (0, 0, i)),
            whole(mesh_rows.shape),
            *[whole(r.shape) for r in remote],
            layer(section, 0, width),
            layer(section, None, width),
            whole(vectors),
            layer(section, 0, width),
            layer(section, 1, width),
            layer(section, None, width),
            whole(vectors),
            whole(vectors),
            layer(section + 1, 0, width),
            whole(lists.shape),
            pl.BlockSpec(memory_space=pltpu.SMEM),
        ],
        out_specs=[whole(s.shape) for s in out_shape],
        out_shape=out_shape,
        scratch_shapes=[
            pltpu.VMEM((table_rows, width), BF16),
            pltpu.VMEM((slots, width), F32),
        ],
        compiler_params=LIMIT,
        cost_estimate=cost(total * (table_rows + 1024) * width, total * width * 4),
        name="round_part",
    )(
        pre, edges, mesh_rows, *remote,
        weights["edge_first"], weights["edge_second"], weights["edge_gain"],
        weights["node_first"], weights["node_first"], weights["node_second"],
        weights["node_bias"], weights["node_gain"], weights["edge_first"], lists, owned,
    )


def decode_local_kernel(section, grid_ref, table_ref, edges_ref, first_ref, bias_ref, node0_ref, node_bias_ref, pre_ref, inner_ref):
    rows = grid_ref[...]
    target = dot(rows, first_ref[0, 0]) + bias_ref[section : section + 1]
    inner_ref[...] = dot(rows, node0_ref[0, 0]) + node_bias_ref[section : section + 1]
    for sender in range(edges_ref.shape[1]):
        ids = column(edges_ref[0, sender : sender + 1, :])
        pre_ref[sender] = dot(one_hot(ids, table_ref.shape[0]), table_ref[...]) + target


def decode_local(grid_rows, table, edges, weights, section):
    count, width = grid_rows.shape
    senders = edges.shape[1]
    block = math_block(count, 256)
    vectors = weights["edge_bias"].shape
    return pl.pallas_call(
        functools.partial(decode_local_kernel, section),
        grid=(count // block,),
        in_specs=[
            pl.BlockSpec((block, width), lambda i: (i, 0)),
            whole(table.shape),
            pl.BlockSpec((1, senders, block), lambda i: (0, 0, i)),
            layer(section, 1, width),
            whole(vectors),
            layer(section, 0, width),
            whole(vectors),
        ],
        out_specs=[
            pl.BlockSpec((senders, block, width), lambda i: (0, i, 0)),
            pl.BlockSpec((block, width), lambda i: (i, 0)),
        ],
        out_shape=[
            jax.ShapeDtypeStruct((senders, count, width), F32),
            jax.ShapeDtypeStruct((count, width), F32),
        ],
        compiler_params=LIMIT,
        cost_estimate=cost(count * width * (2 * width + senders * table.shape[0]), count * width * 16),
        name="decode_local",
    )(grid_rows, table, edges, weights["edge_first"], weights["edge_bias"], weights["node_first"], weights["node_bias"])


def decode_kernel(section, places, split, *refs):
    pre_ref, inner_ref, grid_ref, edges_ref = refs[:4]
    remote = refs[4 : 4 + len(places)]
    second_ref, gain_ref, node1_ref, node2_ref, node_gain_ref, out_ref, table = refs[4 + len(places) :]

    @pl.when(pl.program_id(0) == 0)
    def _():
        place_remote(table, remote, places, None)

    total = None
    for sender in range(edges_ref.shape[1]):
        ids = column(edges_ref[0, sender : sender + 1, :])
        pre = pre_ref[sender] + dot(one_hot(ids, table.shape[0], split), table[...])
        hidden = silu(pre).astype(BF16)
        message = normed(dot(hidden, second_ref[0]), gain_ref[section : section + 1])
        message = message.astype(BF16).astype(F32)
        total = message if total is None else total + message
    inner = inner_ref[...] + dot(total.astype(BF16), node1_ref[0, 0])
    hidden = silu(inner).astype(BF16)
    update = normed(dot(hidden, node2_ref[0]), node_gain_ref[section : section + 1])
    out_ref[...] = (grid_ref[...].astype(F32) + update).astype(BF16)


def decode_part(pre, inner, grid_rows, edges, remote, places, weights, section, split):
    senders, count, width = pre.shape
    block = math_block(count, 256)
    table_rows = sum(r.shape[0] * r.shape[1] for r in remote)
    vectors = weights["edge_bias"].shape
    return pl.pallas_call(
        functools.partial(decode_kernel, section, places, split),
        grid=(count // block,),
        in_specs=[
            pl.BlockSpec((senders, block, width), lambda i: (0, i, 0)),
            pl.BlockSpec((block, width), lambda i: (i, 0)),
            pl.BlockSpec((block, width), lambda i: (i, 0)),
            pl.BlockSpec((1, senders, block), lambda i: (0, 0, i)),
            *[whole(r.shape) for r in remote],
            layer(section, None, width),
            whole(vectors),
            layer(section, 1, width),
            layer(section, None, width),
            whole(vectors),
        ],
        out_specs=pl.BlockSpec((block, width), lambda i: (i, 0)),
        out_shape=jax.ShapeDtypeStruct((count, width), BF16),
        scratch_shapes=[pltpu.VMEM((table_rows, width), BF16)],
        compiler_params=LIMIT,
        cost_estimate=cost(count * width * (5 * width + senders * table_rows), count * width * 16),
        name="decode_part",
    )(
        pre, inner, grid_rows, edges, *remote,
        weights["edge_second"], weights["edge_gain"], weights["node_first"],
        weights["node_second"], weights["node_gain"],
    )


def shift(value, along, step):
    bands, sectors = lax.axis_size("aa"), lax.axis_size("ba")
    pairs = []
    for i in range(bands):
        for j in range(sectors):
            if along == "aa":
                to = ((i + step) % bands) * sectors + j
            else:
                to = i * sectors + (j + step) % sectors
            pairs.append((i * sectors + j, to))
    return lax.ppermute(value, AXES, pairs)


def halo(up, down, right, left, together):
    from_up = shift(up, "aa", 1)
    from_down = shift(down, "aa", -1)
    if together:
        right = jnp.concatenate([right, from_up[0:1], from_down[0:1]], 0)
        left = jnp.concatenate([left, from_up[1:2], from_down[1:2]], 0)
        from_left = shift(right, "ba", 1)
        from_right = shift(left, "ba", -1)
        blocks = [from_up[2:3], from_down[2:3], from_left, from_right]
        places = ((1,), (6,), (3, 0, 5), (4, 2, 7))
        return blocks, places
    from_left = shift(right, "ba", 1)
    from_right = shift(left, "ba", -1)
    right = jnp.concatenate([from_up[0:1], from_down[0:1]], 0)
    left = jnp.concatenate([from_up[1:2], from_down[1:2]], 0)
    corner_left = shift(right, "ba", 1)
    corner_right = shift(left, "ba", -1)
    blocks = [from_up[2:3], from_down[2:3], from_left, from_right, corner_left, corner_right]
    places = ((1,), (6,), (3,), (4,), (0, 5), (2, 7))
    return blocks, places


def per_device(
    grid_nodes, mesh_nodes, owned_nodes, grid_rim, mesh_rim, long_send, g2m_edges, short_edges,
    long_edges, m2g_edges, edge_first, edge_second, edge_bias, edge_gain, node_first, node_second,
    node_bias, node_gain,
):
    weights = dict(
        edge_first=edge_first, edge_second=edge_second, edge_bias=edge_bias, edge_gain=edge_gain,
        node_first=node_first, node_second=node_second, node_bias=node_bias, node_gain=node_gain,
    )
    width = grid_nodes.shape[1]
    slots = mesh_nodes.shape[0]
    depth = mesh_rim.shape[2]
    peers, listed = long_send.shape[1:]
    rim_lists = jnp.concatenate([mesh_rim[0, m : m + 1] for m in SEND_ORDER], 0).reshape(1, 8 * depth)
    long_lists = long_send.reshape(1, peers * listed)
    rim_sends = send_shapes(depth, width)

    blocks, places = halo(*pick_grid(grid_nodes, grid_rim), together=False)
    pre = local_part(grid_nodes, mesh_nodes, g2m_edges, weights, 0, True)
    mesh_one, proj, *sends = round_part(
        pre, g2m_edges, mesh_nodes, blocks, places, weights, 0, True, rim_lists, owned_nodes,
        rim_sends, grid_nodes.shape[0],
    )

    blocks, places = halo(*sends, together=True)
    pre = local_part(proj, mesh_one, short_edges, weights, 1, False)
    mesh_two, proj, sent = round_part(
        pre, short_edges, mesh_one, blocks, places, weights, 1, False, long_lists, owned_nodes,
        [jax.ShapeDtypeStruct((peers * listed, width), BF16)], slots,
    )

    sent = sent.reshape(peers, listed, width)
    arrived = lax.all_to_all(sent, AXES, split_axis=0, concat_axis=0, tiled=True)
    pre = local_part(proj, mesh_two, long_edges, weights, 2, False)
    mesh_three, proj, mesh_out, *sends = round_part(
        pre, long_edges, mesh_two, [arrived.reshape(1, peers * listed, width)], ((0,),), weights, 2,
        False, rim_lists, owned_nodes, rim_sends, slots,
    )

    blocks, places = halo(*sends, together=True)
    pre, inner = decode_local(grid_nodes, proj, m2g_edges, weights, 3)
    grid_out = decode_part(pre, inner, grid_nodes, m2g_edges, blocks, places, weights, 3, slots)
    return grid_out, mesh_out


def solution(mesh):
    rows = P(AXES, None)
    lists = P(AXES, None, None)
    in_specs = (rows, rows, P(AXES)) + (lists,) * 7 + (P(),) * 8
    return jax.shard_map(
        per_device, mesh=mesh, in_specs=in_specs, out_specs=(rows, rows), check_vma=False
    )
```

```python
import functools

import jax
import jax.numpy as jnp
from jax import lax
from jax.experimental import pallas as pl
from jax.experimental.pallas import tpu as pltpu
from jax.sharding import PartitionSpec as P

EPSILON = 1e-05
AXES = ("aa", "ba")
LANES = 128
BF16 = jnp.bfloat16
F32 = jnp.float32
LIMIT = pltpu.CompilerParams(vmem_limit_bytes=28 * 1024 * 1024)

ALONG_AA = (-1, -1, -1, 0, 0, 1, 1, 1)
ALONG_BA = (-1, 0, 1, -1, 1, -1, 0, 1)
UP_LISTS = (7, 5, 6)
DOWN_LISTS = (2, 0, 1)
RIGHT_LIST = 4
LEFT_LIST = 3
SEND_ORDER = UP_LISTS + DOWN_LISTS + (RIGHT_LIST, LEFT_LIST)


def dot(left, right):
    return jnp.dot(left, right, preferred_element_type=F32)


def math_block(total, most):
    block = most
    while total % block:
        block -= LANES
    return block


def round_up(value, unit):
    return -(-value // unit) * unit


def column(row):
    tall = jnp.broadcast_to(row, (LANES, row.shape[1]))
    return jnp.transpose(tall).astype(jnp.int16)


def one_hot(ids, width, base=0):
    lane = lax.broadcasted_iota(jnp.int16, ids.shape, 1)
    parts = [
        jnp.where(ids == lane + jnp.int16(base + start), BF16(1), BF16(0))
        for start in range(0, width, LANES)
    ]
    return parts[0] if len(parts) == 1 else jnp.concatenate(parts, 1)


def silu(value):
    half = 0.5 * value
    return half + half * jnp.tanh(half)


def normed(value):
    average = jnp.mean(value, axis=-1, keepdims=True)
    centred = value - average
    spread = jnp.mean(centred * centred, axis=-1, keepdims=True)
    return centred * lax.rsqrt(spread + EPSILON)


def whole(shape):
    return pl.BlockSpec(shape, lambda *_: (0,) * len(shape))


def cost(macs, moved):
    return pl.CostEstimate(flops=2 * macs, bytes_accessed=moved, transcendentals=0)


HBM = pl.BlockSpec(memory_space=pltpu.HBM)
SMEM = pl.BlockSpec(memory_space=pltpu.SMEM)


def fetch(sources, buffers, arrived):
    copies = [
        pltpu.make_async_copy(source, buffers.at[i], arrived.at[i]) for i, source in enumerate(sources)
    ]
    for copy in copies:
        copy.start()

    def take(index):
        copies[index].wait()
        return buffers[index]

    return take


def fetch_scratch(count, width):
    return [pltpu.VMEM((count, width, width), BF16), pltpu.SemaphoreType.DMA((count,))]


def fill(ref, value):
    rows = value.shape[0]
    ref[:rows] = value
    if ref.shape[0] > rows:
        ref[rows:] = jnp.zeros((ref.shape[0] - rows, ref.shape[1]), ref.dtype)


def clear_tail(ref, rows):
    ref[rows:] = jnp.zeros((ref.shape[0] - rows, ref.shape[1]), ref.dtype)


def row_of(ref, index):
    return ref[index : index + 1]


def added(pre, targets, second, slots):
    hidden = silu(pre).astype(BF16)
    message = normed(dot(hidden, second)).astype(BF16)
    member = lax.broadcasted_iota(jnp.int32, (slots, targets.shape[1]), 0) == targets
    return dot(member.astype(BF16), message)


def updated(rows, total, inner, take, places, gain):
    first, second = places
    inner = inner + dot(total.astype(BF16), take(first))
    update = normed(dot(silu(inner).astype(BF16), take(second))) * gain
    return (rows.astype(F32) + update).astype(BF16)


def pick_kernel(rows_ref, rim_ref, *outs):
    lists = rim_ref[0]
    for chosen, out in enumerate(outs):
        picked = one_hot(column(lists[chosen : chosen + 1]), rows_ref.shape[0])
        out[...] = dot(picked, rows_ref[...]).astype(BF16)


def pick_grid(rows, rim):
    count, width = rows.shape
    depth = rim.shape[2]
    return pl.pallas_call(
        pick_kernel,
        out_shape=[jax.ShapeDtypeStruct((depth, width), BF16)] * 8,
        compiler_params=LIMIT,
        cost_estimate=cost(8 * depth * count * width, 2 * (count + 8 * depth) * width),
        name="pick_grid",
    )(rows, rim)


def send_shapes(depth, width):
    return [jax.ShapeDtypeStruct((n, depth, width), BF16) for n in (3, 3, 1, 1)]


def list_rows(proj_out, lists_ref, sends):
    listed = lists_ref.shape[1]
    size = math_block(listed, 256)
    made = []
    for start in range(0, listed, size):
        picked = one_hot(column(lists_ref[0:1, start : start + size]), proj_out.shape[0])
        made.append(dot(picked, proj_out[...]).astype(BF16))
    made = made[0] if len(made) == 1 else jnp.concatenate(made, 0)
    place = 0
    for ref in sends:
        if len(ref.shape) == 2:
            ref[...] = made
            continue
        depth = ref.shape[1]
        for index in range(ref.shape[0]):
            ref[index] = made[place : place + depth]
            place += depth


WINDOW = 512
BLOCK = 512


def sorted_keys(edges, slots):
    shift = slots.bit_length()
    senders, targets = edges[0, 0:1], edges[0, 1:2]
    senders = jnp.where(targets < slots, senders, 1 << 14)
    return lax.sort((senders << shift) + targets, dimension=1), shift


def below(keys, limit):
    total = keys.shape[1]
    step = 1 << (total.bit_length() - 1)
    found = jnp.int32(0)
    while step:
        place = found + step
        inside = keys[0, jnp.minimum(place, total) - 1] < limit
        found = jnp.where((place <= total) & inside, place, found)
        step //= 2
    return found


def edge_block(start, used, shift, scalars, keys_ref, table, target, pre, second, slots):
    block = pre.shape[0]
    start = pl.multiple_of(start, LANES)
    keys = keys_ref[0:1, pl.ds(start, block)]
    senders = keys >> shift
    targets = keys & ((1 << shift) - 1)
    lowest = pl.multiple_of((scalars[0, start] >> shift) // 16 * 16, 16)
    highest = scalars[0, jnp.minimum(start + block, used) - 1] >> shift

    def window(base):
        ids = column(jnp.clip(senders - base, -1, 1 << 14))
        return dot(one_hot(ids, WINDOW), table[pl.ds(base, WINDOW)])

    pre[...] = window(lowest) + dot(one_hot(column(targets), target.shape[0]), target[...])

    def more(index, carry):
        pre[...] += window(pl.multiple_of(lowest + (index + 1) * WINDOW, 16))
        return carry

    lax.fori_loop(0, (highest - lowest) // WINDOW, more, 0)
    return added(pre[...], targets, second, slots)


def encode_local_kernel(
    section, shift, scalars, keys_ref, grid_ref, mesh_ref, bias_ref, node_bias_ref,
    edge_first, edge_second, node_first, table_out, target_out, total_out, inner_out,
    table, pre, buffers, arrived,
):
    take = fetch(
        [edge_first.at[section, 0], edge_first.at[section, 1], edge_second.at[section], node_first.at[section, 0]],
        buffers, arrived,
    )
    count, slots = grid_ref.shape[0], mesh_ref.shape[0]
    proj = dot(grid_ref[...], take(0)).astype(BF16)
    table_out[...] = proj
    fill(table, proj)
    rows = mesh_ref[...]
    fill(target_out, (dot(rows, take(1)) + row_of(bias_ref, section)).astype(BF16))
    second = take(2)
    inner_out[...] = dot(rows, take(3)) + row_of(node_bias_ref, section)
    total_out[...] = jnp.zeros_like(total_out)
    block = pre.shape[0]
    done = below(scalars, count << shift) // block

    def step(index, carry):
        total_out[...] += edge_block(
            index * block, done * block, shift, scalars, keys_ref, table, target_out, pre, buffers[2], slots
        )
        return carry

    lax.fori_loop(0, done, step, 0)


def encode_local(keys, shift, grid_rows, mesh_rows, weights, section):
    total = keys.shape[1]
    count, width = grid_rows.shape
    slots = mesh_rows.shape[0]
    vmem = pl.BlockSpec(memory_space=pltpu.VMEM)
    return pl.pallas_call(
        functools.partial(encode_local_kernel, section, shift),
        in_specs=[SMEM] + [vmem] * 5 + [HBM] * 3,
        out_shape=[
            jax.ShapeDtypeStruct((count, width), BF16),
            jax.ShapeDtypeStruct((round_up(slots, LANES), width), BF16),
            jax.ShapeDtypeStruct((slots, width), F32),
            jax.ShapeDtypeStruct((slots, width), F32),
        ],
        scratch_shapes=[
            pltpu.VMEM((count + WINDOW, width), BF16),
            pltpu.VMEM((math_block(total, BLOCK), width), F32),
            *fetch_scratch(4, width),
        ],
        compiler_params=LIMIT,
        cost_estimate=cost(total * 1500 * width, 6 * count * width),
        name="encode_local",
    )(
        keys, keys, grid_rows, mesh_rows, weights["edge_bias"], weights["node_bias"],
        weights["edge_first"], weights["edge_second"], weights["node_first"],
    )


def encode_kernel(section, shift, *refs):
    scalars, keys_ref, local_ref, target, total_ref, inner_ref, mesh_ref = refs[:7]
    remote = refs[7:15]
    (
        gain_ref, node_gain_ref, lists_ref, edge_first, edge_second, node_first, node_second,
        mesh_out, proj_out, up, down, right, left, table, pre, total, buffers, arrived,
    ) = refs[15:]
    take = fetch(
        [
            edge_first.at[section, 0], edge_second.at[section], node_first.at[section, 1],
            node_second.at[section], edge_first.at[section + 1, 0],
        ],
        buffers, arrived,
    )
    count, slots = local_ref.shape[0], mesh_ref.shape[0]
    depth = remote[0].shape[0]
    table[:count] = local_ref[...]
    clear_tail(table, count + 8 * depth)
    take(0)
    for chosen, ref in enumerate(remote):
        place = count + (7 - chosen) * depth
        table[place : place + depth] = dot(ref[...], buffers[0]).astype(BF16)
    take(1)
    total[...] = total_ref[...]
    block = pre.shape[0]
    start = below(scalars, count << shift) // block * block
    used = below(scalars, (count + 8 * depth) << shift)

    def step(index, carry):
        total[...] += edge_block(
            start + index * block, used, shift, scalars, keys_ref, table, target, pre, buffers[1], slots
        )
        return carry

    lax.fori_loop(0, (used - start + block - 1) // block, step, 0)
    summed = total[...] * row_of(gain_ref, section)
    fresh = updated(mesh_ref[...], summed, inner_ref[...], take, (2, 3), row_of(node_gain_ref, section))
    mesh_out[...] = fresh
    fill(proj_out, dot(fresh, take(4)).astype(BF16))
    list_rows(proj_out, lists_ref, (up, down, right, left))


def encode(keys, shift, local, target, total, inner, mesh_rows, remote, lists, depth, weights, section):
    edges = keys.shape[1]
    count, width = local.shape
    slots = mesh_rows.shape[0]
    vmem = pl.BlockSpec(memory_space=pltpu.VMEM)
    rows = count + 8 * remote[0].shape[0]
    return pl.pallas_call(
        functools.partial(encode_kernel, section, shift),
        in_specs=[SMEM] + [vmem] * 17 + [HBM] * 4,
        out_shape=[
            jax.ShapeDtypeStruct((slots, width), BF16),
            jax.ShapeDtypeStruct((round_up(slots, LANES), width), BF16),
        ]
        + send_shapes(depth, width),
        scratch_shapes=[
            pltpu.VMEM((rows + WINDOW, width), BF16),
            pltpu.VMEM((math_block(edges, BLOCK), width), F32),
            pltpu.VMEM((slots, width), F32),
            *fetch_scratch(5, width),
        ],
        compiler_params=LIMIT,
        cost_estimate=cost(edges * 1500 * width, 8 * rows * width),
        name="encode",
    )(
        keys, keys, local, target, total, inner, mesh_rows, *remote,
        weights["edge_gain"], weights["node_gain"], lists,
        weights["edge_first"], weights["edge_second"], weights["node_first"], weights["node_second"],
    )


def prepare_kernel(section, mesh_ref, bias_ref, node_bias_ref, edge_first, node_first, target_out, inner_out, buffers, arrived):
    take = fetch([edge_first.at[section, 1], node_first.at[section, 0]], buffers, arrived)
    rows = mesh_ref[...]
    fill(target_out, (dot(rows, take(0)) + row_of(bias_ref, section)).astype(BF16))
    inner_out[...] = dot(rows, take(1)) + row_of(node_bias_ref, section)


def prepare(mesh_rows, weights, section):
    slots, width = mesh_rows.shape
    vmem = pl.BlockSpec(memory_space=pltpu.VMEM)
    return pl.pallas_call(
        functools.partial(prepare_kernel, section),
        in_specs=[vmem] * 3 + [HBM] * 2,
        out_shape=[
            jax.ShapeDtypeStruct((round_up(slots, LANES), width), BF16),
            jax.ShapeDtypeStruct((slots, width), F32),
        ],
        scratch_shapes=fetch_scratch(2, width),
        compiler_params=LIMIT,
        cost_estimate=cost(2 * slots * width * width, 6 * width * width),
        name="prepare",
    )(mesh_rows, weights["edge_bias"], weights["node_bias"], weights["edge_first"], weights["node_first"])


def place_remote(table, remote, places, base):
    for ref, slots in zip(remote, places):
        depth = ref.shape[1]
        for index, slot in enumerate(slots):
            place = base + slot * depth
            table[place : place + depth] = ref[index]


def round_kernel(section, places, last, *refs):
    edges_ref, local_ref, target, inner_ref, mesh_ref = refs[:5]
    remote = refs[5 : 5 + len(places)]
    (
        gain_ref, node_gain_ref, lists_ref, owned_ref, edge_first, edge_second, node_first, node_second,
    ) = refs[5 + len(places) : 13 + len(places)]
    rest = refs[13 + len(places) :]
    mesh_out, proj_out = rest[:2]
    sends = rest[2:-3]
    table, buffers, arrived = rest[-3:]
    if last:
        masked_out, sends = sends[0], sends[1:]
    take = fetch(
        [
            edge_second.at[section], node_first.at[section, 1], node_second.at[section],
            edge_first.at[section + 1, 0],
        ],
        buffers, arrived,
    )
    slots, padded = mesh_ref.shape[0], local_ref.shape[0]
    table[:padded] = local_ref[...]
    place_remote(table, remote, places, padded)
    edges = edges_ref.shape[2]
    block = math_block(edges, 1536)
    summed = None
    for start in range(0, edges, block):
        senders = edges_ref[0, 0:1, start : start + block]
        senders = jnp.where(senders < slots, senders, senders + (padded - slots))
        targets = edges_ref[0, 1:2, start : start + block]
        pre = dot(one_hot(column(senders), table.shape[0]), table[...]) + dot(
            one_hot(column(targets), padded), target[...]
        )
        if start == 0:
            take(0)
        part = added(pre, targets, buffers[0], slots)
        summed = part if summed is None else summed + part
    summed = summed * row_of(gain_ref, section)
    fresh = updated(mesh_ref[...], summed, inner_ref[...], take, (1, 2), row_of(node_gain_ref, section))
    mesh_out[...] = fresh
    if last:
        alive = lax.broadcasted_iota(jnp.int32, fresh.shape, 0) < owned_ref[0]
        masked_out[...] = jnp.where(alive, fresh, jnp.zeros_like(fresh))
    fill(proj_out, dot(fresh, take(3)).astype(BF16))
    list_rows(proj_out, lists_ref, sends)


def round_part(edges, local, target, inner, mesh_rows, remote, places, lists, owned, sends, weights, section):
    slots, width = mesh_rows.shape
    last = section == 2
    padded = local.shape[0]
    table_rows = padded + sum(r.shape[0] * r.shape[1] for r in remote)
    out_shape = [
        jax.ShapeDtypeStruct((slots, width), BF16),
        jax.ShapeDtypeStruct((padded, width), BF16),
    ]
    if last:
        out_shape.append(jax.ShapeDtypeStruct((slots, width), BF16))
    vmem = pl.BlockSpec(memory_space=pltpu.VMEM)
    return pl.pallas_call(
        functools.partial(round_kernel, section, places, last),
        in_specs=[vmem] * (8 + len(remote)) + [SMEM] + [HBM] * 4,
        out_shape=out_shape + sends,
        scratch_shapes=[pltpu.VMEM((table_rows, width), BF16), *fetch_scratch(4, width)],
        compiler_params=LIMIT,
        cost_estimate=cost(edges.shape[2] * (table_rows + 1024) * width, 8 * width * width),
        name="round_part",
    )(
        edges, local, target, inner, mesh_rows, *remote, weights["edge_gain"], weights["node_gain"], lists, owned,
        weights["edge_first"], weights["edge_second"], weights["node_first"], weights["node_second"],
    )


def decode_local_kernel(section, grid_ref, table_ref, edges_ref, bias_ref, edge_first, pre_ref, buffers, arrived):
    @pl.when(pl.program_id(0) == 0)
    def _():
        fetch([edge_first.at[section, 1]], buffers, arrived)(0)

    target = dot(grid_ref[...], buffers[0]) + row_of(bias_ref, section)
    for sender in range(edges_ref.shape[1]):
        ids = column(edges_ref[0, sender : sender + 1, :])
        pre_ref[sender] = (dot(one_hot(ids, table_ref.shape[0]), table_ref[...]) + target).astype(BF16)


def decode_local(grid_rows, table, edges, weights, section):
    count, width = grid_rows.shape
    senders = edges.shape[1]
    block = math_block(count, 256)
    return pl.pallas_call(
        functools.partial(decode_local_kernel, section),
        grid=(count // block,),
        in_specs=[
            pl.BlockSpec((block, width), lambda i: (i, 0)),
            whole(table.shape),
            pl.BlockSpec((1, senders, block), lambda i: (0, 0, i)),
            whole(weights["edge_bias"].shape),
            HBM,
        ],
        out_specs=pl.BlockSpec((senders, block, width), lambda i: (0, i, 0)),
        out_shape=jax.ShapeDtypeStruct((senders, count, width), BF16),
        scratch_shapes=fetch_scratch(1, width),
        compiler_params=LIMIT,
        cost_estimate=cost(count * width * (width + senders * table.shape[0]), count * width * 8),
        name="decode_local",
    )(grid_rows, table, edges, weights["edge_bias"], weights["edge_first"])


def decode_kernel(section, places, split, *refs):
    pre_ref, grid_ref, edges_ref = refs[:3]
    remote = refs[3 : 3 + len(places)]
    (
        gain_ref, node_bias_ref, node_gain_ref, edge_second, node_first, node_second, out_ref,
        table, buffers, arrived,
    ) = refs[3 + len(places) :]

    @pl.when(pl.program_id(0) == 0)
    def _():
        take = fetch(
            [
                edge_second.at[section], node_first.at[section, 0], node_first.at[section, 1],
                node_second.at[section],
            ],
            buffers, arrived,
        )
        place_remote(table, remote, places, 0)
        for index in range(4):
            take(index)

    summed = None
    for sender in range(edges_ref.shape[1]):
        ids = column(edges_ref[0, sender : sender + 1, :])
        pre = pre_ref[sender].astype(F32) + dot(one_hot(ids, table.shape[0], split), table[...])
        message = normed(dot(silu(pre).astype(BF16), buffers[0])).astype(BF16).astype(F32)
        summed = message if summed is None else summed + message
    rows = grid_ref[...]
    summed = (summed * row_of(gain_ref, section)).astype(BF16)
    inner = dot(rows, buffers[1]) + dot(summed, buffers[2]) + row_of(node_bias_ref, section)
    update = normed(dot(silu(inner).astype(BF16), buffers[3])) * row_of(node_gain_ref, section)
    out_ref[...] = (rows.astype(F32) + update).astype(BF16)


def decode_part(pre, grid_rows, edges, remote, places, weights, section, split):
    senders, count, width = pre.shape
    block = math_block(count, 256)
    table_rows = sum(r.shape[0] * r.shape[1] for r in remote)
    vectors = whole(weights["edge_bias"].shape)
    return pl.pallas_call(
        functools.partial(decode_kernel, section, places, split),
        grid=(count // block,),
        in_specs=[
            pl.BlockSpec((senders, block, width), lambda i: (0, i, 0)),
            pl.BlockSpec((block, width), lambda i: (i, 0)),
            pl.BlockSpec((1, senders, block), lambda i: (0, 0, i)),
            *[whole(r.shape) for r in remote],
            vectors, vectors, vectors, HBM, HBM, HBM,
        ],
        out_specs=pl.BlockSpec((block, width), lambda i: (i, 0)),
        out_shape=jax.ShapeDtypeStruct((count, width), BF16),
        scratch_shapes=[pltpu.VMEM((table_rows, width), BF16), *fetch_scratch(4, width)],
        compiler_params=LIMIT,
        cost_estimate=cost(count * width * (6 * width + senders * table_rows), count * width * 12),
        name="decode_part",
    )(
        pre, grid_rows, edges, *remote, weights["edge_gain"], weights["node_bias"], weights["node_gain"],
        weights["edge_second"], weights["node_first"], weights["node_second"],
    )


def shift_rows(value, step_aa, step_ba):
    bands, sectors = lax.axis_size("aa"), lax.axis_size("ba")
    pairs = []
    for i in range(bands):
        for j in range(sectors):
            to = ((i + step_aa) % bands) * sectors + (j + step_ba) % sectors
            pairs.append((i * sectors + j, to))
    return lax.ppermute(value, AXES, pairs)


def direct_halo(lists):
    return [shift_rows(rows, ALONG_AA[m], ALONG_BA[m]) for m, rows in enumerate(lists)]


def join_kernel(up_ref, down_ref, right_ref, left_ref, right_out, left_out):
    for index, (own, out) in enumerate(((right_ref, right_out), (left_ref, left_out))):
        out[0] = own[0]
        out[1] = up_ref[index]
        out[2] = down_ref[index]


def halo(up, down, right, left):
    from_up = shift_rows(up, 1, 0)
    from_down = shift_rows(down, -1, 0)
    joined = jax.ShapeDtypeStruct((3,) + right.shape[1:], BF16)
    right, left = pl.pallas_call(
        join_kernel, out_shape=[joined, joined], compiler_params=LIMIT, name="join"
    )(from_up, from_down, right, left)
    from_left = shift_rows(right, 0, 1)
    from_right = shift_rows(left, 0, -1)
    return [from_up[2:3], from_down[2:3], from_left, from_right], ((1,), (6,), (3, 0, 5), (4, 2, 7))


def per_device(
    grid_nodes, mesh_nodes, owned_nodes, grid_rim, mesh_rim, long_send, g2m_edges, short_edges,
    long_edges, m2g_edges, edge_first, edge_second, edge_bias, edge_gain, node_first, node_second,
    node_bias, node_gain,
):
    weights = dict(
        edge_first=edge_first, edge_second=edge_second, edge_bias=edge_bias, edge_gain=edge_gain,
        node_first=node_first, node_second=node_second, node_bias=node_bias, node_gain=node_gain,
    )
    width = grid_nodes.shape[1]
    slots = mesh_nodes.shape[0]
    depth = mesh_rim.shape[2]
    peers, listed = long_send.shape[1:]

    remote = direct_halo(pick_grid(grid_nodes, grid_rim))
    keys, bits = sorted_keys(g2m_edges, slots)
    rim_lists = jnp.concatenate([mesh_rim[0, m : m + 1] for m in SEND_ORDER], 0).reshape(1, 8 * depth)
    long_lists = long_send.reshape(1, peers * listed)
    rim_sends = send_shapes(depth, width)
    proj, target, total, inner = encode_local(keys, bits, grid_nodes, mesh_nodes, weights, 0)
    mesh_one, proj, *sends = encode(
        keys, bits, proj, target, total, inner, mesh_nodes, remote, rim_lists, depth, weights, 0
    )

    remote, places = halo(*sends)
    target, inner = prepare(mesh_one, weights, 1)
    mesh_two, proj, sent = round_part(
        short_edges, proj, target, inner, mesh_one, remote, places, long_lists, owned_nodes,
        [jax.ShapeDtypeStruct((peers * listed, width), BF16)], weights, 1,
    )

    sent = sent.reshape(peers, listed, width)
    arrived = lax.all_to_all(sent, AXES, split_axis=0, concat_axis=0, tiled=True)
    target, inner = prepare(mesh_two, weights, 2)
    mesh_three, proj, mesh_out, *sends = round_part(
        long_edges, proj, target, inner, mesh_two, [arrived.reshape(1, peers * listed, width)], ((0,),),
        rim_lists, owned_nodes, rim_sends, weights, 2,
    )

    remote, places = halo(*sends)
    pre = decode_local(grid_nodes, proj, m2g_edges, weights, 3)
    grid_out = decode_part(pre, grid_nodes, m2g_edges, remote, places, weights, 3, slots)
    return grid_out, mesh_out


def solution(mesh):
    rows = P(AXES, None)
    lists = P(AXES, None, None)
    in_specs = (rows, rows, P(AXES)) + (lists,) * 7 + (P(),) * 8
    return jax.shard_map(
        per_device, mesh=mesh, in_specs=in_specs, out_specs=(rows, rows), check_vma=False
    )
```

```python
import functools

import jax
import jax.numpy as jnp
from jax import lax
from jax.experimental import pallas as pl
from jax.experimental.pallas import tpu as pltpu
from jax.sharding import PartitionSpec as P

EPSILON = 1e-05
AXES = ("aa", "ba")
LANES = 128
BF16 = jnp.bfloat16
F32 = jnp.float32
LIMIT = pltpu.CompilerParams(vmem_limit_bytes=28 * 1024 * 1024)

UP_LISTS = (7, 5, 6)
DOWN_LISTS = (2, 0, 1)
RIGHT_LIST = 4
LEFT_LIST = 3
SEND_ORDER = UP_LISTS + DOWN_LISTS + (RIGHT_LIST, LEFT_LIST)


def dot(left, right):
    return jnp.dot(left, right, preferred_element_type=F32)


def math_block(total, most):
    block = most
    while total % block:
        block -= LANES
    return block


def round_up(value, unit):
    return -(-value // unit) * unit


def column(row):
    tall = jnp.broadcast_to(row, (LANES, row.shape[1]))
    return jnp.transpose(tall).astype(jnp.int16)


def one_hot(ids, width, base=0):
    lane = lax.broadcasted_iota(jnp.int16, ids.shape, 1)
    parts = [
        jnp.where(ids == lane + jnp.int16(base + start), BF16(1), BF16(0))
        for start in range(0, width, LANES)
    ]
    return parts[0] if len(parts) == 1 else jnp.concatenate(parts, 1)


def silu(value):
    half = 0.5 * value
    return half + half * jnp.tanh(half)


def normed(value):
    average = jnp.mean(value, axis=-1, keepdims=True)
    centred = value - average
    spread = jnp.mean(centred * centred, axis=-1, keepdims=True)
    return centred * lax.rsqrt(spread + EPSILON)


def whole(shape):
    return pl.BlockSpec(shape, lambda *_: (0,) * len(shape))


def cost(macs, moved):
    return pl.CostEstimate(flops=2 * macs, bytes_accessed=moved, transcendentals=0)


HBM = pl.BlockSpec(memory_space=pltpu.HBM)
SMEM = pl.BlockSpec(memory_space=pltpu.SMEM)


def stay(stack):
    return pltpu.with_memory_space_constraint(stack, pltpu.HBM)


def near(value):
    return pltpu.with_memory_space_constraint(value, pltpu.VMEM)


def fetch(sources, buffers, arrived):
    copies = [
        pltpu.make_async_copy(source, buffers.at[i], arrived.at[i]) for i, source in enumerate(sources)
    ]
    for copy in copies:
        copy.start()
    return copies


def fetch_scratch(count, width):
    return [pltpu.VMEM((count, width, width), BF16), pltpu.SemaphoreType.DMA((count,))]


def matrices(count, width):
    return pltpu.VMEM((count, width, width), BF16)


def fill(ref, value):
    rows = value.shape[0]
    ref[:rows] = value
    if ref.shape[0] > rows:
        ref[rows:] = jnp.zeros((ref.shape[0] - rows, ref.shape[1]), ref.dtype)


def clear_tail(ref, rows):
    ref[rows:] = jnp.zeros((ref.shape[0] - rows, ref.shape[1]), ref.dtype)


def row_of(ref, index):
    return ref[index : index + 1]


def added(pre, targets, second, slots):
    hidden = silu(pre).astype(BF16)
    message = normed(dot(hidden, second)).astype(BF16)
    member = lax.broadcasted_iota(jnp.int32, (slots, targets.shape[1]), 0) == targets
    return dot(member.astype(BF16), message)


def updated(rows, total, inner, first, second, gain):
    inner = inner + dot(total.astype(BF16), first)
    update = normed(dot(silu(inner).astype(BF16), second)) * gain
    return (rows.astype(F32) + update).astype(BF16)


def side_base():
    return jnp.where(lax.axis_index("aa") % 2 == 0, 5, 0)


def pick_kernel(rows_ref, rim_ref, pair_out, right_out, left_out, *outer_outs):
    depth = right_out.shape[0]
    pair = side_base()
    outer = 5 - pair

    def pick(chosen):
        ids = column(rim_ref[0, pl.ds(chosen, 1), :])
        return dot(one_hot(ids, rows_ref.shape[0]), rows_ref[...]).astype(BF16)

    for index, offset in enumerate((2, 0, 1)):
        pair_out[index * depth : (index + 1) * depth] = pick(pair + offset)
    right_out[...] = pick(RIGHT_LIST)
    left_out[...] = pick(LEFT_LIST)
    for out, offset in zip(outer_outs, (2, 0, 1)):
        out[...] = pick(outer + offset)


def pick_grid(rows, rim):
    count, width = rows.shape
    depth = rim.shape[2]
    block = jax.ShapeDtypeStruct((depth, width), BF16)
    return pl.pallas_call(
        pick_kernel,
        out_shape=[jax.ShapeDtypeStruct((3 * depth, width), BF16)] + [block] * 5,
        compiler_params=LIMIT,
        cost_estimate=cost(8 * depth * count * width, 2 * (count + 8 * depth) * width),
        name="pick_grid",
    )(rows, rim)


def pair_join_kernel(shift, slots, pair_ref, right_ref, left_ref, edges_ref, right_out, left_out, keys_out):
    depth = right_ref.shape[0]
    for index, (own, out) in enumerate(((right_ref, right_out), (left_ref, left_out))):
        out[:depth] = own[...]
        out[depth:] = pair_ref[index * depth : (index + 1) * depth]
    senders, targets = edges_ref[0, 0:1], edges_ref[0, 1:2]
    senders = jnp.where(targets < slots, senders, 1 << 14)
    keys_out[...] = (senders << shift) + targets


def pair_join(pair, right, left, edges, slots):
    depth, width = right.shape
    shift = slots.bit_length()
    joined = jax.ShapeDtypeStruct((2 * depth, width), BF16)
    right, left, keys = pl.pallas_call(
        functools.partial(pair_join_kernel, shift, slots),
        out_shape=[joined, joined, jax.ShapeDtypeStruct((1, edges.shape[2]), jnp.int32)],
        compiler_params=LIMIT,
        name="pair_join",
    )(pair, right, left, edges)
    return right, left, lax.sort(keys.reshape(-1)).reshape(1, -1), shift


def grid_halo(rows, rim, edges, slots):
    pair, right, left, *outer = pick_grid(rows, rim)
    pair = move(pair, lambda i, j: (i ^ 1, j))
    right, left, keys, shift = pair_join(pair, right, left, edges, slots)
    other = lambda i: i + 1 if i % 2 else i - 1
    arrived = [
        move(right, lambda i, j: (i, j + 1)),
        move(left, lambda i, j: (i, j - 1)),
        move(outer[0], lambda i, j: (other(i), j + 1)),
        move(outer[1], lambda i, j: (other(i), j - 1)),
        move(outer[2], lambda i, j: (other(i), j)),
    ]
    return [pair] + arrived, keys, shift


def send_shapes(depth, width):
    return [jax.ShapeDtypeStruct((n, depth, width), BF16) for n in (3, 3, 1, 1)]


def list_rows(proj_out, lists_ref, sends):
    listed = lists_ref.shape[1]
    size = math_block(listed, 256)
    made = []
    for start in range(0, listed, size):
        picked = one_hot(column(lists_ref[0:1, start : start + size]), proj_out.shape[0])
        made.append(dot(picked, proj_out[...]).astype(BF16))
    made = made[0] if len(made) == 1 else jnp.concatenate(made, 0)
    place = 0
    for ref in sends:
        if len(ref.shape) == 2:
            ref[...] = made
            continue
        depth = ref.shape[1]
        for index in range(ref.shape[0]):
            ref[index] = made[place : place + depth]
            place += depth


WINDOW = 512
BLOCK = 512


def below(keys, limit):
    total = keys.shape[1]
    step = 1 << (total.bit_length() - 1)
    found = jnp.int32(0)
    while step:
        place = found + step
        inside = keys[0, jnp.minimum(place, total) - 1] < limit
        found = jnp.where((place <= total) & inside, place, found)
        step //= 2
    return found


def edge_block(start, used, shift, scalars, keys_ref, table, target, pre, second, slots):
    block = pre.shape[0]
    start = pl.multiple_of(start, LANES)
    keys = keys_ref[0:1, pl.ds(start, block)]
    senders = keys >> shift
    targets = keys & ((1 << shift) - 1)
    lowest = pl.multiple_of((scalars[0, start] >> shift) // 16 * 16, 16)
    highest = scalars[0, jnp.minimum(start + block, used) - 1] >> shift

    def window(base):
        ids = column(jnp.clip(senders - base, -1, 1 << 14))
        return dot(one_hot(ids, WINDOW), table[pl.ds(base, WINDOW)])

    pre[...] = window(lowest) + dot(one_hot(column(targets), target.shape[0]), target[...])

    def more(index, carry):
        pre[...] += window(pl.multiple_of(lowest + (index + 1) * WINDOW, 16))
        return carry

    lax.fori_loop(0, (highest - lowest) // WINDOW, more, 0)
    return added(pre[...], targets, second, slots)


def encode_local_kernel(
    section, shift, scalars, keys_ref, grid_ref, mesh_ref, bias_ref, node_bias_ref,
    edge_first, edge_second, node_first, node_second, table_out, target_out, total_out, inner_out, later,
    table, pre, own, arrived, later_arrived,
):
    copies = fetch(
        [edge_first.at[section, 0], edge_first.at[section, 1], node_first.at[section, 0]], own, arrived
    )
    copies += fetch(
        [
            edge_second.at[section], edge_first.at[section, 0], node_first.at[section, 1],
            node_second.at[section], edge_first.at[section + 1, 0],
        ],
        later, later_arrived,
    )
    count, slots = grid_ref.shape[0], mesh_ref.shape[0]
    copies[0].wait()
    proj = dot(grid_ref[...], own[0]).astype(BF16)
    table_out[...] = proj
    fill(table, proj)
    rows = mesh_ref[...]
    copies[1].wait()
    fill(target_out, (dot(rows, own[1]) + row_of(bias_ref, section)).astype(BF16))
    copies[2].wait()
    inner_out[...] = dot(rows, own[2]) + row_of(node_bias_ref, section)
    for copy in copies[3:]:
        copy.wait()
    total_out[...] = jnp.zeros_like(total_out)
    block = pre.shape[0]
    done = below(scalars, count << shift) // block

    def step(index, carry):
        total_out[...] += edge_block(
            index * block, done * block, shift, scalars, keys_ref, table, target_out, pre, later[0], slots
        )
        return carry

    lax.fori_loop(0, done, step, 0)


def encode_local(keys, shift, grid_rows, mesh_rows, weights, section):
    total = keys.shape[1]
    count, width = grid_rows.shape
    slots = mesh_rows.shape[0]
    vmem = pl.BlockSpec(memory_space=pltpu.VMEM)
    return pl.pallas_call(
        functools.partial(encode_local_kernel, section, shift),
        in_specs=[SMEM] + [vmem] * 5 + [HBM] * 4,
        out_shape=[
            pltpu.VMEM((count, width), BF16),
            pltpu.VMEM((round_up(slots, LANES), width), BF16),
            pltpu.VMEM((slots, width), F32),
            pltpu.VMEM((slots, width), F32),
            matrices(5, width),
        ],
        scratch_shapes=[
            pltpu.VMEM((count + WINDOW, width), BF16),
            pltpu.VMEM((math_block(total, BLOCK), width), F32),
            *fetch_scratch(3, width),
            pltpu.SemaphoreType.DMA((5,)),
        ],
        compiler_params=LIMIT,
        name="encode_local",
    )(
        keys, keys, grid_rows, mesh_rows, weights["edge_bias"], weights["node_bias"],
        weights["edge_first"], weights["edge_second"], weights["node_first"], weights["node_second"],
    )


def encode_kernel(section, shift, *refs):
    scalars, keys_ref, local_ref, target, total_ref, inner_ref, stack, mesh_ref = refs[:8]
    pair_ref, right_ref, left_ref, outer_right, outer_left, outer_ref = refs[8:14]
    gain_ref, node_gain_ref, lists_ref = refs[14:17]
    mesh_out, proj_out, up, down, right, left, table, pre, total = refs[17:]
    count, slots = local_ref.shape[0], mesh_ref.shape[0]
    depth = outer_ref.shape[0]
    table[:count] = local_ref[...]
    clear_tail(table, count + 8 * depth)
    pair = side_base()
    outer = 5 - pair
    for ref, start, direction in (
        (pair_ref, 2 * depth, pair + 1),
        (right_ref, 0, 3),
        (right_ref, depth, pair),
        (left_ref, 0, 4),
        (left_ref, depth, pair + 2),
        (outer_right, 0, outer),
        (outer_left, 0, outer + 2),
        (outer_ref, 0, outer + 1),
    ):
        place = pl.multiple_of(count + direction * depth, LANES)
        table[pl.ds(place, depth)] = dot(ref[start : start + depth], stack[1]).astype(BF16)
    total[...] = total_ref[...]
    block = pre.shape[0]
    start = below(scalars, count << shift) // block * block
    used = below(scalars, (count + 8 * depth) << shift)

    def step(index, carry):
        total[...] += edge_block(
            start + index * block, used, shift, scalars, keys_ref, table, target, pre, stack[0], slots
        )
        return carry

    lax.fori_loop(0, (used - start + block - 1) // block, step, 0)
    summed = total[...] * row_of(gain_ref, section)
    fresh = updated(mesh_ref[...], summed, inner_ref[...], stack[2], stack[3], row_of(node_gain_ref, section))
    mesh_out[...] = fresh
    fill(proj_out, dot(fresh, stack[4]).astype(BF16))
    list_rows(proj_out, lists_ref, (up, down, right, left))


def encode(keys, shift, prepared, mesh_rows, remote, lists, depth, weights, section):
    edges = keys.shape[1]
    prepared = [near(value) for value in prepared]
    count, width = prepared[0].shape
    slots = mesh_rows.shape[0]
    vmem = pl.BlockSpec(memory_space=pltpu.VMEM)
    rows = count + 8 * remote[-1].shape[0]
    return pl.pallas_call(
        functools.partial(encode_kernel, section, shift),
        in_specs=[SMEM] + [vmem] * 16,
        out_shape=[
            pltpu.VMEM((slots, width), BF16),
            pltpu.VMEM((round_up(slots, LANES), width), BF16),
        ]
        + send_shapes(depth, width),
        scratch_shapes=[
            pltpu.VMEM((rows + WINDOW, width), BF16),
            pltpu.VMEM((math_block(edges, BLOCK), width), F32),
            pltpu.VMEM((slots, width), F32),
        ],
        compiler_params=LIMIT,
        name="encode",
    )(keys, keys, *prepared, mesh_rows, *remote, weights["edge_gain"], weights["node_gain"], lists)


def prepare_kernel(
    section, mesh_ref, bias_ref, node_bias_ref, edge_first, edge_second, node_first, node_second,
    target_out, inner_out, later, own, arrived, later_arrived,
):
    copies = fetch([edge_first.at[section, 1], node_first.at[section, 0]], own, arrived)
    copies += fetch(
        [
            edge_second.at[section], node_first.at[section, 1], node_second.at[section],
            edge_first.at[section + 1, 0],
        ],
        later, later_arrived,
    )
    rows = mesh_ref[...]
    copies[0].wait()
    fill(target_out, (dot(rows, own[0]) + row_of(bias_ref, section)).astype(BF16))
    copies[1].wait()
    inner_out[...] = dot(rows, own[1]) + row_of(node_bias_ref, section)
    for copy in copies[2:]:
        copy.wait()


def prepare(mesh_rows, weights, section):
    slots, width = mesh_rows.shape
    vmem = pl.BlockSpec(memory_space=pltpu.VMEM)
    return pl.pallas_call(
        functools.partial(prepare_kernel, section),
        in_specs=[vmem] * 3 + [HBM] * 4,
        out_shape=[
            pltpu.VMEM((round_up(slots, LANES), width), BF16),
            pltpu.VMEM((slots, width), F32),
            matrices(4, width),
        ],
        scratch_shapes=fetch_scratch(2, width) + [pltpu.SemaphoreType.DMA((4,))],
        compiler_params=LIMIT,
        name="prepare",
    )(
        near(mesh_rows), weights["edge_bias"], weights["node_bias"],
        weights["edge_first"], weights["edge_second"], weights["node_first"], weights["node_second"],
    )


def place_remote(table, remote, places, base):
    for ref, slots in zip(remote, places):
        depth = ref.shape[1]
        for index, slot in enumerate(slots):
            place = base + slot * depth
            table[place : place + depth] = ref[index]


def round_kernel(section, places, last, *refs):
    edges_ref, local_ref, target, inner_ref, stack, mesh_ref = refs[:6]
    remote = refs[6 : 6 + len(places)]
    gain_ref, node_gain_ref, lists_ref, owned_ref = refs[6 + len(places) : 10 + len(places)]
    rest = refs[10 + len(places) :]
    mesh_out, proj_out = rest[:2]
    sends = rest[2:-1]
    table = rest[-1]
    if last:
        masked_out, sends = sends[0], sends[1:]
    slots, padded = mesh_ref.shape[0], local_ref.shape[0]
    table[:padded] = local_ref[...]
    place_remote(table, remote, places, padded)
    edges = edges_ref.shape[2]
    block = math_block(edges, 1536)
    summed = None
    for start in range(0, edges, block):
        senders = edges_ref[0, 0:1, start : start + block]
        senders = jnp.where(senders < slots, senders, senders + (padded - slots))
        targets = edges_ref[0, 1:2, start : start + block]
        pre = dot(one_hot(column(senders), table.shape[0]), table[...]) + dot(
            one_hot(column(targets), padded), target[...]
        )
        part = added(pre, targets, stack[0], slots)
        summed = part if summed is None else summed + part
    summed = summed * row_of(gain_ref, section)
    fresh = updated(mesh_ref[...], summed, inner_ref[...], stack[1], stack[2], row_of(node_gain_ref, section))
    mesh_out[...] = fresh
    if last:
        alive = lax.broadcasted_iota(jnp.int32, fresh.shape, 0) < owned_ref[0]
        masked_out[...] = jnp.where(alive, fresh, jnp.zeros_like(fresh))
    fill(proj_out, dot(fresh, stack[3]).astype(BF16))
    list_rows(proj_out, lists_ref, sends)


def round_part(edges, local, prepared, mesh_rows, remote, places, lists, owned, sends, weights, section):
    slots, width = mesh_rows.shape
    last = section == 2
    padded = local.shape[0]
    table_rows = padded + sum(r.shape[0] * r.shape[1] for r in remote)
    out_shape = [pltpu.VMEM((slots, width), BF16), pltpu.VMEM((padded, width), BF16)]
    if last:
        out_shape.append(jax.ShapeDtypeStruct((slots, width), BF16))
    vmem = pl.BlockSpec(memory_space=pltpu.VMEM)
    return pl.pallas_call(
        functools.partial(round_kernel, section, places, last),
        in_specs=[vmem] * (9 + len(remote)) + [SMEM],
        out_shape=out_shape + sends,
        scratch_shapes=[pltpu.VMEM((table_rows, width), BF16)],
        compiler_params=LIMIT,
        name="round_part",
    )(
        edges, near(local), *[near(value) for value in prepared], near(mesh_rows), *remote,
        weights["edge_gain"], weights["node_gain"], lists, owned,
    )


def decode_local_kernel(
    section, grid_ref, table_ref, edges_ref, bias_ref, edge_first, edge_second, node_first, node_second,
    pre_ref, later, own, arrived, later_arrived,
):
    copies = fetch([edge_first.at[section, 1]], own, arrived)
    copies += fetch(
        [
            edge_second.at[section], node_first.at[section, 0], node_first.at[section, 1],
            node_second.at[section],
        ],
        later, later_arrived,
    )
    copies[0].wait()
    count = grid_ref.shape[0]
    block = math_block(count, 512)
    for start in range(0, count, block):
        target = dot(grid_ref[start : start + block], own[0]) + row_of(bias_ref, section)
        for sender in range(edges_ref.shape[1]):
            ids = column(edges_ref[0, sender : sender + 1, start : start + block])
            pre = dot(one_hot(ids, table_ref.shape[0]), table_ref[...]) + target
            pre_ref[sender, start : start + block] = pre.astype(BF16)
    for copy in copies[1:]:
        copy.wait()


def decode_local(grid_rows, table, edges, weights, section):
    count, width = grid_rows.shape
    senders = edges.shape[1]
    vmem = pl.BlockSpec(memory_space=pltpu.VMEM)
    return pl.pallas_call(
        functools.partial(decode_local_kernel, section),
        in_specs=[vmem] * 4 + [HBM] * 4,
        out_shape=[pltpu.VMEM((senders, count, width), BF16), matrices(4, width)],
        scratch_shapes=fetch_scratch(1, width) + [pltpu.SemaphoreType.DMA((4,))],
        compiler_params=LIMIT,
        name="decode_local",
    )(
        grid_rows, near(table), edges, weights["edge_bias"],
        weights["edge_first"], weights["edge_second"], weights["node_first"], weights["node_second"],
    )


def decode_kernel(section, places, split, *refs):
    pre_ref, stack, grid_ref, edges_ref = refs[:4]
    remote = refs[4 : 4 + len(places)]
    gain_ref, node_bias_ref, node_gain_ref, out_ref, table, ready, sent = refs[4 + len(places) :]
    place_remote(table, remote, places, 0)
    count = grid_ref.shape[0]
    block = math_block(count, 512)
    copies = []
    for index, start in enumerate(range(0, count, block)):
        part = slice(start, start + block)
        summed = None
        for sender in range(edges_ref.shape[1]):
            ids = column(edges_ref[0, sender : sender + 1, part])
            pre = pre_ref[sender, part].astype(F32) + dot(one_hot(ids, table.shape[0], split), table[...])
            message = normed(dot(silu(pre).astype(BF16), stack[0])).astype(BF16).astype(F32)
            summed = message if summed is None else summed + message
        rows = grid_ref[part]
        summed = (summed * row_of(gain_ref, section)).astype(BF16)
        inner = dot(rows, stack[1]) + dot(summed, stack[2]) + row_of(node_bias_ref, section)
        update = normed(dot(silu(inner).astype(BF16), stack[3])) * row_of(node_gain_ref, section)
        ready[part] = (rows.astype(F32) + update).astype(BF16)
        copies.append(pltpu.make_async_copy(ready.at[part], out_ref.at[part], sent.at[index]))
        copies[-1].start()
    for copy in copies:
        copy.wait()


def decode_part(prepared, grid_rows, edges, remote, places, weights, section, split):
    count, width = grid_rows.shape
    table_rows = sum(r.shape[0] * r.shape[1] for r in remote)
    vmem = pl.BlockSpec(memory_space=pltpu.VMEM)
    return pl.pallas_call(
        functools.partial(decode_kernel, section, places, split),
        in_specs=[vmem] * (7 + len(remote)),
        out_specs=pl.BlockSpec(memory_space=pl.ANY),
        out_shape=jax.ShapeDtypeStruct((count, width), BF16),
        scratch_shapes=[
            pltpu.VMEM((table_rows, width), BF16),
            pltpu.VMEM((count, width), BF16),
            pltpu.SemaphoreType.DMA((count // math_block(count, 512),)),
        ],
        compiler_params=LIMIT,
        name="decode_part",
    )(
        *[near(value) for value in prepared], grid_rows, edges, *remote,
        weights["edge_gain"], weights["node_bias"], weights["node_gain"],
    )


def move(value, target):
    bands, sectors = lax.axis_size("aa"), lax.axis_size("ba")
    pairs = []
    for i in range(bands):
        for j in range(sectors):
            band, sector = target(i, j)
            pairs.append((i * sectors + j, band % bands * sectors + sector % sectors))
    return lax.ppermute(value, AXES, pairs)


def join_kernel(up_ref, down_ref, right_ref, left_ref, right_out, left_out):
    for index, (own, out) in enumerate(((right_ref, right_out), (left_ref, left_out))):
        out[0] = own[0]
        out[1] = up_ref[index]
        out[2] = down_ref[index]


def halo(up, down, right, left):
    from_up = move(up, lambda i, j: (i + 1, j))
    from_down = move(down, lambda i, j: (i - 1, j))
    joined = jax.ShapeDtypeStruct((3,) + right.shape[1:], BF16)
    right, left = pl.pallas_call(
        join_kernel, out_shape=[joined, joined], compiler_params=LIMIT, name="join"
    )(from_up, from_down, right, left)
    from_left = move(right, lambda i, j: (i, j + 1))
    from_right = move(left, lambda i, j: (i, j - 1))
    return [from_up[2:3], from_down[2:3], from_left, from_right], ((1,), (6,), (3, 0, 5), (4, 2, 7))


def per_device(
    grid_nodes, mesh_nodes, owned_nodes, grid_rim, mesh_rim, long_send, g2m_edges, short_edges,
    long_edges, m2g_edges, edge_first, edge_second, edge_bias, edge_gain, node_first, node_second,
    node_bias, node_gain,
):
    weights = dict(
        edge_bias=edge_bias, edge_gain=edge_gain, node_bias=node_bias, node_gain=node_gain,
        edge_first=stay(edge_first), edge_second=stay(edge_second),
        node_first=stay(node_first), node_second=stay(node_second),
    )
    width = grid_nodes.shape[1]
    slots = mesh_nodes.shape[0]
    depth = mesh_rim.shape[2]
    peers, listed = long_send.shape[1:]

    remote, keys, shift = grid_halo(grid_nodes, grid_rim, g2m_edges, slots)
    rim_lists = jnp.concatenate([mesh_rim[0, m : m + 1] for m in SEND_ORDER], 0).reshape(1, 8 * depth)
    long_lists = long_send.reshape(1, peers * listed)
    rim_sends = send_shapes(depth, width)
    prepared = encode_local(keys, shift, grid_nodes, mesh_nodes, weights, 0)
    mesh_one, proj, *sends = encode(keys, shift, prepared, mesh_nodes, remote, rim_lists, depth, weights, 0)

    remote, places = halo(*sends)
    prepared = prepare(mesh_one, weights, 1)
    mesh_two, proj, sent = round_part(
        short_edges, proj, prepared, mesh_one, remote, places, long_lists, owned_nodes,
        [jax.ShapeDtypeStruct((peers * listed, width), BF16)], weights, 1,
    )

    sent = sent.reshape(peers, listed, width)
    arrived = lax.all_to_all(sent, AXES, split_axis=0, concat_axis=0, tiled=True)
    prepared = prepare(mesh_two, weights, 2)
    mesh_three, proj, mesh_out, *sends = round_part(
        long_edges, proj, prepared, mesh_two, [arrived.reshape(1, peers * listed, width)], ((0,),),
        rim_lists, owned_nodes, rim_sends, weights, 2,
    )

    remote, places = halo(*sends)
    prepared = decode_local(grid_nodes, proj, m2g_edges, weights, 3)
    grid_out = decode_part(prepared, grid_nodes, m2g_edges, remote, places, weights, 3, slots)
    return grid_out, mesh_out


def solution(mesh):
    rows = P(AXES, None)
    lists = P(AXES, None, None)
    in_specs = (rows, rows, P(AXES)) + (lists,) * 7 + (P(),) * 8
    return jax.shard_map(
        per_device, mesh=mesh, in_specs=in_specs, out_specs=(rows, rows), check_vma=False
    )
```

```python
import functools

import jax
import jax.numpy as jnp
from jax import lax
from jax.experimental import pallas as pl
from jax.experimental.pallas import tpu as pltpu
from jax.sharding import PartitionSpec as P

EPSILON = 1e-05
AXES = ("aa", "ba")
LANES = 128
BF16 = jnp.bfloat16
F32 = jnp.float32
LIMIT = pltpu.CompilerParams(vmem_limit_bytes=28 * 1024 * 1024)

UP_LISTS = (7, 5, 6)
DOWN_LISTS = (2, 0, 1)
RIGHT_LIST = 4
LEFT_LIST = 3
SEND_ORDER = UP_LISTS + DOWN_LISTS + (RIGHT_LIST, LEFT_LIST)


def dot(left, right):
    return jnp.dot(left, right, preferred_element_type=F32)


def math_block(total, most):
    block = most
    while total % block:
        block -= LANES
    return block


def round_up(value, unit):
    return -(-value // unit) * unit


def column(row):
    tall = jnp.broadcast_to(row, (LANES, row.shape[1]))
    return jnp.transpose(tall).astype(jnp.int16)


def one_hot(ids, width, base=0):
    lane = lax.broadcasted_iota(jnp.int16, ids.shape, 1)
    parts = [
        jnp.where(ids == lane + jnp.int16(base + start), BF16(1), BF16(0))
        for start in range(0, width, LANES)
    ]
    return parts[0] if len(parts) == 1 else jnp.concatenate(parts, 1)


def silu(value):
    half = 0.5 * value
    return half + half * jnp.tanh(half)


def normed(value):
    average = jnp.mean(value, axis=-1, keepdims=True)
    centred = value - average
    spread = jnp.mean(centred * centred, axis=-1, keepdims=True)
    return centred * lax.rsqrt(spread + EPSILON)


def whole(shape):
    return pl.BlockSpec(shape, lambda *_: (0,) * len(shape))


def cost(macs, moved):
    return pl.CostEstimate(flops=2 * macs, bytes_accessed=moved, transcendentals=0)


HBM = pl.BlockSpec(memory_space=pltpu.HBM)
SMEM = pl.BlockSpec(memory_space=pltpu.SMEM)


def stay(stack):
    return pltpu.with_memory_space_constraint(stack, pltpu.HBM)


def near(value):
    return pltpu.with_memory_space_constraint(value, pltpu.VMEM)


def held(value, section):
    return pltpu.with_memory_space_constraint(value, place_of(section))


def place_of(section):
    return pltpu.HBM if section == 2 else pltpu.VMEM


def fetch(sources, buffers, arrived):
    copies = [
        pltpu.make_async_copy(source, buffers.at[i], arrived.at[i]) for i, source in enumerate(sources)
    ]
    for copy in copies:
        copy.start()
    return copies


def fetch_scratch(count, width):
    return [pltpu.VMEM((count, width, width), BF16), pltpu.SemaphoreType.DMA((count,))]


def matrices(count, width):
    return pltpu.VMEM((count, width, width), BF16)


def fill(ref, value):
    rows = value.shape[0]
    ref[:rows] = value
    if ref.shape[0] > rows:
        ref[rows:] = jnp.zeros((ref.shape[0] - rows, ref.shape[1]), ref.dtype)


def clear_tail(ref, rows):
    ref[rows:] = jnp.zeros((ref.shape[0] - rows, ref.shape[1]), ref.dtype)


def row_of(ref, index):
    return ref[index : index + 1]


def added(pre, targets, second, slots):
    hidden = silu(pre).astype(BF16)
    message = normed(dot(hidden, second)).astype(BF16)
    member = lax.broadcasted_iota(jnp.int32, (slots, targets.shape[1]), 0) == targets
    return dot(member.astype(BF16), message)


def updated(rows, total, inner, first, second, gain):
    inner = inner + dot(total.astype(BF16), first)
    update = normed(dot(silu(inner).astype(BF16), second)) * gain
    return (rows.astype(F32) + update).astype(BF16)


def side_base():
    return jnp.where(lax.axis_index("aa") % 2 == 0, 5, 0)


def send_shapes(depth, width):
    return [jax.ShapeDtypeStruct((n, depth, width), BF16) for n in (3, 3, 1, 1)]


def list_rows(proj_out, lists_ref, sends):
    if len(lists_ref.shape) == 3:
        ids = jnp.concatenate([column(lists_ref[0, m : m + 1]) for m in SEND_ORDER], 0)
    else:
        ids = column(lists_ref[...])
    listed = ids.shape[0]
    size = math_block(listed, 256)
    made = []
    for start in range(0, listed, size):
        picked = one_hot(ids[start : start + size], proj_out.shape[0])
        made.append(dot(picked, proj_out[...]).astype(BF16))
    made = made[0] if len(made) == 1 else jnp.concatenate(made, 0)
    place = 0
    for ref in sends:
        if len(ref.shape) == 2:
            ref[...] = made
            continue
        depth = ref.shape[1]
        for index in range(ref.shape[0]):
            ref[index] = made[place : place + depth]
            place += depth


def pick_kernel(rows_hbm, rim_hbm, pair_out, *refs):
    singles, (rows, rim, rows_here, rim_here) = refs[:5], refs[5:]
    depth = singles[0].shape[0]
    parts = rows_here.shape[0]
    size = rows.shape[0] // parts
    copies = [pltpu.make_async_copy(rim_hbm, rim, rim_here.at[0])]
    for part in range(parts):
        span = pl.ds(part * size, size)
        copies.append(pltpu.make_async_copy(rows_hbm.at[span], rows.at[span], rows_here.at[part]))
    for copy in copies:
        copy.start()
    pair = side_base()
    outer = 5 - pair
    chosen = [pair + 2, pair, pair + 1, RIGHT_LIST, LEFT_LIST, outer + 2, outer, outer + 1]
    copies[0].wait()
    ids = [column(rim[0, pl.ds(index, 1), :]) for index in chosen]
    picked = [None] * len(ids)
    for part in range(parts):
        copies[part + 1].wait()
        values = rows[part * size : (part + 1) * size]
        for index, listed in enumerate(ids):
            found = dot(one_hot(listed, size, part * size), values)
            picked[index] = found if part == 0 else picked[index] + found
    for index in range(3):
        pair_out[index * depth : (index + 1) * depth] = picked[index].astype(BF16)
    for out, found in zip(singles, picked[3:]):
        out[...] = found.astype(BF16)


def pick_grid(rows, rim):
    count, width = rows.shape
    depth = rim.shape[2]
    parts = count // 256 if count % 256 == 0 else 1
    block = pltpu.VMEM((depth, width), BF16)
    return pl.pallas_call(
        pick_kernel,
        in_specs=[HBM, HBM],
        out_shape=[pltpu.VMEM((3 * depth, width), BF16)] + [block] * 5,
        scratch_shapes=[
            pltpu.VMEM((count, width), BF16),
            pltpu.VMEM(rim.shape, jnp.int32),
            pltpu.SemaphoreType.DMA((parts,)),
            pltpu.SemaphoreType.DMA((1,)),
        ],
        compiler_params=LIMIT,
        name="pick_grid",
    )(stay(rows), stay(rim))


def pair_join_kernel(pair_ref, right_ref, left_ref, right_out, left_out):
    depth = right_ref.shape[0]
    for index, (own, out) in enumerate(((right_ref, right_out), (left_ref, left_out))):
        out[:depth] = own[...]
        out[depth:] = pair_ref[index * depth : (index + 1) * depth]


def pair_join(pair, right, left):
    depth, width = right.shape
    return pl.pallas_call(
        pair_join_kernel,
        out_shape=[pltpu.VMEM((2 * depth, width), BF16)] * 2,
        compiler_params=LIMIT,
        name="pair_join",
    )(pair, right, left)


def grid_halo(rows, rim):
    pair, right, left, *outer = pick_grid(rows, rim)
    pair = move(pair, lambda i, j: (i ^ 1, j))
    right, left = pair_join(pair, right, left)
    other = lambda i: i + 1 if i % 2 else i - 1
    remote = [
        pair,
        move(right, lambda i, j: (i, j + 1)),
        move(left, lambda i, j: (i, j - 1)),
        move(outer[0], lambda i, j: (other(i), j + 1)),
        move(outer[1], lambda i, j: (other(i), j - 1)),
        move(outer[2], lambda i, j: (other(i), j)),
    ]
    return remote, right


def encode_local_kernel(
    section, grid_hbm, mesh_ref, edges_ref, bias_ref, node_bias_ref, gain_ref, node_gain_ref, after_ref,
    edge_first, edge_second, node_first, node_second,
    pre_out, inner_out, later, edges_out, mesh_out, gains_out,
    grid_rows, table, target, own, grid_arrived, arrived, later_arrived,
):
    grid_copy = pltpu.make_async_copy(grid_hbm, grid_rows, grid_arrived.at[0])
    grid_copy.start()
    copies = fetch(
        [edge_first.at[section, 1], edge_first.at[section, 0], node_first.at[section, 0]], own, arrived
    )
    copies += fetch(
        [
            edge_first.at[section, 0], edge_second.at[section], node_first.at[section, 1],
            node_second.at[section], edge_first.at[section + 1, 0],
        ],
        later, later_arrived,
    )
    edges_out[...] = edges_ref[...]
    gains_out[0:1] = row_of(gain_ref, section)
    gains_out[1:2] = row_of(node_gain_ref, section)
    rows = mesh_ref[...]
    mesh_out[...] = rows
    copies[0].wait()
    fill(target, (dot(rows, own[0]) + row_of(bias_ref, section)).astype(BF16))
    grid_copy.wait()
    copies[1].wait()
    fill(table, dot(grid_rows[...], own[1]).astype(BF16))
    edges = edges_ref.shape[2]
    block = math_block(edges, 1024)
    for start in range(0, edges, block):
        part = slice(start, start + block)
        senders = column(edges_ref[0, 0:1, part])
        targets = column(edges_ref[0, 1:2, part])
        pre_out[part] = dot(one_hot(senders, table.shape[0]), table[...]) + dot(
            one_hot(targets, target.shape[0]), target[...]
        )
    copies[2].wait()
    inner_out[...] = dot(rows, own[2]) + row_of(node_bias_ref, section)
    for copy in copies[3:]:
        copy.wait()


def encode_local(grid_rows, mesh_rows, edges, after, weights, section):
    total = edges.shape[2]
    count, width = grid_rows.shape
    slots = mesh_rows.shape[0]
    vmem = pl.BlockSpec(memory_space=pltpu.VMEM)
    return pl.pallas_call(
        functools.partial(encode_local_kernel, section),
        in_specs=[HBM] + [vmem] * 6 + [pl.BlockSpec(memory_space=pl.ANY)] + [HBM] * 4,
        out_shape=[
            pltpu.VMEM((total, width), F32),
            pltpu.VMEM((slots, width), F32),
            matrices(5, width),
            pltpu.VMEM(edges.shape, edges.dtype),
            pltpu.VMEM(mesh_rows.shape, BF16),
            pltpu.VMEM((2, width), F32),
        ],
        scratch_shapes=[
            pltpu.VMEM((count, width), BF16),
            pltpu.VMEM((round_up(count, LANES), width), BF16),
            pltpu.VMEM((round_up(slots, LANES), width), BF16),
            pltpu.VMEM((3, width, width), BF16),
            pltpu.SemaphoreType.DMA((1,)),
            pltpu.SemaphoreType.DMA((3,)),
            pltpu.SemaphoreType.DMA((5,)),
        ],
        compiler_params=LIMIT,
        name="encode_local",
    )(
        stay(grid_rows), stay(mesh_rows), stay(edges), stay(weights["edge_bias"]), stay(weights["node_bias"]),
        stay(weights["edge_gain"]), stay(weights["node_gain"]), after,
        weights["edge_first"], weights["edge_second"], weights["node_first"], weights["node_second"],
    )


def halo_part(pre, edges_ref, part, table, base):
    senders = edges_ref[0, 0:1, part] - base
    return pre + dot(one_hot(column(senders), table.shape[0]), table[...])


def encode_sides_kernel(count, pre_ref, edges_ref, stack, pair_ref, right_ref, left_ref, pre_out, table):
    depth = right_ref.shape[0] // 2
    pair = side_base()
    first = jnp.where(pair == 0, 0, 3)
    for ref, start, direction in (
        (pair_ref, 2 * depth, pair + 1),
        (right_ref, 0, 3),
        (right_ref, depth, pair),
        (left_ref, 0, 4),
        (left_ref, depth, pair + 2),
    ):
        place = pl.multiple_of((direction - first) * depth, LANES)
        table[pl.ds(place, depth)] = dot(ref[start : start + depth], stack[0]).astype(BF16)
    edges = pre_ref.shape[0]
    block = math_block(edges, 1024)
    for start in range(0, edges, block):
        part = slice(start, start + block)
        pre_out[part] = halo_part(pre_ref[part], edges_ref, part, table, count + first * depth)


def encode_sides(pre, edges, stack, remote, count):
    depth, width = remote[1].shape[0] // 2, pre.shape[1]
    return pl.pallas_call(
        functools.partial(encode_sides_kernel, count),
        out_shape=pltpu.VMEM(pre.shape, F32),
        scratch_shapes=[pltpu.VMEM((5 * depth, width), BF16)],
        input_output_aliases={0: 0},
        compiler_params=LIMIT,
        name="encode_sides",
    )(near(pre), near(edges), near(stack), *remote)


def encode_kernel(count, *refs):
    pre_ref, edges_ref, stack, inner_ref, mesh_ref, outer_right, outer_left, outer_ref = refs[:8]
    gains_ref, lists_ref = refs[8:10]
    mesh_out, proj_out, up, down, right, left, table = refs[10:]
    slots = mesh_ref.shape[0]
    depth = outer_ref.shape[0]
    for index, ref in enumerate((outer_right, outer_ref, outer_left)):
        table[index * depth : (index + 1) * depth] = dot(ref[...], stack[0]).astype(BF16)
    base = count + (5 - side_base()) * depth
    edges = pre_ref.shape[0]
    block = math_block(edges, 1024)
    summed = None
    for start in range(0, edges, block):
        part = slice(start, start + block)
        pre = halo_part(pre_ref[part], edges_ref, part, table, base)
        made = added(pre, edges_ref[0, 1:2, part], stack[1], slots)
        summed = made if summed is None else summed + made
    summed = summed * row_of(gains_ref, 0)
    fresh = updated(mesh_ref[...], summed, inner_ref[...], stack[2], stack[3], row_of(gains_ref, 1))
    mesh_out[...] = fresh
    fill(proj_out, dot(fresh, stack[4]).astype(BF16))
    list_rows(proj_out, lists_ref, (up, down, right, left))


def encode(prepared, remote, lists, depth, count):
    pre, inner, stack, edges, mesh_rows, gains = [near(value) for value in prepared]
    slots, width = mesh_rows.shape
    pre = near(encode_sides(pre, edges, stack, remote[:3], count))
    return pl.pallas_call(
        functools.partial(encode_kernel, count),
        out_shape=[
            pltpu.VMEM((slots, width), BF16),
            pltpu.VMEM((round_up(slots, LANES), width), BF16),
        ]
        + send_shapes(depth, width),
        scratch_shapes=[pltpu.VMEM((3 * remote[-1].shape[0], width), BF16)],
        compiler_params=LIMIT,
        name="encode",
    )(pre, edges, stack, inner, mesh_rows, *remote[3:], gains, lists)


def prepare_kernel(
    section, mesh_ref, bias_ref, node_bias_ref, edge_first, edge_second, node_first, node_second,
    target_out, inner_out, later, own, arrived, later_arrived,
):
    copies = fetch([edge_first.at[section, 1], node_first.at[section, 0]], own, arrived)
    copies += fetch(
        [
            edge_second.at[section], node_first.at[section, 1], node_second.at[section],
            edge_first.at[section + 1, 0],
        ],
        later, later_arrived,
    )
    rows = mesh_ref[...]
    copies[0].wait()
    fill(target_out, (dot(rows, own[0]) + row_of(bias_ref, section)).astype(BF16))
    copies[1].wait()
    inner_out[...] = dot(rows, own[1]) + row_of(node_bias_ref, section)
    for copy in copies[2:]:
        copy.wait()


def prepare(mesh_rows, weights, section):
    slots, width = mesh_rows.shape
    vmem = pl.BlockSpec(memory_space=pltpu.VMEM)
    return pl.pallas_call(
        functools.partial(prepare_kernel, section),
        in_specs=[vmem] * 3 + [HBM] * 4,
        out_shape=[
            place_of(section)((round_up(slots, LANES), width), BF16),
            place_of(section)((slots, width), F32),
            matrices(4, width),
        ],
        scratch_shapes=fetch_scratch(2, width) + [pltpu.SemaphoreType.DMA((4,))],
        compiler_params=LIMIT,
        name="prepare",
    )(
        held(mesh_rows, section), weights["edge_bias"], weights["node_bias"],
        weights["edge_first"], weights["edge_second"], weights["node_first"], weights["node_second"],
    )


def place_remote(table, remote, places, base):
    for ref, slots in zip(remote, places):
        depth = ref.shape[1]
        for index, slot in enumerate(slots):
            place = base + slot * depth
            table[place : place + depth] = ref[index]


def round_kernel(section, places, last, *refs):
    edges_ref, local_ref, target, inner_ref, stack, mesh_ref = refs[:6]
    remote = refs[6 : 6 + len(places)]
    gain_ref, node_gain_ref, lists_ref, owned_ref = refs[6 + len(places) : 10 + len(places)]
    rest = refs[10 + len(places) :]
    mesh_out, proj_out = rest[:2]
    sends = rest[2:-1]
    table = rest[-1]
    if last:
        masked_out, sends = sends[0], sends[1:]
    slots, padded = mesh_ref.shape[0], local_ref.shape[0]
    table[:padded] = local_ref[...]
    place_remote(table, remote, places, padded)
    edges = edges_ref.shape[2]
    block = math_block(edges, 1536)
    summed = None
    for start in range(0, edges, block):
        senders = edges_ref[0, 0:1, start : start + block]
        senders = jnp.where(senders < slots, senders, senders + (padded - slots))
        targets = edges_ref[0, 1:2, start : start + block]
        pre = dot(one_hot(column(senders), table.shape[0]), table[...]) + dot(
            one_hot(column(targets), padded), target[...]
        )
        part = added(pre, targets, stack[0], slots)
        summed = part if summed is None else summed + part
    summed = summed * row_of(gain_ref, section)
    fresh = updated(mesh_ref[...], summed, inner_ref[...], stack[1], stack[2], row_of(node_gain_ref, section))
    mesh_out[...] = fresh
    if last:
        alive = lax.broadcasted_iota(jnp.int32, fresh.shape, 0) < owned_ref[0]
        masked_out[...] = jnp.where(alive, fresh, jnp.zeros_like(fresh))
    fill(proj_out, dot(fresh, stack[3]).astype(BF16))
    list_rows(proj_out, lists_ref, sends)


def round_part(edges, local, prepared, mesh_rows, remote, places, lists, owned, sends, weights, section):
    slots, width = mesh_rows.shape
    last = section == 2
    padded = local.shape[0]
    table_rows = padded + sum(r.shape[0] * r.shape[1] for r in remote)
    space = place_of(section + 1)
    out_shape = [space((slots, width), BF16), space((padded, width), BF16)]
    if last:
        out_shape.append(jax.ShapeDtypeStruct((slots, width), BF16))
    vmem = pl.BlockSpec(memory_space=pltpu.VMEM)
    return pl.pallas_call(
        functools.partial(round_kernel, section, places, last),
        in_specs=[vmem] * (9 + len(remote)) + [SMEM],
        out_shape=out_shape + sends,
        scratch_shapes=[pltpu.VMEM((table_rows, width), BF16)],
        compiler_params=LIMIT,
        name="round_part",
    )(
        edges, held(local, section), *[held(value, section) for value in prepared[:2]], near(prepared[2]),
        held(mesh_rows, section), *remote,
        weights["edge_gain"], weights["node_gain"], lists, owned,
    )


def decode_local_kernel(
    section, grid_ref, table_ref, edges_ref, bias_ref, edge_first, edge_second, node_first, node_second,
    pre_ref, later, own, arrived, later_arrived,
):
    copies = fetch([edge_first.at[section, 1]], own, arrived)
    copies += fetch(
        [
            edge_second.at[section], node_first.at[section, 0], node_first.at[section, 1],
            node_second.at[section],
        ],
        later, later_arrived,
    )
    copies[0].wait()
    count = grid_ref.shape[0]
    block = math_block(count, 512)
    for start in range(0, count, block):
        target = dot(grid_ref[start : start + block], own[0]) + row_of(bias_ref, section)
        for sender in range(edges_ref.shape[1]):
            ids = column(edges_ref[0, sender : sender + 1, start : start + block])
            pre = dot(one_hot(ids, table_ref.shape[0]), table_ref[...]) + target
            pre_ref[sender, start : start + block] = pre.astype(BF16)
    for copy in copies[1:]:
        copy.wait()


def decode_local(grid_rows, table, edges, weights, section):
    count, width = grid_rows.shape
    senders = edges.shape[1]
    vmem = pl.BlockSpec(memory_space=pltpu.VMEM)
    return pl.pallas_call(
        functools.partial(decode_local_kernel, section),
        in_specs=[vmem] * 4 + [HBM] * 4,
        out_shape=[pltpu.VMEM((senders, count, width), BF16), matrices(4, width)],
        scratch_shapes=fetch_scratch(1, width) + [pltpu.SemaphoreType.DMA((4,))],
        compiler_params=LIMIT,
        name="decode_local",
    )(
        grid_rows, near(table), edges, weights["edge_bias"],
        weights["edge_first"], weights["edge_second"], weights["node_first"], weights["node_second"],
    )


def decode_kernel(section, places, split, *refs):
    pre_ref, stack, grid_ref, edges_ref = refs[:4]
    remote = refs[4 : 4 + len(places)]
    gain_ref, node_bias_ref, node_gain_ref, out_ref, table, ready, sent = refs[4 + len(places) :]
    place_remote(table, remote, places, 0)
    count = grid_ref.shape[0]
    block = math_block(count, 512)
    copies = []
    for index, start in enumerate(range(0, count, block)):
        part = slice(start, start + block)
        summed = None
        for sender in range(edges_ref.shape[1]):
            ids = column(edges_ref[0, sender : sender + 1, part])
            pre = pre_ref[sender, part].astype(F32) + dot(one_hot(ids, table.shape[0], split), table[...])
            message = normed(dot(silu(pre).astype(BF16), stack[0])).astype(BF16).astype(F32)
            summed = message if summed is None else summed + message
        rows = grid_ref[part]
        summed = (summed * row_of(gain_ref, section)).astype(BF16)
        inner = dot(rows, stack[1]) + dot(summed, stack[2]) + row_of(node_bias_ref, section)
        update = normed(dot(silu(inner).astype(BF16), stack[3])) * row_of(node_gain_ref, section)
        ready[part] = (rows.astype(F32) + update).astype(BF16)
        copies.append(pltpu.make_async_copy(ready.at[part], out_ref.at[part], sent.at[index]))
        copies[-1].start()
    for copy in copies:
        copy.wait()


def decode_part(prepared, grid_rows, edges, remote, places, weights, section, split):
    count, width = grid_rows.shape
    table_rows = sum(r.shape[0] * r.shape[1] for r in remote)
    vmem = pl.BlockSpec(memory_space=pltpu.VMEM)
    return pl.pallas_call(
        functools.partial(decode_kernel, section, places, split),
        in_specs=[vmem] * (7 + len(remote)),
        out_specs=pl.BlockSpec(memory_space=pl.ANY),
        out_shape=jax.ShapeDtypeStruct((count, width), BF16),
        scratch_shapes=[
            pltpu.VMEM((table_rows, width), BF16),
            pltpu.VMEM((count, width), BF16),
            pltpu.SemaphoreType.DMA((count // math_block(count, 512),)),
        ],
        compiler_params=LIMIT,
        name="decode_part",
    )(
        *[near(value) for value in prepared], grid_rows, edges, *remote,
        weights["edge_gain"], weights["node_bias"], weights["node_gain"],
    )


def move(value, target):
    bands, sectors = lax.axis_size("aa"), lax.axis_size("ba")
    pairs = []
    for i in range(bands):
        for j in range(sectors):
            band, sector = target(i, j)
            pairs.append((i * sectors + j, band % bands * sectors + sector % sectors))
    return lax.ppermute(value, AXES, pairs)


def join_kernel(up_ref, down_ref, right_ref, left_ref, right_out, left_out):
    for index, (own, out) in enumerate(((right_ref, right_out), (left_ref, left_out))):
        out[0] = own[0]
        out[1] = up_ref[index]
        out[2] = down_ref[index]


def halo(up, down, right, left):
    from_up = move(up, lambda i, j: (i + 1, j))
    from_down = move(down, lambda i, j: (i - 1, j))
    joined = jax.ShapeDtypeStruct((3,) + right.shape[1:], BF16)
    right, left = pl.pallas_call(
        join_kernel, out_shape=[joined, joined], compiler_params=LIMIT, name="join"
    )(from_up, from_down, right, left)
    from_left = move(right, lambda i, j: (i, j + 1))
    from_right = move(left, lambda i, j: (i, j - 1))
    return [from_up[2:3], from_down[2:3], from_left, from_right], ((1,), (6,), (3, 0, 5), (4, 2, 7))


def per_device(
    grid_nodes, mesh_nodes, owned_nodes, grid_rim, mesh_rim, long_send, g2m_edges, short_edges,
    long_edges, m2g_edges, edge_first, edge_second, edge_bias, edge_gain, node_first, node_second,
    node_bias, node_gain,
):
    weights = dict(
        edge_bias=edge_bias, edge_gain=edge_gain, node_bias=node_bias, node_gain=node_gain,
        edge_first=stay(edge_first), edge_second=stay(edge_second),
        node_first=stay(node_first), node_second=stay(node_second),
    )
    width = grid_nodes.shape[1]
    slots = mesh_nodes.shape[0]
    depth = mesh_rim.shape[2]
    peers, listed = long_send.shape[1:]

    remote, joined = grid_halo(grid_nodes, grid_rim)
    long_lists = long_send.reshape(1, peers * listed)
    rim_sends = send_shapes(depth, width)
    prepared = encode_local(grid_nodes, mesh_nodes, g2m_edges, joined, weights, 0)
    mesh_one, proj, *sends = encode(prepared, remote, mesh_rim, depth, grid_nodes.shape[0])

    remote, places = halo(*sends)
    prepared = prepare(mesh_one, weights, 1)
    mesh_two, proj, sent = round_part(
        short_edges, proj, prepared, mesh_one, remote, places, long_lists, owned_nodes,
        [jax.ShapeDtypeStruct((peers * listed, width), BF16)], weights, 1,
    )

    sent = sent.reshape(peers, listed, width)
    arrived = lax.all_to_all(sent, AXES, split_axis=0, concat_axis=0, tiled=True)
    prepared = prepare(mesh_two, weights, 2)
    mesh_three, proj, mesh_out, *sends = round_part(
        long_edges, proj, prepared, mesh_two, [arrived.reshape(1, peers * listed, width)], ((0,),),
        mesh_rim, owned_nodes, rim_sends, weights, 2,
    )

    remote, places = halo(*sends)
    prepared = decode_local(grid_nodes, proj, m2g_edges, weights, 3)
    grid_out = decode_part(prepared, grid_nodes, m2g_edges, remote, places, weights, 3, slots)
    return grid_out, mesh_out


def solution(mesh):
    rows = P(AXES, None)
    lists = P(AXES, None, None)
    in_specs = (rows, rows, P(AXES)) + (lists,) * 7 + (P(),) * 8
    return jax.shard_map(
        per_device, mesh=mesh, in_specs=in_specs, out_specs=(rows, rows), check_vma=False
    )
```

```python
import functools

import jax
import jax.numpy as jnp
from jax import lax
from jax.experimental import pallas as pl
from jax.experimental.pallas import tpu as pltpu
from jax.sharding import PartitionSpec as P

EPSILON = 1e-05
AXES = ("aa", "ba")
LANES = 128
BF16 = jnp.bfloat16
F32 = jnp.float32
LIMIT = pltpu.CompilerParams(vmem_limit_bytes=28 * 1024 * 1024)

UP_LISTS = (7, 5, 6)
DOWN_LISTS = (2, 0, 1)
RIGHT_LIST = 4
LEFT_LIST = 3
SEND_ORDER = UP_LISTS + DOWN_LISTS + (RIGHT_LIST, LEFT_LIST)


def dot(left, right):
    return jnp.dot(left, right, preferred_element_type=F32)


def math_block(total, most):
    block = most
    while total % block:
        block -= LANES
    return block


def round_up(value, unit):
    return -(-value // unit) * unit


def column(row):
    tall = jnp.broadcast_to(row, (LANES, row.shape[1]))
    return jnp.transpose(tall).astype(jnp.int16)


def one_hot(ids, width, base=0):
    lane = lax.broadcasted_iota(jnp.int16, ids.shape, 1)
    parts = [
        jnp.where(ids == lane + jnp.int16(base + start), BF16(1), BF16(0))
        for start in range(0, width, LANES)
    ]
    return parts[0] if len(parts) == 1 else jnp.concatenate(parts, 1)


def silu(value):
    half = (0.5 * value).astype(BF16)
    return half + half * jnp.tanh(half)


def centre(ref, index):
    weight = ref[index].astype(F32)
    ref[index] = (weight - jnp.mean(weight, axis=-1, keepdims=True)).astype(BF16)


def normed(value):
    spread = jnp.mean(value * value, axis=-1, keepdims=True)
    return value * lax.rsqrt(spread + EPSILON)


def whole(shape):
    return pl.BlockSpec(shape, lambda *_: (0,) * len(shape))


def cost(macs, moved):
    return pl.CostEstimate(flops=2 * macs, bytes_accessed=moved, transcendentals=0)


HBM = pl.BlockSpec(memory_space=pltpu.HBM)
SMEM = pl.BlockSpec(memory_space=pltpu.SMEM)


def stay(stack):
    return pltpu.with_memory_space_constraint(stack, pltpu.HBM)


def near(value):
    return pltpu.with_memory_space_constraint(value, pltpu.VMEM)


def held(value, section):
    return pltpu.with_memory_space_constraint(value, place_of(section))


def place_of(section):
    return pltpu.HBM if section == 2 else pltpu.VMEM


def fetch(sources, buffers, arrived):
    copies = [
        pltpu.make_async_copy(source, buffers.at[i], arrived.at[i]) for i, source in enumerate(sources)
    ]
    for copy in copies:
        copy.start()
    return copies


def fetch_scratch(count, width):
    return [pltpu.VMEM((count, width, width), BF16), pltpu.SemaphoreType.DMA((count,))]


def matrices(count, width):
    return pltpu.VMEM((count, width, width), BF16)


def fill(ref, value):
    rows = value.shape[0]
    ref[:rows] = value
    if ref.shape[0] > rows:
        ref[rows:] = jnp.zeros((ref.shape[0] - rows, ref.shape[1]), ref.dtype)


def clear_tail(ref, rows):
    ref[rows:] = jnp.zeros((ref.shape[0] - rows, ref.shape[1]), ref.dtype)


def row_of(ref, index):
    return ref[index : index + 1]


def added(pre, targets, second, slots):
    hidden = silu(pre)
    message = normed(dot(hidden, second)).astype(BF16)
    member = lax.broadcasted_iota(jnp.int32, (slots, targets.shape[1]), 0) == targets
    return dot(member.astype(BF16), message)


def updated(rows, total, inner, first, second, gain):
    inner = inner + dot(total.astype(BF16), first)
    update = normed(dot(silu(inner), second)) * gain
    return (rows.astype(F32) + update).astype(BF16)


def side_base():
    return jnp.where(lax.axis_index("aa") % 2 == 0, 5, 0)


def send_shapes(depth, width):
    return [jax.ShapeDtypeStruct((n, depth, width), BF16) for n in (3, 3, 1, 1)]


def list_rows(proj_out, lists_ref, sends):
    if len(lists_ref.shape) == 3:
        ids = jnp.concatenate([column(lists_ref[0, m : m + 1]) for m in SEND_ORDER], 0)
    else:
        ids = column(lists_ref[...])
    listed = ids.shape[0]
    size = math_block(listed, 256)
    made = []
    for start in range(0, listed, size):
        picked = one_hot(ids[start : start + size], proj_out.shape[0])
        made.append(dot(picked, proj_out[...]).astype(BF16))
    made = made[0] if len(made) == 1 else jnp.concatenate(made, 0)
    place = 0
    for ref in sends:
        if len(ref.shape) == 2:
            ref[...] = made
            continue
        depth = ref.shape[1]
        for index in range(ref.shape[0]):
            ref[index] = made[place : place + depth]
            place += depth


def pick_pair_kernel(rows_hbm, rim_hbm, pair_out, rows, rim, rows_here, rim_here):
    depth = rim.shape[2]
    parts = rows_here.shape[0]
    size = rows.shape[0] // parts
    copies = [pltpu.make_async_copy(rim_hbm, rim, rim_here.at[0])]
    for part in range(parts):
        span = pl.ds(part * size, size)
        copies.append(pltpu.make_async_copy(rows_hbm.at[span], rows.at[span], rows_here.at[part]))
    for copy in copies:
        copy.start()
    pair = side_base()
    copies[0].wait()
    ids = [column(rim[0, pl.ds(pair + offset, 1), :]) for offset in (2, 0, 1)]
    picked = [None] * len(ids)
    for part in range(parts):
        copies[part + 1].wait()
        values = rows[part * size : (part + 1) * size]
        for index, listed in enumerate(ids):
            found = dot(one_hot(listed, size, part * size), values)
            picked[index] = found if part == 0 else picked[index] + found
    for index, found in enumerate(picked):
        pair_out[index * depth : (index + 1) * depth] = found.astype(BF16)


def pick_pair(rows, rim):
    count, width = rows.shape
    parts = count // 256 if count % 256 == 0 else 1
    return pl.pallas_call(
        pick_pair_kernel,
        in_specs=[HBM, HBM],
        out_shape=[
            pltpu.VMEM((3 * rim.shape[2], width), BF16),
            pltpu.VMEM((count, width), BF16),
            pltpu.VMEM(rim.shape, jnp.int32),
        ],
        scratch_shapes=[pltpu.SemaphoreType.DMA((parts,)), pltpu.SemaphoreType.DMA((1,))],
        compiler_params=LIMIT,
        name="pick_pair",
    )(stay(rows), stay(rim))


def pick_rest_kernel(section, rows_ref, rim_ref, edge_first, node_first, mesh_hbm, edges_hbm, *refs):
    vectors, refs = refs[:4], refs[4:]
    outs, (stack, mesh, edges, rows_of, arrived, mesh_here, edges_here, vectors_here) = refs[:5], refs[5:]
    copies = fetch(
        [edge_first.at[section, 1], edge_first.at[section, 0], node_first.at[section, 0]], stack, arrived
    )
    copies.append(pltpu.make_async_copy(mesh_hbm, mesh, mesh_here.at[0]))
    copies.append(pltpu.make_async_copy(edges_hbm, edges, edges_here.at[0]))
    for index, vector in enumerate(vectors):
        copies.append(
            pltpu.make_async_copy(
                vector.at[pl.ds(section, 1)], rows_of.at[pl.ds(index, 1)], vectors_here.at[index]
            )
        )
    for copy in copies[3:]:
        copy.start()
    outer = 5 - side_base()
    for out, chosen in zip(outs, (RIGHT_LIST, LEFT_LIST, outer + 2, outer, outer + 1)):
        ids = column(rim_ref[0, pl.ds(chosen, 1), :])
        out[...] = dot(one_hot(ids, rows_ref.shape[0]), rows_ref[...]).astype(BF16)
    for copy in copies:
        copy.wait()


def pick_rest(rows, rim, mesh_rows, edges, weights, section):
    width = rows.shape[1]
    vmem = pl.BlockSpec(memory_space=pltpu.VMEM)
    return pl.pallas_call(
        functools.partial(pick_rest_kernel, section),
        in_specs=[vmem] * 2 + [HBM] * 8,
        out_shape=[pltpu.VMEM((rim.shape[2], width), BF16)] * 5
        + [
            matrices(3, width),
            pltpu.VMEM(mesh_rows.shape, BF16),
            pltpu.VMEM(edges.shape, edges.dtype),
            pltpu.VMEM((4, width), F32),
        ],
        scratch_shapes=[pltpu.SemaphoreType.DMA((n,)) for n in (3, 1, 1, 4)],
        compiler_params=LIMIT,
        name="pick_rest",
    )(
        near(rows), near(rim), weights["edge_first"], weights["node_first"], stay(mesh_rows), stay(edges),
        stay(weights["edge_bias"]), stay(weights["node_bias"]), stay(weights["edge_gain"]),
        stay(weights["node_gain"]),
    )


def pair_join_kernel(pair_ref, right_ref, left_ref, right_out, left_out):
    depth = right_ref.shape[0]
    for index, (own, out) in enumerate(((right_ref, right_out), (left_ref, left_out))):
        out[:depth] = own[...]
        out[depth:] = pair_ref[index * depth : (index + 1) * depth]


def pair_join(pair, right, left):
    depth, width = right.shape
    return pl.pallas_call(
        pair_join_kernel,
        out_shape=[pltpu.VMEM((2 * depth, width), BF16)] * 2,
        compiler_params=LIMIT,
        name="pair_join",
    )(pair, right, left)


def grid_halo(rows, rim, mesh_rows, edges, weights, section):
    pair, rows, rim = pick_pair(rows, rim)
    pair = move(pair, lambda i, j: (i ^ 1, j))
    right, left, *rest = pick_rest(rows, rim, mesh_rows, edges, weights, section)
    outer, kept = rest[:3], rest[3:]
    right, left = pair_join(pair, right, left)
    other = lambda i: i + 1 if i % 2 else i - 1
    remote = [
        pair,
        move(right, lambda i, j: (i, j + 1)),
        move(left, lambda i, j: (i, j - 1)),
        move(outer[0], lambda i, j: (other(i), j + 1)),
        move(outer[1], lambda i, j: (other(i), j - 1)),
        move(outer[2], lambda i, j: (other(i), j)),
    ]
    return remote, right, rows, kept


def encode_local_kernel(
    section, grid_ref, stack, mesh_ref, edges_ref, vectors, after_ref,
    edge_first, edge_second, node_first, node_second, pre_out, inner_out, later, table, target, arrived,
):
    copies = fetch(
        [
            edge_first.at[section, 0], edge_second.at[section], node_first.at[section, 1],
            node_second.at[section], edge_first.at[section + 1, 0],
        ],
        later, arrived,
    )
    rows = mesh_ref[...]
    fill(target, (dot(rows, stack[0]) + row_of(vectors, 0)).astype(BF16))
    fill(table, dot(grid_ref[...], stack[1]).astype(BF16))
    inner_out[...] = dot(rows, stack[2]) + row_of(vectors, 1)
    edges = edges_ref.shape[2]
    block = math_block(edges, 1024)
    for start in range(0, edges, block):
        part = slice(start, start + block)
        senders = column(edges_ref[0, 0:1, part])
        targets = column(edges_ref[0, 1:2, part])
        pre_out[part] = dot(one_hot(senders, table.shape[0]), table[...]) + dot(
            one_hot(targets, target.shape[0]), target[...]
        )
    for copy in copies:
        copy.wait()
    centre(later, 1)
    centre(later, 3)


def encode_local(grid_rows, kept, after, weights, section):
    stack, mesh_rows, edges, vectors = [near(value) for value in kept]
    total = edges.shape[2]
    count, width = grid_rows.shape
    slots = mesh_rows.shape[0]
    vmem = pl.BlockSpec(memory_space=pltpu.VMEM)
    return pl.pallas_call(
        functools.partial(encode_local_kernel, section),
        in_specs=[vmem] * 5 + [pl.BlockSpec(memory_space=pl.ANY)] + [HBM] * 4,
        out_shape=[
            pltpu.VMEM((total, width), F32),
            pltpu.VMEM((slots, width), F32),
            matrices(5, width),
        ],
        scratch_shapes=[
            pltpu.VMEM((round_up(count, LANES), width), BF16),
            pltpu.VMEM((round_up(slots, LANES), width), BF16),
            pltpu.SemaphoreType.DMA((5,)),
        ],
        compiler_params=LIMIT,
        name="encode_local",
    )(
        near(grid_rows), stack, mesh_rows, edges, vectors, after,
        weights["edge_first"], weights["edge_second"], weights["node_first"], weights["node_second"],
    )


def halo_part(pre, edges_ref, part, table, base):
    senders = edges_ref[0, 0:1, part] - base
    return pre + dot(one_hot(column(senders), table.shape[0]), table[...])


def encode_sides_kernel(count, pre_ref, edges_ref, stack, pair_ref, right_ref, left_ref, pre_out, table):
    depth = right_ref.shape[0] // 2
    pair = side_base()
    first = jnp.where(pair == 0, 0, 3)
    for ref, start, direction in (
        (pair_ref, 2 * depth, pair + 1),
        (right_ref, 0, 3),
        (right_ref, depth, pair),
        (left_ref, 0, 4),
        (left_ref, depth, pair + 2),
    ):
        place = pl.multiple_of((direction - first) * depth, LANES)
        table[pl.ds(place, depth)] = dot(ref[start : start + depth], stack[0]).astype(BF16)
    edges = pre_ref.shape[0]
    block = math_block(edges, 1024)
    for start in range(0, edges, block):
        part = slice(start, start + block)
        pre_out[part] = halo_part(pre_ref[part], edges_ref, part, table, count + first * depth)


def encode_sides(pre, edges, stack, remote, count):
    depth, width = remote[1].shape[0] // 2, pre.shape[1]
    return pl.pallas_call(
        functools.partial(encode_sides_kernel, count),
        out_shape=pltpu.VMEM(pre.shape, F32),
        scratch_shapes=[pltpu.VMEM((5 * depth, width), BF16)],
        input_output_aliases={0: 0},
        compiler_params=LIMIT,
        name="encode_sides",
    )(near(pre), near(edges), near(stack), *remote)


def encode_kernel(count, *refs):
    pre_ref, edges_ref, stack, inner_ref, mesh_ref, outer_right, outer_left, outer_ref = refs[:8]
    vectors, lists_ref = refs[8:10]
    mesh_out, proj_out, up, down, right, left, table = refs[10:]
    slots = mesh_ref.shape[0]
    depth = outer_ref.shape[0]
    for index, ref in enumerate((outer_right, outer_ref, outer_left)):
        table[index * depth : (index + 1) * depth] = dot(ref[...], stack[0]).astype(BF16)
    base = count + (5 - side_base()) * depth
    edges = pre_ref.shape[0]
    block = math_block(edges, 1024)
    summed = None
    for start in range(0, edges, block):
        part = slice(start, start + block)
        pre = halo_part(pre_ref[part], edges_ref, part, table, base)
        made = added(pre, edges_ref[0, 1:2, part], stack[1], slots)
        summed = made if summed is None else summed + made
    summed = summed * row_of(vectors, 2)
    fresh = updated(mesh_ref[...], summed, inner_ref[...], stack[2], stack[3], row_of(vectors, 3))
    mesh_out[...] = fresh
    fill(proj_out, dot(fresh, stack[4]).astype(BF16))
    list_rows(proj_out, lists_ref, (up, down, right, left))


def encode(prepared, kept, remote, lists, depth, count):
    pre, inner, stack = [near(value) for value in prepared]
    mesh_rows, edges, vectors = [near(value) for value in kept[1:]]
    slots, width = mesh_rows.shape
    pre = near(encode_sides(pre, edges, stack, remote[:3], count))
    return pl.pallas_call(
        functools.partial(encode_kernel, count),
        out_shape=[
            pltpu.VMEM((slots, width), BF16),
            pltpu.VMEM((round_up(slots, LANES), width), BF16),
        ]
        + send_shapes(depth, width),
        scratch_shapes=[pltpu.VMEM((3 * remote[-1].shape[0], width), BF16)],
        compiler_params=LIMIT,
        name="encode",
    )(pre, edges, stack, inner, mesh_rows, *remote[3:], vectors, lists)


def prepare_kernel(
    section, mesh_ref, bias_ref, node_bias_ref, edge_first, edge_second, node_first, node_second,
    target_out, inner_out, later, own, arrived, later_arrived,
):
    copies = fetch([edge_first.at[section, 1], node_first.at[section, 0]], own, arrived)
    copies += fetch(
        [
            edge_second.at[section], node_first.at[section, 1], node_second.at[section],
            edge_first.at[section + 1, 0],
        ],
        later, later_arrived,
    )
    rows = mesh_ref[...]
    copies[0].wait()
    fill(target_out, (dot(rows, own[0]) + row_of(bias_ref, section)).astype(BF16))
    copies[1].wait()
    inner_out[...] = dot(rows, own[1]) + row_of(node_bias_ref, section)
    for copy in copies[2:]:
        copy.wait()
    centre(later, 0)
    centre(later, 2)


def prepare(mesh_rows, weights, section):
    slots, width = mesh_rows.shape
    vmem = pl.BlockSpec(memory_space=pltpu.VMEM)
    return pl.pallas_call(
        functools.partial(prepare_kernel, section),
        in_specs=[vmem] * 3 + [HBM] * 4,
        out_shape=[
            place_of(section)((round_up(slots, LANES), width), BF16),
            place_of(section)((slots, width), F32),
            matrices(4, width),
        ],
        scratch_shapes=fetch_scratch(2, width) + [pltpu.SemaphoreType.DMA((4,))],
        compiler_params=LIMIT,
        name="prepare",
    )(
        held(mesh_rows, section), weights["edge_bias"], weights["node_bias"],
        weights["edge_first"], weights["edge_second"], weights["node_first"], weights["node_second"],
    )


def place_remote(table, remote, places, base):
    for ref, slots in zip(remote, places):
        depth = ref.shape[1]
        for index, slot in enumerate(slots):
            place = base + slot * depth
            table[place : place + depth] = ref[index]


def round_kernel(section, places, last, *refs):
    edges_ref, local_ref, target, inner_ref, stack, mesh_ref = refs[:6]
    remote = refs[6 : 6 + len(places)]
    gain_ref, node_gain_ref, lists_ref, owned_ref = refs[6 + len(places) : 10 + len(places)]
    rest = refs[10 + len(places) :]
    slots, padded = mesh_ref.shape[0], local_ref.shape[0]
    if last:
        table, target_here, inner_here, mesh_here, here = rest[-5:]
        rest = rest[:-5]
        copies = [
            pltpu.make_async_copy(local_ref, table.at[pl.ds(0, padded)], here.at[0]),
            pltpu.make_async_copy(target, target_here, here.at[1]),
            pltpu.make_async_copy(inner_ref, inner_here, here.at[2]),
            pltpu.make_async_copy(mesh_ref, mesh_here, here.at[3]),
        ]
        for copy in copies:
            copy.start()
        target, inner_ref, mesh_ref = target_here, inner_here, mesh_here
    else:
        table = rest[-1]
        rest = rest[:-1]
        table[:padded] = local_ref[...]
    mesh_out, proj_out = rest[:2]
    sends = rest[2:]
    if last:
        masked_out, sends = sends[0], sends[1:]
    place_remote(table, remote, places, padded)
    if last:
        for copy in copies:
            copy.wait()
    edges = edges_ref.shape[2]
    block = math_block(edges, 1536)
    summed = None
    for start in range(0, edges, block):
        senders = edges_ref[0, 0:1, start : start + block]
        senders = jnp.where(senders < slots, senders, senders + (padded - slots))
        targets = edges_ref[0, 1:2, start : start + block]
        pre = dot(one_hot(column(senders), table.shape[0]), table[...]) + dot(
            one_hot(column(targets), padded), target[...]
        )
        part = added(pre, targets, stack[0], slots)
        summed = part if summed is None else summed + part
    summed = summed * row_of(gain_ref, section)
    fresh = updated(mesh_ref[...], summed, inner_ref[...], stack[1], stack[2], row_of(node_gain_ref, section))
    mesh_out[...] = fresh
    if last:
        alive = lax.broadcasted_iota(jnp.int32, fresh.shape, 0) < owned_ref[0]
        masked_out[...] = jnp.where(alive, fresh, jnp.zeros_like(fresh))
    fill(proj_out, dot(fresh, stack[3]).astype(BF16))
    list_rows(proj_out, lists_ref, sends)


def round_part(edges, local, prepared, mesh_rows, remote, places, lists, owned, sends, weights, section):
    slots, width = mesh_rows.shape
    last = section == 2
    padded = local.shape[0]
    table_rows = padded + sum(r.shape[0] * r.shape[1] for r in remote)
    space = place_of(section + 1)
    out_shape = [space((slots, width), BF16), space((padded, width), BF16)]
    if last:
        out_shape.append(jax.ShapeDtypeStruct((slots, width), BF16))
    scratch = [pltpu.VMEM((table_rows, width), BF16)]
    if last:
        scratch += [pltpu.VMEM(value.shape, value.dtype) for value in (*prepared[:2], mesh_rows)]
        scratch.append(pltpu.SemaphoreType.DMA((4,)))
    vmem = pl.BlockSpec(memory_space=pltpu.VMEM)
    return pl.pallas_call(
        functools.partial(round_kernel, section, places, last),
        in_specs=[vmem] + [HBM if last else vmem] * 3 + [vmem] + [HBM if last else vmem]
        + [vmem] * (3 + len(remote))
        + [SMEM],
        out_shape=out_shape + sends,
        scratch_shapes=scratch,
        compiler_params=LIMIT,
        name="round_part",
    )(
        edges, held(local, section), *[held(value, section) for value in prepared[:2]], near(prepared[2]),
        held(mesh_rows, section), *remote,
        weights["edge_gain"], weights["node_gain"], lists, owned,
    )


def decode_local_kernel(
    section, grid_ref, table_ref, edges_ref, bias_ref, edge_first, edge_second, node_first, node_second,
    pre_ref, later, own, arrived, later_arrived,
):
    copies = fetch([edge_first.at[section, 1]], own, arrived)
    copies += fetch(
        [
            edge_second.at[section], node_first.at[section, 0], node_first.at[section, 1],
            node_second.at[section],
        ],
        later, later_arrived,
    )
    copies[0].wait()
    count = grid_ref.shape[0]
    block = math_block(count, 512)
    for start in range(0, count, block):
        target = dot(grid_ref[start : start + block], own[0]) + row_of(bias_ref, section)
        for sender in range(edges_ref.shape[1]):
            ids = column(edges_ref[0, sender : sender + 1, start : start + block])
            pre = dot(one_hot(ids, table_ref.shape[0]), table_ref[...]) + target
            pre_ref[sender, start : start + block] = pre.astype(BF16)
    for copy in copies[1:]:
        copy.wait()
    centre(later, 0)
    centre(later, 3)


def decode_local(grid_rows, table, edges, weights, section):
    count, width = grid_rows.shape
    senders = edges.shape[1]
    vmem = pl.BlockSpec(memory_space=pltpu.VMEM)
    return pl.pallas_call(
        functools.partial(decode_local_kernel, section),
        in_specs=[vmem] * 4 + [HBM] * 4,
        out_shape=[pltpu.VMEM((senders, count, width), BF16), matrices(4, width)],
        scratch_shapes=fetch_scratch(1, width) + [pltpu.SemaphoreType.DMA((4,))],
        compiler_params=LIMIT,
        name="decode_local",
    )(
        grid_rows, near(table), edges, weights["edge_bias"],
        weights["edge_first"], weights["edge_second"], weights["node_first"], weights["node_second"],
    )


def decode_kernel(section, places, split, *refs):
    pre_ref, stack, grid_ref, edges_ref = refs[:4]
    remote = refs[4 : 4 + len(places)]
    gain_ref, node_bias_ref, node_gain_ref, out_ref, table, ready, sent = refs[4 + len(places) :]
    place_remote(table, remote, places, 0)
    count = grid_ref.shape[0]
    block = math_block(count, 512)
    copies = []
    for index, start in enumerate(range(0, count, block)):
        part = slice(start, start + block)
        summed = None
        for sender in range(edges_ref.shape[1]):
            ids = column(edges_ref[0, sender : sender + 1, part])
            pre = pre_ref[sender, part].astype(F32) + dot(one_hot(ids, table.shape[0], split), table[...])
            message = normed(dot(silu(pre), stack[0])).astype(BF16).astype(F32)
            summed = message if summed is None else summed + message
        rows = grid_ref[part]
        summed = (summed * row_of(gain_ref, section)).astype(BF16)
        inner = dot(rows, stack[1]) + dot(summed, stack[2]) + row_of(node_bias_ref, section)
        update = normed(dot(silu(inner), stack[3])) * row_of(node_gain_ref, section)
        ready[part] = (rows.astype(F32) + update).astype(BF16)
        copies.append(pltpu.make_async_copy(ready.at[part], out_ref.at[part], sent.at[index]))
        copies[-1].start()
    for copy in copies:
        copy.wait()


def decode_part(prepared, grid_rows, edges, remote, places, weights, section, split):
    count, width = grid_rows.shape
    table_rows = sum(r.shape[0] * r.shape[1] for r in remote)
    vmem = pl.BlockSpec(memory_space=pltpu.VMEM)
    return pl.pallas_call(
        functools.partial(decode_kernel, section, places, split),
        in_specs=[vmem] * (7 + len(remote)),
        out_specs=pl.BlockSpec(memory_space=pl.ANY),
        out_shape=jax.ShapeDtypeStruct((count, width), BF16),
        scratch_shapes=[
            pltpu.VMEM((table_rows, width), BF16),
            pltpu.VMEM((count, width), BF16),
            pltpu.SemaphoreType.DMA((count // math_block(count, 512),)),
        ],
        compiler_params=LIMIT,
        name="decode_part",
    )(
        *[near(value) for value in prepared], grid_rows, edges, *remote,
        weights["edge_gain"], weights["node_bias"], weights["node_gain"],
    )


def move(value, target):
    bands, sectors = lax.axis_size("aa"), lax.axis_size("ba")
    pairs = []
    for i in range(bands):
        for j in range(sectors):
            band, sector = target(i, j)
            pairs.append((i * sectors + j, band % bands * sectors + sector % sectors))
    return lax.ppermute(value, AXES, pairs)


def join_kernel(up_ref, down_ref, right_ref, left_ref, right_out, left_out):
    for index, (own, out) in enumerate(((right_ref, right_out), (left_ref, left_out))):
        out[0] = own[0]
        out[1] = up_ref[index]
        out[2] = down_ref[index]


def halo(up, down, right, left):
    from_up = move(up, lambda i, j: (i + 1, j))
    from_down = move(down, lambda i, j: (i - 1, j))
    joined = jax.ShapeDtypeStruct((3,) + right.shape[1:], BF16)
    right, left = pl.pallas_call(
        join_kernel, out_shape=[joined, joined], compiler_params=LIMIT, name="join"
    )(from_up, from_down, right, left)
    from_left = move(right, lambda i, j: (i, j + 1))
    from_right = move(left, lambda i, j: (i, j - 1))
    return [from_up[2:3], from_down[2:3], from_left, from_right], ((1,), (6,), (3, 0, 5), (4, 2, 7))


def per_device(
    grid_nodes, mesh_nodes, owned_nodes, grid_rim, mesh_rim, long_send, g2m_edges, short_edges,
    long_edges, m2g_edges, edge_first, edge_second, edge_bias, edge_gain, node_first, node_second,
    node_bias, node_gain,
):
    weights = dict(
        edge_bias=edge_bias, edge_gain=edge_gain, node_bias=node_bias, node_gain=node_gain,
        edge_first=stay(edge_first), edge_second=stay(edge_second),
        node_first=stay(node_first), node_second=stay(node_second),
    )
    width = grid_nodes.shape[1]
    slots = mesh_nodes.shape[0]
    depth = mesh_rim.shape[2]
    peers, listed = long_send.shape[1:]

    long_lists = long_send.reshape(1, peers * listed)
    rim_sends = send_shapes(depth, width)
    remote, joined, tile, kept = grid_halo(grid_nodes, grid_rim, mesh_nodes, g2m_edges, weights, 0)
    prepared = encode_local(tile, kept, joined, weights, 0)
    mesh_one, proj, *sends = encode(prepared, kept, remote, mesh_rim, depth, grid_nodes.shape[0])

    remote, places = halo(*sends)
    prepared = prepare(mesh_one, weights, 1)
    mesh_two, proj, sent = round_part(
        short_edges, proj, prepared, mesh_one, remote, places, long_lists, owned_nodes,
        [jax.ShapeDtypeStruct((peers * listed, width), BF16)], weights, 1,
    )

    sent = sent.reshape(peers, listed, width)
    arrived = lax.all_to_all(sent, AXES, split_axis=0, concat_axis=0, tiled=True)
    prepared = prepare(mesh_two, weights, 2)
    mesh_three, proj, mesh_out, *sends = round_part(
        long_edges, proj, prepared, mesh_two, [arrived.reshape(1, peers * listed, width)], ((0,),),
        mesh_rim, owned_nodes, rim_sends, weights, 2,
    )

    remote, places = halo(*sends)
    prepared = decode_local(grid_nodes, proj, m2g_edges, weights, 3)
    grid_out = decode_part(prepared, grid_nodes, m2g_edges, remote, places, weights, 3, slots)
    return grid_out, mesh_out


def solution(mesh):
    rows = P(AXES, None)
    lists = P(AXES, None, None)
    in_specs = (rows, rows, P(AXES)) + (lists,) * 7 + (P(),) * 8
    return jax.shard_map(
        per_device, mesh=mesh, in_specs=in_specs, out_specs=(rows, rows), check_vma=False
    )
```

```python
import functools

import jax
import jax.numpy as jnp
from jax import lax
from jax.experimental import pallas as pl
from jax.experimental.pallas import tpu as pltpu
from jax.sharding import PartitionSpec as P

EPSILON = 1e-05
AXES = ("aa", "ba")
LANES = 128
BF16 = jnp.bfloat16
F32 = jnp.float32
LIMIT = pltpu.CompilerParams(vmem_limit_bytes=20 * 1024 * 1024)

UP_LISTS = (7, 5, 6)
DOWN_LISTS = (2, 0, 1)
RIGHT_LIST = 4
LEFT_LIST = 3
SEND_ORDER = UP_LISTS + DOWN_LISTS + (RIGHT_LIST, LEFT_LIST)


def dot(left, right):
    return jnp.dot(left, right, preferred_element_type=F32)


def math_block(total, most):
    block = most
    while total % block:
        block -= LANES
    return block


def round_up(value, unit):
    return -(-value // unit) * unit


def column(row):
    tall = jnp.broadcast_to(row, (LANES, row.shape[1]))
    return jnp.transpose(tall).astype(jnp.int16)


def one_hot(ids, width, base=0):
    lane = lax.broadcasted_iota(jnp.int16, ids.shape, 1)
    parts = [
        jnp.where(ids == lane + jnp.int16(base + start), BF16(1), BF16(0))
        for start in range(0, width, LANES)
    ]
    return parts[0] if len(parts) == 1 else jnp.concatenate(parts, 1)


def silu(value):
    half = (0.5 * value).astype(BF16)
    return half + half * jnp.tanh(half)


def centred(weight):
    weight = weight.astype(F32)
    return (weight - jnp.mean(weight, axis=-1, keepdims=True)).astype(BF16)


def normed(value):
    spread = jnp.mean(value * value, axis=-1, keepdims=True)
    return value * lax.rsqrt(spread + EPSILON)


def whole(shape):
    return pl.BlockSpec(shape, lambda *_: (0,) * len(shape))


def cost(macs, moved):
    return pl.CostEstimate(flops=2 * macs, bytes_accessed=moved, transcendentals=0)


HBM = pl.BlockSpec(memory_space=pltpu.HBM)
SMEM = pl.BlockSpec(memory_space=pltpu.SMEM)


def stay(stack):
    return pltpu.with_memory_space_constraint(stack, pltpu.HBM)


def near(value):
    return pltpu.with_memory_space_constraint(value, pltpu.VMEM)


def held(value, section):
    return pltpu.with_memory_space_constraint(value, place_of(section))


def place_of(section):
    return pltpu.HBM if section == 2 else pltpu.VMEM


def fetch(sources, buffers, arrived):
    copies = [
        pltpu.make_async_copy(source, buffers.at[i], arrived.at[i]) for i, source in enumerate(sources)
    ]
    for copy in copies:
        copy.start()
    return copies


def fetch_scratch(count, width):
    return [pltpu.VMEM((count, width, width), BF16), pltpu.SemaphoreType.DMA((count,))]


def matrices(count, width):
    return pltpu.VMEM((count, width, width), BF16)


def fill(ref, value):
    rows = value.shape[0]
    ref[:rows] = value
    if ref.shape[0] > rows:
        ref[rows:] = jnp.zeros((ref.shape[0] - rows, ref.shape[1]), ref.dtype)


def clear_tail(ref, rows):
    ref[rows:] = jnp.zeros((ref.shape[0] - rows, ref.shape[1]), ref.dtype)


def row_of(ref, index):
    return ref[index : index + 1]


def added(pre, targets, second, slots):
    hidden = silu(pre)
    message = normed(dot(hidden, second)).astype(BF16)
    member = lax.broadcasted_iota(jnp.int32, (slots, targets.shape[1]), 0) == targets
    return dot(member.astype(BF16), message)


def updated(rows, total, inner, first, second, gain):
    inner = inner + dot(total.astype(BF16), first)
    update = normed(dot(silu(inner), second)) * gain
    return (rows.astype(F32) + update).astype(BF16)


def side_base():
    return jnp.where(lax.axis_index("aa") % 2 == 0, 5, 0)


def send_shapes(depth, width):
    return [jax.ShapeDtypeStruct((n, depth, width), BF16) for n in (3, 3, 1, 1)]


def list_rows(proj_out, lists_ref, sends):
    if len(lists_ref.shape) == 3:
        ids = jnp.concatenate([column(lists_ref[0, m : m + 1]) for m in SEND_ORDER], 0)
    else:
        ids = column(lists_ref[...])
    listed = ids.shape[0]
    size = math_block(listed, 256)
    made = []
    for start in range(0, listed, size):
        picked = one_hot(ids[start : start + size], proj_out.shape[0])
        made.append(dot(picked, proj_out[...]).astype(BF16))
    made = made[0] if len(made) == 1 else jnp.concatenate(made, 0)
    place = 0
    for ref in sends:
        if len(ref.shape) == 2:
            ref[...] = made
            continue
        depth = ref.shape[1]
        for index in range(ref.shape[0]):
            ref[index] = made[place : place + depth]
            place += depth


def pick_pair_kernel(rows_hbm, rim_hbm, pair_out, rows, rim, rows_here, rim_here):
    depth = rim.shape[2]
    parts = rows_here.shape[0]
    size = rows.shape[0] // parts
    copies = [pltpu.make_async_copy(rim_hbm, rim, rim_here.at[0])]
    for part in range(parts):
        span = pl.ds(part * size, size)
        copies.append(pltpu.make_async_copy(rows_hbm.at[span], rows.at[span], rows_here.at[part]))
    for copy in copies:
        copy.start()
    pair = side_base()
    copies[0].wait()
    ids = [column(rim[0, pl.ds(pair + offset, 1), :]) for offset in (2, 0, 1)]
    picked = [None] * len(ids)
    for part in range(parts):
        copies[part + 1].wait()
        values = rows[part * size : (part + 1) * size]
        for index, listed in enumerate(ids):
            found = dot(one_hot(listed, size, part * size), values)
            picked[index] = found if part == 0 else picked[index] + found
    for index, found in enumerate(picked):
        pair_out[index * depth : (index + 1) * depth] = found.astype(BF16)


def pick_pair(rows, rim):
    count, width = rows.shape
    parts = count // 256 if count % 256 == 0 else 1
    return pl.pallas_call(
        pick_pair_kernel,
        in_specs=[HBM, HBM],
        out_shape=[
            pltpu.VMEM((3 * rim.shape[2], width), BF16),
            pltpu.VMEM((count, width), BF16),
            pltpu.VMEM(rim.shape, jnp.int32),
        ],
        scratch_shapes=[pltpu.SemaphoreType.DMA((parts,)), pltpu.SemaphoreType.DMA((1,))],
        compiler_params=LIMIT,
        name="pick_pair",
    )(stay(rows), stay(rim))


def pick_outer_kernel(rows_ref, rim_ref, after_ref, *outs):
    outer = 5 - side_base()
    for out, offset in zip(outs, (2, 0, 1)):
        ids = column(rim_ref[0, pl.ds(outer + offset, 1), :])
        out[...] = dot(one_hot(ids, rows_ref.shape[0]), rows_ref[...]).astype(BF16)


def pick_outer(rows, rim, after):
    vmem = pl.BlockSpec(memory_space=pltpu.VMEM)
    return pl.pallas_call(
        pick_outer_kernel,
        in_specs=[vmem, vmem, pl.BlockSpec(memory_space=pl.ANY)],
        out_shape=[pltpu.VMEM((rim.shape[2], rows.shape[1]), BF16)] * 3,
        compiler_params=LIMIT,
        name="pick_outer",
    )(near(rows), near(rim), after)


def pick_rest_kernel(section, rows_ref, rim_ref, edge_first, node_first, mesh_hbm, edges_hbm, *refs):
    vectors, refs = refs[:4], refs[4:]
    outs, (stack, mesh, edges, rows_of, arrived, mesh_here, edges_here, vectors_here) = refs[:2], refs[2:]
    copies = fetch(
        [edge_first.at[section, 1], edge_first.at[section, 0], node_first.at[section, 0]], stack, arrived
    )
    copies.append(pltpu.make_async_copy(mesh_hbm, mesh, mesh_here.at[0]))
    copies.append(pltpu.make_async_copy(edges_hbm, edges, edges_here.at[0]))
    for index, vector in enumerate(vectors):
        copies.append(
            pltpu.make_async_copy(
                vector.at[pl.ds(section, 1)], rows_of.at[pl.ds(index, 1)], vectors_here.at[index]
            )
        )
    for copy in copies[3:]:
        copy.start()
    for out, chosen in zip(outs, (RIGHT_LIST, LEFT_LIST)):
        ids = column(rim_ref[0, pl.ds(chosen, 1), :])
        out[...] = dot(one_hot(ids, rows_ref.shape[0]), rows_ref[...]).astype(BF16)
    for copy in copies:
        copy.wait()


def pick_rest(rows, rim, mesh_rows, edges, weights, section):
    width = rows.shape[1]
    vmem = pl.BlockSpec(memory_space=pltpu.VMEM)
    return pl.pallas_call(
        functools.partial(pick_rest_kernel, section),
        in_specs=[vmem] * 2 + [HBM] * 8,
        out_shape=[pltpu.VMEM((rim.shape[2], width), BF16)] * 2
        + [
            matrices(3, width),
            pltpu.VMEM(mesh_rows.shape, BF16),
            pltpu.VMEM(edges.shape, edges.dtype),
            pltpu.VMEM((4, width), F32),
        ],
        scratch_shapes=[pltpu.SemaphoreType.DMA((n,)) for n in (3, 1, 1, 4)],
        compiler_params=LIMIT,
        name="pick_rest",
    )(
        near(rows), near(rim), weights["edge_first"], weights["node_first"], stay(mesh_rows), stay(edges),
        stay(weights["edge_bias"]), stay(weights["node_bias"]), stay(weights["edge_gain"]),
        stay(weights["node_gain"]),
    )


def pair_join_kernel(pair_ref, right_ref, left_ref, right_out, left_out):
    depth = right_ref.shape[0]
    for index, (own, out) in enumerate(((right_ref, right_out), (left_ref, left_out))):
        out[:depth] = own[...]
        out[depth:] = pair_ref[index * depth : (index + 1) * depth]


def pair_join(pair, right, left):
    depth, width = right.shape
    return pl.pallas_call(
        pair_join_kernel,
        out_shape=[pltpu.VMEM((2 * depth, width), BF16)] * 2,
        compiler_params=LIMIT,
        name="pair_join",
    )(pair, right, left)


def grid_halo(rows, rim, mesh_rows, edges, weights, section):
    pair, rows, rim = pick_pair(rows, rim)
    pair = move(pair, lambda i, j: (i ^ 1, j))
    right, left, *kept = pick_rest(rows, rim, mesh_rows, edges, weights, section)
    right, left = pair_join(pair, right, left)
    outer = pick_outer(rows, rim, right)
    bands = lax.axis_size("aa")
    other = lambda i: i + 1 if i % 2 else i - 1
    inside = lambda i: 0 <= other(i) < bands
    remote = [
        pair,
        move(right, lambda i, j: (i, j + 1)),
        move(left, lambda i, j: (i, j - 1)),
        move(outer[0], lambda i, j: (other(i), j + 1) if inside(i) else None),
        move(outer[1], lambda i, j: (other(i), j - 1) if inside(i) else None),
        move(outer[2], lambda i, j: (other(i), j)),
    ]
    return remote, right, rows, kept


def encode_local_kernel(
    section, grid_ref, stack, mesh_ref, edges_ref, vectors, after_ref,
    edge_first, edge_second, node_first, node_second, pre_out, inner_out, later, table, target, arrived,
):
    copies = fetch(
        [
            edge_first.at[section, 0], edge_second.at[section], node_first.at[section, 1],
            node_second.at[section], edge_first.at[section + 1, 0],
        ],
        later, arrived,
    )
    rows = mesh_ref[...]
    fill(target, (dot(rows, stack[0]) + row_of(vectors, 0)).astype(BF16))
    fill(table, dot(grid_ref[...], stack[1]).astype(BF16))
    inner_out[...] = dot(rows, stack[2]) + row_of(vectors, 1)
    edges = edges_ref.shape[2]
    block = math_block(edges, 1024)
    for start in range(0, edges, block):
        part = slice(start, start + block)
        senders = column(edges_ref[0, 0:1, part])
        targets = column(edges_ref[0, 1:2, part])
        pre_out[part] = dot(one_hot(senders, table.shape[0]), table[...]) + dot(
            one_hot(targets, target.shape[0]), target[...]
        )
    for copy in copies:
        copy.wait()
    later[1] = centred(later[1])
    later[3] = centred(later[3])


def encode_local(grid_rows, kept, after, weights, section):
    stack, mesh_rows, edges, vectors = [near(value) for value in kept]
    total = edges.shape[2]
    count, width = grid_rows.shape
    slots = mesh_rows.shape[0]
    vmem = pl.BlockSpec(memory_space=pltpu.VMEM)
    return pl.pallas_call(
        functools.partial(encode_local_kernel, section),
        in_specs=[vmem] * 5 + [pl.BlockSpec(memory_space=pl.ANY)] + [HBM] * 4,
        out_shape=[
            pltpu.VMEM((total, width), F32),
            pltpu.VMEM((slots, width), F32),
            matrices(5, width),
        ],
        scratch_shapes=[
            pltpu.VMEM((round_up(count, LANES), width), BF16),
            pltpu.VMEM((round_up(slots, LANES), width), BF16),
            pltpu.SemaphoreType.DMA((5,)),
        ],
        compiler_params=LIMIT,
        name="encode_local",
    )(
        near(grid_rows), stack, mesh_rows, edges, vectors, after,
        weights["edge_first"], weights["edge_second"], weights["node_first"], weights["node_second"],
    )


def encode_kernel(count, *refs):
    pre_ref, edges_ref, stack, inner_ref, mesh_ref = refs[:5]
    pair_ref, right_ref, left_ref, outer_right, outer_left, outer_ref = refs[5:11]
    vectors, lists_ref = refs[11:13]
    mesh_out, proj_out, up, down, right, left, table = refs[13:]
    slots = mesh_ref.shape[0]
    depth = outer_ref.shape[0]
    pair = side_base()
    outer = 5 - pair
    for ref, start, direction in (
        (pair_ref, 2 * depth, pair + 1),
        (right_ref, 0, 3),
        (right_ref, depth, pair),
        (left_ref, 0, 4),
        (left_ref, depth, pair + 2),
        (outer_right, 0, outer),
        (outer_left, 0, outer + 2),
        (outer_ref, 0, outer + 1),
    ):
        place = pl.multiple_of(direction * depth, LANES)
        table[pl.ds(place, depth)] = dot(ref[start : start + depth], stack[0]).astype(BF16)
    edges = pre_ref.shape[0]
    block = math_block(edges, 1024)
    summed = None
    for start in range(0, edges, block):
        part = slice(start, start + block)
        senders = column(edges_ref[0, 0:1, part] - count)
        pre = pre_ref[part] + dot(one_hot(senders, table.shape[0]), table[...])
        made = added(pre, edges_ref[0, 1:2, part], stack[1], slots)
        summed = made if summed is None else summed + made
    summed = summed * row_of(vectors, 2)
    fresh = updated(mesh_ref[...], summed, inner_ref[...], stack[2], stack[3], row_of(vectors, 3))
    mesh_out[...] = fresh
    fill(proj_out, dot(fresh, stack[4]).astype(BF16))
    list_rows(proj_out, lists_ref, (up, down, right, left))


def encode(prepared, kept, remote, lists, depth, count):
    pre, inner, stack = [near(value) for value in prepared]
    mesh_rows, edges, vectors = [near(value) for value in kept[1:]]
    slots, width = mesh_rows.shape
    return pl.pallas_call(
        functools.partial(encode_kernel, count),
        out_shape=[
            pltpu.VMEM((slots, width), BF16),
            pltpu.VMEM((round_up(slots, LANES), width), BF16),
        ]
        + send_shapes(depth, width),
        scratch_shapes=[pltpu.VMEM((8 * remote[-1].shape[0], width), BF16)],
        compiler_params=LIMIT,
        name="encode",
    )(pre, edges, stack, inner, mesh_rows, *remote, vectors, lists)


def prepare_kernel(
    section, mesh_ref, bias_ref, node_bias_ref, edge_first, edge_second, node_first, node_second,
    target_out, inner_out, later, own, arrived, later_arrived,
):
    copies = fetch([edge_first.at[section, 1], node_first.at[section, 0]], own, arrived)
    copies += fetch(
        [
            edge_second.at[section], node_second.at[section], node_first.at[section, 1],
            edge_first.at[section + 1, 0],
        ],
        later, later_arrived,
    )
    rows = mesh_ref[...]
    copies[0].wait()
    fill(target_out, (dot(rows, own[0]) + row_of(bias_ref, section)).astype(BF16))
    copies[1].wait()
    inner_out[...] = dot(rows, own[1]) + row_of(node_bias_ref, section)
    for copy in copies[2:]:
        copy.wait()
    later[0] = centred(later[0])
    later[1] = centred(later[1])


def prepare(mesh_rows, weights, section):
    slots, width = mesh_rows.shape
    vmem = pl.BlockSpec(memory_space=pltpu.VMEM)
    return pl.pallas_call(
        functools.partial(prepare_kernel, section),
        in_specs=[vmem] * 3 + [HBM] * 4,
        out_shape=[
            place_of(section)((round_up(slots, LANES), width), BF16),
            place_of(section)((slots, width), F32),
            matrices(4, width),
        ],
        scratch_shapes=fetch_scratch(2, width) + [pltpu.SemaphoreType.DMA((4,))],
        compiler_params=LIMIT,
        name="prepare",
    )(
        held(mesh_rows, section), weights["edge_bias"], weights["node_bias"],
        weights["edge_first"], weights["edge_second"], weights["node_first"], weights["node_second"],
    )


def receivers_kernel(section, mesh_ref, bias_ref, node_bias_ref, edge_first, node_first, target_out, inner_out, own, arrived):
    copies = fetch([edge_first.at[section, 1], node_first.at[section, 0]], own, arrived)
    rows = mesh_ref[...]
    copies[0].wait()
    fill(target_out, (dot(rows, own[0]) + row_of(bias_ref, section)).astype(BF16))
    copies[1].wait()
    inner_out[...] = dot(rows, own[1]) + row_of(node_bias_ref, section)


def receivers(mesh_rows, weights, section):
    slots, width = mesh_rows.shape
    vmem = pl.BlockSpec(memory_space=pltpu.VMEM)
    return pl.pallas_call(
        functools.partial(receivers_kernel, section),
        in_specs=[vmem] * 3 + [HBM] * 2,
        out_shape=[pltpu.VMEM((round_up(slots, LANES), width), BF16), pltpu.VMEM((slots, width), F32)],
        scratch_shapes=fetch_scratch(2, width),
        compiler_params=LIMIT,
        name="receivers",
    )(near(mesh_rows), weights["edge_bias"], weights["node_bias"], weights["edge_first"], weights["node_first"])


def layers_kernel(section, after_ref, edge_first, edge_second, node_first, node_second, later, arrived):
    copies = fetch(
        [
            edge_second.at[section], node_second.at[section], node_first.at[section, 1],
            edge_first.at[section + 1, 0],
        ],
        later, arrived,
    )
    for index in (0, 1):
        copies[index].wait()
        later[index] = centred(later[index])
    for copy in copies[2:]:
        copy.wait()


def layers(after, weights, section):
    width = after.shape[-1]
    return pl.pallas_call(
        functools.partial(layers_kernel, section),
        in_specs=[pl.BlockSpec(memory_space=pl.ANY)] + [HBM] * 4,
        out_shape=matrices(4, width),
        scratch_shapes=[pltpu.SemaphoreType.DMA((4,))],
        compiler_params=LIMIT,
        name="layers",
    )(after, weights["edge_first"], weights["edge_second"], weights["node_first"], weights["node_second"])


def place_remote(table, remote, places, base):
    for ref, slots in zip(remote, places):
        depth = ref.shape[1]
        for index, slot in enumerate(slots):
            place = base + slot * depth
            table[place : place + depth] = ref[index]


def round_kernel(section, places, last, *refs):
    edges_ref, local_ref, target, inner_ref, stack, mesh_ref = refs[:6]
    remote = refs[6 : 6 + len(places)]
    gain_ref, node_gain_ref, lists_ref, owned_ref = refs[6 + len(places) : 10 + len(places)]
    rest = refs[10 + len(places) :]
    slots, padded = mesh_ref.shape[0], local_ref.shape[0]
    if last:
        table, target_here, inner_here, mesh_here, here = rest[-5:]
        rest = rest[:-5]
        copies = [
            pltpu.make_async_copy(local_ref, table.at[pl.ds(0, padded)], here.at[0]),
            pltpu.make_async_copy(target, target_here, here.at[1]),
            pltpu.make_async_copy(inner_ref, inner_here, here.at[2]),
            pltpu.make_async_copy(mesh_ref, mesh_here, here.at[3]),
        ]
        for copy in copies:
            copy.start()
        target, inner_ref, mesh_ref = target_here, inner_here, mesh_here
    else:
        table = rest[-1]
        rest = rest[:-1]
        table[:padded] = local_ref[...]
    mesh_out, proj_out = rest[:2]
    sends = rest[2:]
    place_remote(table, remote, places, padded)
    if last:
        for copy in copies:
            copy.wait()
    edges = edges_ref.shape[2]
    block = math_block(edges, 1536)
    summed = None
    for start in range(0, edges, block):
        senders = edges_ref[0, 0:1, start : start + block]
        senders = jnp.where(senders < slots, senders, senders + (padded - slots))
        targets = edges_ref[0, 1:2, start : start + block]
        pre = dot(one_hot(column(senders), table.shape[0]), table[...]) + dot(
            one_hot(column(targets), padded), target[...]
        )
        part = added(pre, targets, stack[0], slots)
        summed = part if summed is None else summed + part
    summed = summed * row_of(gain_ref, section)
    fresh = updated(mesh_ref[...], summed, inner_ref[...], stack[2], stack[1], row_of(node_gain_ref, section))
    if last:
        alive = lax.broadcasted_iota(jnp.int32, fresh.shape, 0) < owned_ref[0]
        mesh_out[...] = jnp.where(alive, fresh, jnp.zeros_like(fresh))
    else:
        mesh_out[...] = fresh
    fill(proj_out, dot(fresh, stack[3]).astype(BF16))
    list_rows(proj_out, lists_ref, sends)


def round_part(edges, local, prepared, mesh_rows, remote, places, lists, owned, sends, weights, section):
    slots, width = mesh_rows.shape
    last = section == 2
    padded = local.shape[0]
    table_rows = padded + sum(r.shape[0] * r.shape[1] for r in remote)
    space = place_of(section + 1)
    out_shape = [
        jax.ShapeDtypeStruct((slots, width), BF16) if last else space((slots, width), BF16),
        space((padded, width), BF16),
    ]
    scratch = [pltpu.VMEM((table_rows, width), BF16)]
    if last:
        scratch += [pltpu.VMEM(value.shape, value.dtype) for value in (*prepared[:2], mesh_rows)]
        scratch.append(pltpu.SemaphoreType.DMA((4,)))
    vmem = pl.BlockSpec(memory_space=pltpu.VMEM)
    return pl.pallas_call(
        functools.partial(round_kernel, section, places, last),
        in_specs=[vmem] + [HBM if last else vmem] * 3 + [vmem] + [HBM if last else vmem]
        + [vmem] * (3 + len(remote))
        + [SMEM],
        out_shape=out_shape + sends,
        scratch_shapes=scratch,
        compiler_params=LIMIT,
        name="round_part",
    )(
        edges, held(local, section), *[held(value, section) for value in prepared[:2]], near(prepared[2]),
        held(mesh_rows, section), *remote,
        weights["edge_gain"], weights["node_gain"], lists, owned,
    )


def grid_receivers_kernel(section, grid_ref, bias_ref, edge_first, edge_second, target_out, later, own, arrived, later_arrived):
    copies = fetch([edge_first.at[section, 1]], own, arrived)
    copies += fetch([edge_second.at[section]], later, later_arrived)
    copies[0].wait()
    target_out[...] = (dot(grid_ref[...], own[0]) + row_of(bias_ref, section)).astype(BF16)
    copies[1].wait()
    later[0] = centred(later[0])


def grid_receivers(grid_rows, weights, section):
    vmem = pl.BlockSpec(memory_space=pltpu.VMEM)
    width = grid_rows.shape[1]
    return pl.pallas_call(
        functools.partial(grid_receivers_kernel, section),
        in_specs=[vmem] * 2 + [HBM] * 2,
        out_shape=[pltpu.VMEM(grid_rows.shape, BF16), matrices(1, width)],
        scratch_shapes=fetch_scratch(1, width) + [pltpu.SemaphoreType.DMA((1,))],
        compiler_params=LIMIT,
        name="grid_receivers",
    )(grid_rows, weights["edge_bias"], weights["edge_first"], weights["edge_second"])


def decode_local_kernel(
    section, target_ref, table_ref, edges_ref, after_ref, node_first, node_second, pre_ref, later, arrived
):
    copies = fetch(
        [node_second.at[section], node_first.at[section, 0], node_first.at[section, 1]], later, arrived
    )
    count = target_ref.shape[0]
    block = math_block(count, 512)
    for start in range(0, count, block):
        target = target_ref[start : start + block].astype(F32)
        for sender in range(edges_ref.shape[1]):
            ids = column(edges_ref[0, sender : sender + 1, start : start + block])
            pre = dot(one_hot(ids, table_ref.shape[0]), table_ref[...]) + target
            pre_ref[sender, start : start + block] = pre.astype(BF16)
    copies[0].wait()
    later[0] = centred(later[0])
    for copy in copies[1:]:
        copy.wait()


def decode_local(target, table, edges, after, weights, section):
    count, width = target.shape
    senders = edges.shape[1]
    vmem = pl.BlockSpec(memory_space=pltpu.VMEM)
    return pl.pallas_call(
        functools.partial(decode_local_kernel, section),
        in_specs=[vmem] * 3 + [pl.BlockSpec(memory_space=pl.ANY), HBM, HBM],
        out_shape=[pltpu.VMEM((senders, count, width), BF16), matrices(3, width)],
        scratch_shapes=[pltpu.SemaphoreType.DMA((3,))],
        compiler_params=LIMIT,
        name="decode_local",
    )(near(target), near(table), edges, after, weights["node_first"], weights["node_second"])


def decode_kernel(section, places, split, *refs):
    pre_ref, second, layers, grid_ref, edges_ref = refs[:5]
    remote = refs[5 : 5 + len(places)]
    gain_ref, node_bias_ref, node_gain_ref, out_ref, table, ready, sent = refs[5 + len(places) :]
    place_remote(table, remote, places, 0)
    count = grid_ref.shape[0]
    block = math_block(count, 512)
    copies = []
    for index, start in enumerate(range(0, count, block)):
        part = slice(start, start + block)
        summed = None
        for sender in range(edges_ref.shape[1]):
            ids = column(edges_ref[0, sender : sender + 1, part])
            pre = pre_ref[sender, part].astype(F32) + dot(one_hot(ids, table.shape[0], split), table[...])
            message = normed(dot(silu(pre), second[0])).astype(BF16).astype(F32)
            summed = message if summed is None else summed + message
        rows = grid_ref[part]
        summed = (summed * row_of(gain_ref, section)).astype(BF16)
        inner = dot(rows, layers[1]) + dot(summed, layers[2]) + row_of(node_bias_ref, section)
        update = normed(dot(silu(inner), layers[0])) * row_of(node_gain_ref, section)
        ready[part] = (rows.astype(F32) + update).astype(BF16)
        copies.append(pltpu.make_async_copy(ready.at[part], out_ref.at[part], sent.at[index]))
        copies[-1].start()
    for copy in copies:
        copy.wait()


def decode_part(prepared, grid_rows, edges, remote, places, weights, section, split):
    count, width = grid_rows.shape
    table_rows = sum(r.shape[0] * r.shape[1] for r in remote)
    vmem = pl.BlockSpec(memory_space=pltpu.VMEM)
    return pl.pallas_call(
        functools.partial(decode_kernel, section, places, split),
        in_specs=[vmem] * (8 + len(remote)),
        out_specs=pl.BlockSpec(memory_space=pl.ANY),
        out_shape=jax.ShapeDtypeStruct((count, width), BF16),
        scratch_shapes=[
            pltpu.VMEM((table_rows, width), BF16),
            pltpu.VMEM((count, width), BF16),
            pltpu.SemaphoreType.DMA((count // math_block(count, 512),)),
        ],
        compiler_params=LIMIT,
        name="decode_part",
    )(
        *[near(value) for value in prepared], grid_rows, edges, *remote,
        weights["edge_gain"], weights["node_bias"], weights["node_gain"],
    )


def move(value, target):
    bands, sectors = lax.axis_size("aa"), lax.axis_size("ba")
    pairs = []
    for i in range(bands):
        for j in range(sectors):
            place = target(i, j)
            if place is None:
                continue
            band, sector = place
            pairs.append((i * sectors + j, band % bands * sectors + sector % sectors))
    return lax.ppermute(value, AXES, pairs)


def join_kernel(up_ref, down_ref, right_ref, left_ref, after_ref, right_out, left_out):
    for index, (own, out) in enumerate(((right_ref, right_out), (left_ref, left_out))):
        out[0] = own[0]
        out[1] = up_ref[index]
        out[2] = down_ref[index]


def halo(up, down, right, left, after):
    from_up = move(up, lambda i, j: (i + 1, j))
    from_down = move(down, lambda i, j: (i - 1, j))
    joined = jax.ShapeDtypeStruct((3,) + right.shape[1:], BF16)
    right, left = pl.pallas_call(
        join_kernel,
        in_specs=[pl.BlockSpec(memory_space=pltpu.VMEM)] * 4 + [pl.BlockSpec(memory_space=pl.ANY)],
        out_shape=[joined, joined],
        compiler_params=LIMIT,
        name="join",
    )(from_up, from_down, right, left, after)
    from_left = move(right, lambda i, j: (i, j + 1))
    from_right = move(left, lambda i, j: (i, j - 1))
    blocks = [from_up[2:3], from_down[2:3], from_left, from_right]
    return blocks, ((1,), (6,), (3, 0, 5), (4, 2, 7)), right


def per_device(
    grid_nodes, mesh_nodes, owned_nodes, grid_rim, mesh_rim, long_send, g2m_edges, short_edges,
    long_edges, m2g_edges, edge_first, edge_second, edge_bias, edge_gain, node_first, node_second,
    node_bias, node_gain,
):
    weights = dict(
        edge_bias=edge_bias, edge_gain=edge_gain, node_bias=node_bias, node_gain=node_gain,
        edge_first=stay(edge_first), edge_second=stay(edge_second),
        node_first=stay(node_first), node_second=stay(node_second),
    )
    width = grid_nodes.shape[1]
    slots = mesh_nodes.shape[0]
    depth = mesh_rim.shape[2]
    peers, listed = long_send.shape[1:]

    long_lists = long_send.reshape(1, peers * listed)
    rim_sends = send_shapes(depth, width)
    remote, joined, tile, kept = grid_halo(grid_nodes, grid_rim, mesh_nodes, g2m_edges, weights, 0)
    prepared = encode_local(tile, kept, joined, weights, 0)
    mesh_one, proj, *sends = encode(prepared, kept, remote, mesh_rim, depth, grid_nodes.shape[0])

    target, inner = receivers(mesh_one, weights, 1)
    remote, places, joined = halo(*sends, target)
    prepared = target, inner, layers(joined, weights, 1)
    mesh_two, proj, sent = round_part(
        short_edges, proj, prepared, mesh_one, remote, places, long_lists, owned_nodes,
        [jax.ShapeDtypeStruct((peers * listed, width), BF16)], weights, 1,
    )

    sent = sent.reshape(peers, listed, width)
    arrived = lax.all_to_all(sent, AXES, split_axis=0, concat_axis=0, tiled=True)
    prepared = prepare(mesh_two, weights, 2)
    mesh_out, proj, *sends = round_part(
        long_edges, proj, prepared, mesh_two, [arrived.reshape(1, peers * listed, width)], ((0,),),
        mesh_rim, owned_nodes, rim_sends, weights, 2,
    )

    target, second = grid_receivers(grid_nodes, weights, 3)
    remote, places, joined = halo(*sends, target)
    pre, stack = decode_local(target, proj, m2g_edges, joined, weights, 3)
    grid_out = decode_part(
        (pre, second, stack), grid_nodes, m2g_edges, remote, places, weights, 3, slots
    )
    return grid_out, mesh_out


def solution(mesh):
    rows = P(AXES, None)
    lists = P(AXES, None, None)
    in_specs = (rows, rows, P(AXES)) + (lists,) * 7 + (P(),) * 8
    return jax.shard_map(
        per_device, mesh=mesh, in_specs=in_specs, out_specs=(rows, rows), check_vma=False
    )
```

```python
import functools

import jax
import jax.numpy as jnp
from jax import lax
from jax.experimental import pallas as pl
from jax.experimental.pallas import tpu as pltpu
from jax.sharding import PartitionSpec as P

EPSILON = 1e-05
AXES = ("aa", "ba")
LANES = 128
BF16 = jnp.bfloat16
F32 = jnp.float32
LIMIT = pltpu.CompilerParams(vmem_limit_bytes=20 * 1024 * 1024)

UP_LISTS = (7, 5, 6)
DOWN_LISTS = (2, 0, 1)
RIGHT_LIST = 4
LEFT_LIST = 3
SEND_ORDER = UP_LISTS + DOWN_LISTS + (RIGHT_LIST, LEFT_LIST)


def dot(left, right):
    return jnp.dot(left, right, preferred_element_type=F32)


def math_block(total, most):
    block = most
    while total % block:
        block -= LANES
    return block


def round_up(value, unit):
    return -(-value // unit) * unit


def column(row):
    tall = jnp.broadcast_to(row, (LANES, row.shape[1]))
    return jnp.transpose(tall).astype(jnp.int16)


def one_hot(ids, width, base=0):
    lane = lax.broadcasted_iota(jnp.int16, ids.shape, 1)
    parts = [
        jnp.where(ids == lane + jnp.int16(base + start), BF16(1), BF16(0))
        for start in range(0, width, LANES)
    ]
    return parts[0] if len(parts) == 1 else jnp.concatenate(parts, 1)


def silu(value):
    half = (0.5 * value).astype(BF16)
    return half + half * jnp.tanh(half)


def centred(weight):
    weight = weight.astype(F32)
    return (weight - jnp.mean(weight, axis=-1, keepdims=True)).astype(BF16)


def normed(value):
    spread = jnp.mean(value * value, axis=-1, keepdims=True)
    return value * lax.rsqrt(spread + EPSILON)


def whole(shape):
    return pl.BlockSpec(shape, lambda *_: (0,) * len(shape))


def cost(macs, moved):
    return pl.CostEstimate(flops=2 * macs, bytes_accessed=moved, transcendentals=0)


HBM = pl.BlockSpec(memory_space=pltpu.HBM)
SMEM = pl.BlockSpec(memory_space=pltpu.SMEM)


def stay(stack):
    return pltpu.with_memory_space_constraint(stack, pltpu.HBM)


def near(value):
    return pltpu.with_memory_space_constraint(value, pltpu.VMEM)


def held(value, section):
    return pltpu.with_memory_space_constraint(value, place_of(section))


def place_of(section):
    return pltpu.HBM if section == 2 else pltpu.VMEM


def fetch(sources, buffers, arrived):
    copies = [
        pltpu.make_async_copy(source, buffers.at[i], arrived.at[i]) for i, source in enumerate(sources)
    ]
    for copy in copies:
        copy.start()
    return copies


def fetch_scratch(count, width):
    return [pltpu.VMEM((count, width, width), BF16), pltpu.SemaphoreType.DMA((count,))]


def matrices(count, width):
    return pltpu.VMEM((count, width, width), BF16)


def fill(ref, value):
    rows = value.shape[0]
    ref[:rows] = value
    if ref.shape[0] > rows:
        ref[rows:] = jnp.zeros((ref.shape[0] - rows, ref.shape[1]), ref.dtype)


def clear_tail(ref, rows):
    ref[rows:] = jnp.zeros((ref.shape[0] - rows, ref.shape[1]), ref.dtype)


def row_of(ref, index):
    return ref[index : index + 1]


def added(pre, targets, second, slots):
    hidden = silu(pre)
    message = normed(dot(hidden, second)).astype(BF16)
    member = lax.broadcasted_iota(jnp.int32, (slots, targets.shape[1]), 0) == targets
    return dot(member.astype(BF16), message)


def updated(rows, total, inner, first, second, gain):
    inner = inner + dot(total.astype(BF16), first)
    update = normed(dot(silu(inner), second)) * gain
    return (rows.astype(F32) + update).astype(BF16)


def side_base():
    return jnp.where(lax.axis_index("aa") % 2 == 0, 5, 0)


def send_shapes(depth, width):
    return [jax.ShapeDtypeStruct((n, depth, width), BF16) for n in (3, 3, 1, 1)]


def list_rows(proj_out, lists_ref, sends):
    if len(lists_ref.shape) == 3:
        ids = jnp.concatenate([column(lists_ref[0, m : m + 1]) for m in SEND_ORDER], 0)
    else:
        ids = column(lists_ref[...])
    listed = ids.shape[0]
    size = math_block(listed, 256)
    made = []
    for start in range(0, listed, size):
        picked = one_hot(ids[start : start + size], proj_out.shape[0])
        made.append(dot(picked, proj_out[...]).astype(BF16))
    made = made[0] if len(made) == 1 else jnp.concatenate(made, 0)
    place = 0
    for ref in sends:
        if len(ref.shape) == 2:
            ref[...] = made
            continue
        depth = ref.shape[1]
        for index in range(ref.shape[0]):
            ref[index] = made[place : place + depth]
            place += depth


def pick_pair_kernel(rows_hbm, rim_hbm, pair_out, rows, rim, rows_here, rim_here):
    depth = rim.shape[2]
    parts = rows_here.shape[0]
    size = rows.shape[0] // parts
    copies = [pltpu.make_async_copy(rim_hbm, rim, rim_here.at[0])]
    for part in range(parts):
        span = pl.ds(part * size, size)
        copies.append(pltpu.make_async_copy(rows_hbm.at[span], rows.at[span], rows_here.at[part]))
    for copy in copies:
        copy.start()
    pair = side_base()
    copies[0].wait()
    ids = [column(rim[0, pl.ds(pair + offset, 1), :]) for offset in (2, 0, 1)]
    picked = [None] * len(ids)
    for part in range(parts):
        copies[part + 1].wait()
        values = rows[part * size : (part + 1) * size]
        for index, listed in enumerate(ids):
            found = dot(one_hot(listed, size, part * size), values)
            picked[index] = found if part == 0 else picked[index] + found
    for index, found in enumerate(picked):
        pair_out[index * depth : (index + 1) * depth] = found.astype(BF16)


def pick_pair(rows, rim):
    count, width = rows.shape
    parts = count // 256 if count % 256 == 0 else 1
    return pl.pallas_call(
        pick_pair_kernel,
        in_specs=[HBM, HBM],
        out_shape=[
            pltpu.VMEM((3 * rim.shape[2], width), BF16),
            pltpu.VMEM((count, width), BF16),
            pltpu.VMEM(rim.shape, jnp.int32),
        ],
        scratch_shapes=[pltpu.SemaphoreType.DMA((parts,)), pltpu.SemaphoreType.DMA((1,))],
        compiler_params=LIMIT,
        name="pick_pair",
    )(stay(rows), stay(rim))


def pick_outer_kernel(rows_ref, rim_ref, after_ref, *outs):
    outer = 5 - side_base()
    for out, offset in zip(outs, (2, 0, 1)):
        ids = column(rim_ref[0, pl.ds(outer + offset, 1), :])
        out[...] = dot(one_hot(ids, rows_ref.shape[0]), rows_ref[...]).astype(BF16)


def pick_outer(rows, rim, after):
    vmem = pl.BlockSpec(memory_space=pltpu.VMEM)
    return pl.pallas_call(
        pick_outer_kernel,
        in_specs=[vmem, vmem, pl.BlockSpec(memory_space=pl.ANY)],
        out_shape=[pltpu.VMEM((rim.shape[2], rows.shape[1]), BF16)] * 3,
        compiler_params=LIMIT,
        name="pick_outer",
    )(near(rows), near(rim), after)


def pick_rest_kernel(section, rows_ref, rim_ref, edge_first, node_first, mesh_hbm, edges_hbm, *refs):
    vectors, refs = refs[:4], refs[4:]
    outs, (stack, mesh, edges, rows_of, arrived, mesh_here, edges_here, vectors_here) = refs[:2], refs[2:]
    copies = fetch(
        [edge_first.at[section, 1], edge_first.at[section, 0], node_first.at[section, 0]], stack, arrived
    )
    copies.append(pltpu.make_async_copy(mesh_hbm, mesh, mesh_here.at[0]))
    copies.append(pltpu.make_async_copy(edges_hbm, edges, edges_here.at[0]))
    for index, vector in enumerate(vectors):
        copies.append(
            pltpu.make_async_copy(
                vector.at[pl.ds(section, 1)], rows_of.at[pl.ds(index, 1)], vectors_here.at[index]
            )
        )
    for copy in copies[3:]:
        copy.start()
    for out, chosen in zip(outs, (RIGHT_LIST, LEFT_LIST)):
        ids = column(rim_ref[0, pl.ds(chosen, 1), :])
        out[...] = dot(one_hot(ids, rows_ref.shape[0]), rows_ref[...]).astype(BF16)
    for copy in copies:
        copy.wait()


def pick_rest(rows, rim, mesh_rows, edges, weights, section):
    width = rows.shape[1]
    vmem = pl.BlockSpec(memory_space=pltpu.VMEM)
    return pl.pallas_call(
        functools.partial(pick_rest_kernel, section),
        in_specs=[vmem] * 2 + [HBM] * 8,
        out_shape=[pltpu.VMEM((rim.shape[2], width), BF16)] * 2
        + [
            matrices(3, width),
            pltpu.VMEM(mesh_rows.shape, BF16),
            pltpu.VMEM(edges.shape, edges.dtype),
            pltpu.VMEM((4, width), F32),
        ],
        scratch_shapes=[pltpu.SemaphoreType.DMA((n,)) for n in (3, 1, 1, 4)],
        compiler_params=LIMIT,
        name="pick_rest",
    )(
        near(rows), near(rim), weights["edge_first"], weights["node_first"], stay(mesh_rows), stay(edges),
        stay(weights["edge_bias"]), stay(weights["node_bias"]), stay(weights["edge_gain"]),
        stay(weights["node_gain"]),
    )


def pair_join_kernel(pair_ref, right_ref, left_ref, right_out, left_out):
    depth = right_ref.shape[0]
    for index, (own, out) in enumerate(((right_ref, right_out), (left_ref, left_out))):
        out[:depth] = own[...]
        out[depth:] = pair_ref[index * depth : (index + 1) * depth]


def pair_join(pair, right, left):
    depth, width = right.shape
    return pl.pallas_call(
        pair_join_kernel,
        out_shape=[pltpu.VMEM((2 * depth, width), BF16)] * 2,
        compiler_params=LIMIT,
        name="pair_join",
    )(pair, right, left)


def grid_halo(rows, rim, mesh_rows, edges, weights, section):
    pair, rows, rim = pick_pair(rows, rim)
    pair = move(pair, lambda i, j: (i ^ 1, j))
    right, left, *kept = pick_rest(rows, rim, mesh_rows, edges, weights, section)
    right, left = pair_join(pair, right, left)
    outer = pick_outer(rows, rim, right)
    bands = lax.axis_size("aa")
    other = lambda i: i + 1 if i % 2 else i - 1
    inside = lambda i: 0 <= other(i) < bands
    remote = [
        pair,
        move(right, lambda i, j: (i, j + 1)),
        move(left, lambda i, j: (i, j - 1)),
        move(outer[0], lambda i, j: (other(i), j + 1) if inside(i) else None),
        move(outer[1], lambda i, j: (other(i), j - 1) if inside(i) else None),
        move(outer[2], lambda i, j: (other(i), j)),
    ]
    return remote, right, rows, kept


def encode_local_kernel(
    section, grid_ref, stack, mesh_ref, edges_ref, vectors, after_ref,
    edge_first, edge_second, node_first, node_second, pre_out, inner_out, later, table, target, arrived,
):
    copies = fetch(
        [
            edge_first.at[section, 0], edge_second.at[section], node_first.at[section, 1],
            node_second.at[section], edge_first.at[section + 1, 0],
        ],
        later, arrived,
    )
    rows = mesh_ref[...]
    fill(target, (dot(rows, stack[0]) + row_of(vectors, 0)).astype(BF16))
    fill(table, dot(grid_ref[...], stack[1]).astype(BF16))
    inner_out[...] = dot(rows, stack[2]) + row_of(vectors, 1)
    edges = edges_ref.shape[2]
    block = math_block(edges, 1024)
    for start in range(0, edges, block):
        part = slice(start, start + block)
        senders = column(edges_ref[0, 0:1, part])
        targets = column(edges_ref[0, 1:2, part])
        pre_out[part] = dot(one_hot(senders, table.shape[0]), table[...]) + dot(
            one_hot(targets, target.shape[0]), target[...]
        )
    for copy in copies:
        copy.wait()
    later[1] = centred(later[1])
    later[3] = centred(later[3])


def encode_local(grid_rows, kept, after, weights, section):
    stack, mesh_rows, edges, vectors = [near(value) for value in kept]
    total = edges.shape[2]
    count, width = grid_rows.shape
    slots = mesh_rows.shape[0]
    vmem = pl.BlockSpec(memory_space=pltpu.VMEM)
    return pl.pallas_call(
        functools.partial(encode_local_kernel, section),
        in_specs=[vmem] * 5 + [pl.BlockSpec(memory_space=pl.ANY)] + [HBM] * 4,
        out_shape=[
            pltpu.VMEM((total, width), F32),
            pltpu.VMEM((slots, width), F32),
            matrices(5, width),
        ],
        scratch_shapes=[
            pltpu.VMEM((round_up(count, LANES), width), BF16),
            pltpu.VMEM((round_up(slots, LANES), width), BF16),
            pltpu.SemaphoreType.DMA((5,)),
        ],
        compiler_params=LIMIT,
        name="encode_local",
    )(
        near(grid_rows), stack, mesh_rows, edges, vectors, after,
        weights["edge_first"], weights["edge_second"], weights["node_first"], weights["node_second"],
    )


def encode_kernel(count, *refs):
    pre_ref, edges_ref, stack, inner_ref, mesh_ref = refs[:5]
    pair_ref, right_ref, left_ref, outer_right, outer_left, outer_ref = refs[5:11]
    vectors, lists_ref = refs[11:13]
    mesh_out, proj_out, up, down, right, left, table = refs[13:]
    slots = mesh_ref.shape[0]
    depth = outer_ref.shape[0]
    pair = side_base()
    outer = 5 - pair
    for ref, start, direction in (
        (pair_ref, 2 * depth, pair + 1),
        (right_ref, 0, 3),
        (right_ref, depth, pair),
        (left_ref, 0, 4),
        (left_ref, depth, pair + 2),
        (outer_right, 0, outer),
        (outer_left, 0, outer + 2),
        (outer_ref, 0, outer + 1),
    ):
        place = pl.multiple_of(direction * depth, LANES)
        table[pl.ds(place, depth)] = dot(ref[start : start + depth], stack[0]).astype(BF16)
    edges = pre_ref.shape[0]
    block = math_block(edges, 1024)
    summed = None
    for start in range(0, edges, block):
        part = slice(start, start + block)
        senders = column(edges_ref[0, 0:1, part] - count)
        pre = pre_ref[part] + dot(one_hot(senders, table.shape[0]), table[...])
        made = added(pre, edges_ref[0, 1:2, part], stack[1], slots)
        summed = made if summed is None else summed + made
    summed = summed * row_of(vectors, 2)
    fresh = updated(mesh_ref[...], summed, inner_ref[...], stack[2], stack[3], row_of(vectors, 3))
    mesh_out[...] = fresh
    fill(proj_out, dot(fresh, stack[4]).astype(BF16))
    list_rows(proj_out, lists_ref, (up, down, right, left))


def encode(prepared, kept, remote, lists, depth, count):
    pre, inner, stack = [near(value) for value in prepared]
    mesh_rows, edges, vectors = [near(value) for value in kept[1:]]
    slots, width = mesh_rows.shape
    return pl.pallas_call(
        functools.partial(encode_kernel, count),
        out_shape=[
            pltpu.VMEM((slots, width), BF16),
            pltpu.VMEM((round_up(slots, LANES), width), BF16),
        ]
        + send_shapes(depth, width),
        scratch_shapes=[pltpu.VMEM((8 * remote[-1].shape[0], width), BF16)],
        compiler_params=LIMIT,
        name="encode",
    )(pre, edges, stack, inner, mesh_rows, *remote, vectors, lists)


def prepare_kernel(
    section, mesh_ref, bias_ref, node_bias_ref, edge_first, edge_second, node_first, node_second,
    target_out, inner_out, later, own, arrived, later_arrived,
):
    copies = fetch([edge_first.at[section, 1], node_first.at[section, 0]], own, arrived)
    copies += fetch(
        [
            edge_second.at[section], node_second.at[section], node_first.at[section, 1],
            edge_first.at[section + 1, 0],
        ],
        later, later_arrived,
    )
    rows = mesh_ref[...]
    copies[0].wait()
    fill(target_out, (dot(rows, own[0]) + row_of(bias_ref, section)).astype(BF16))
    copies[1].wait()
    inner_out[...] = dot(rows, own[1]) + row_of(node_bias_ref, section)
    for copy in copies[2:]:
        copy.wait()
    later[0] = centred(later[0])
    later[1] = centred(later[1])


def prepare(mesh_rows, weights, section):
    slots, width = mesh_rows.shape
    vmem = pl.BlockSpec(memory_space=pltpu.VMEM)
    return pl.pallas_call(
        functools.partial(prepare_kernel, section),
        in_specs=[vmem] * 3 + [HBM] * 4,
        out_shape=[
            place_of(section)((round_up(slots, LANES), width), BF16),
            place_of(section)((slots, width), F32),
            matrices(4, width),
        ],
        scratch_shapes=fetch_scratch(2, width) + [pltpu.SemaphoreType.DMA((4,))],
        compiler_params=LIMIT,
        name="prepare",
    )(
        held(mesh_rows, section), weights["edge_bias"], weights["node_bias"],
        weights["edge_first"], weights["edge_second"], weights["node_first"], weights["node_second"],
    )


def receivers_kernel(section, mesh_ref, bias_ref, node_bias_ref, edge_first, node_first, target_out, inner_out, own, arrived):
    copies = fetch([edge_first.at[section, 1], node_first.at[section, 0]], own, arrived)
    rows = mesh_ref[...]
    copies[0].wait()
    fill(target_out, (dot(rows, own[0]) + row_of(bias_ref, section)).astype(BF16))
    copies[1].wait()
    inner_out[...] = dot(rows, own[1]) + row_of(node_bias_ref, section)


def receivers(mesh_rows, weights, section):
    slots, width = mesh_rows.shape
    vmem = pl.BlockSpec(memory_space=pltpu.VMEM)
    return pl.pallas_call(
        functools.partial(receivers_kernel, section),
        in_specs=[vmem] * 3 + [HBM] * 2,
        out_shape=[pltpu.VMEM((round_up(slots, LANES), width), BF16), pltpu.VMEM((slots, width), F32)],
        scratch_shapes=fetch_scratch(2, width),
        compiler_params=LIMIT,
        name="receivers",
    )(near(mesh_rows), weights["edge_bias"], weights["node_bias"], weights["edge_first"], weights["node_first"])


def layers_kernel(section, after_ref, edge_first, edge_second, node_first, node_second, later, arrived):
    copies = fetch(
        [
            edge_second.at[section], node_second.at[section], node_first.at[section, 1],
            edge_first.at[section + 1, 0],
        ],
        later, arrived,
    )
    for index in (0, 1):
        copies[index].wait()
        later[index] = centred(later[index])
    for copy in copies[2:]:
        copy.wait()


def layers(after, weights, section):
    width = after.shape[-1]
    return pl.pallas_call(
        functools.partial(layers_kernel, section),
        in_specs=[pl.BlockSpec(memory_space=pl.ANY)] + [HBM] * 4,
        out_shape=matrices(4, width),
        scratch_shapes=[pltpu.SemaphoreType.DMA((4,))],
        compiler_params=LIMIT,
        name="layers",
    )(after, weights["edge_first"], weights["edge_second"], weights["node_first"], weights["node_second"])


def place_remote(table, remote, places, base):
    for ref, slots in zip(remote, places):
        depth = ref.shape[1]
        for index, slot in enumerate(slots):
            place = base + slot * depth
            table[place : place + depth] = ref[index]


def round_kernel(section, places, last, *refs):
    edges_ref, local_ref, target, inner_ref, stack, mesh_ref = refs[:6]
    remote = refs[6 : 6 + len(places)]
    gain_ref, node_gain_ref, lists_ref, owned_ref = refs[6 + len(places) : 10 + len(places)]
    rest = refs[10 + len(places) :]
    slots, padded = mesh_ref.shape[0], local_ref.shape[0]
    if last:
        table, target_here, inner_here, mesh_here, here = rest[-5:]
        rest = rest[:-5]
        copies = [
            pltpu.make_async_copy(local_ref, table.at[pl.ds(0, padded)], here.at[0]),
            pltpu.make_async_copy(target, target_here, here.at[1]),
            pltpu.make_async_copy(inner_ref, inner_here, here.at[2]),
            pltpu.make_async_copy(mesh_ref, mesh_here, here.at[3]),
        ]
        for copy in copies:
            copy.start()
        target, inner_ref, mesh_ref = target_here, inner_here, mesh_here
    else:
        table = rest[-1]
        rest = rest[:-1]
        table[:padded] = local_ref[...]
    mesh_out, proj_out = rest[:2]
    sends = rest[2:]
    place_remote(table, remote, places, padded)
    waiting = copies if last else []
    edges = edges_ref.shape[2]
    block = math_block(edges, 1536)
    summed = None
    for start in range(0, edges, block):
        senders = edges_ref[0, 0:1, start : start + block]
        targets = edges_ref[0, 1:2, start : start + block]
        senders = column(senders)
        pre = dot(one_hot(senders, table.shape[0] - padded, slots), table[padded:])
        for copy in waiting[:2]:
            copy.wait()
        waiting = []
        own = jnp.where(senders < slots, senders, jnp.int16(-1))
        pre = pre + dot(one_hot(own, padded), table[:padded])
        pre = pre + dot(one_hot(column(targets), padded), target[...])
        part = added(pre, targets, stack[0], slots)
        summed = part if summed is None else summed + part
    summed = summed * row_of(gain_ref, section)
    for copy in copies[2:] if last else []:
        copy.wait()
    fresh = updated(mesh_ref[...], summed, inner_ref[...], stack[2], stack[1], row_of(node_gain_ref, section))
    if last:
        alive = lax.broadcasted_iota(jnp.int32, fresh.shape, 0) < owned_ref[0]
        mesh_out[...] = jnp.where(alive, fresh, jnp.zeros_like(fresh))
    else:
        mesh_out[...] = fresh
    fill(proj_out, dot(fresh, stack[3]).astype(BF16))
    list_rows(proj_out, lists_ref, sends)


def round_part(edges, local, prepared, mesh_rows, remote, places, lists, owned, sends, weights, section):
    slots, width = mesh_rows.shape
    last = section == 2
    padded = local.shape[0]
    table_rows = padded + sum(r.shape[0] * r.shape[1] for r in remote)
    space = place_of(section + 1)
    out_shape = [
        jax.ShapeDtypeStruct((slots, width), BF16) if last else space((slots, width), BF16),
        space((padded, width), BF16),
    ]
    scratch = [pltpu.VMEM((table_rows, width), BF16)]
    if last:
        scratch += [pltpu.VMEM(value.shape, value.dtype) for value in (*prepared[:2], mesh_rows)]
        scratch.append(pltpu.SemaphoreType.DMA((4,)))
    vmem = pl.BlockSpec(memory_space=pltpu.VMEM)
    return pl.pallas_call(
        functools.partial(round_kernel, section, places, last),
        in_specs=[vmem] + [HBM if last else vmem] * 3 + [vmem] + [HBM if last else vmem]
        + [vmem] * (3 + len(remote))
        + [SMEM],
        out_shape=out_shape + sends,
        scratch_shapes=scratch,
        compiler_params=LIMIT,
        name="round_part",
    )(
        edges, held(local, section), *[held(value, section) for value in prepared[:2]], near(prepared[2]),
        held(mesh_rows, section), *remote,
        weights["edge_gain"], weights["node_gain"], lists, owned,
    )


def grid_receivers_kernel(section, grid_ref, bias_ref, edge_first, edge_second, target_out, later, own, arrived, later_arrived):
    copies = fetch([edge_first.at[section, 1]], own, arrived)
    copies += fetch([edge_second.at[section]], later, later_arrived)
    copies[0].wait()
    target_out[...] = (dot(grid_ref[...], own[0]) + row_of(bias_ref, section)).astype(BF16)
    copies[1].wait()
    later[0] = centred(later[0])


def grid_receivers(grid_rows, weights, section):
    vmem = pl.BlockSpec(memory_space=pltpu.VMEM)
    width = grid_rows.shape[1]
    return pl.pallas_call(
        functools.partial(grid_receivers_kernel, section),
        in_specs=[vmem] * 2 + [HBM] * 2,
        out_shape=[pltpu.VMEM(grid_rows.shape, BF16), matrices(1, width)],
        scratch_shapes=fetch_scratch(1, width) + [pltpu.SemaphoreType.DMA((1,))],
        compiler_params=LIMIT,
        name="grid_receivers",
    )(grid_rows, weights["edge_bias"], weights["edge_first"], weights["edge_second"])


def decode_local_kernel(
    section, target_ref, table_ref, edges_ref, after_ref, node_first, node_second, pre_ref, later, arrived
):
    copies = fetch(
        [node_second.at[section], node_first.at[section, 0], node_first.at[section, 1]], later, arrived
    )
    count = target_ref.shape[0]
    block = math_block(count, 512)
    for start in range(0, count, block):
        target = target_ref[start : start + block].astype(F32)
        for sender in range(edges_ref.shape[1]):
            ids = column(edges_ref[0, sender : sender + 1, start : start + block])
            pre = dot(one_hot(ids, table_ref.shape[0]), table_ref[...]) + target
            pre_ref[sender, start : start + block] = pre.astype(BF16)
    copies[0].wait()
    later[0] = centred(later[0])
    for copy in copies[1:]:
        copy.wait()


def decode_local(target, table, edges, after, weights, section):
    count, width = target.shape
    senders = edges.shape[1]
    vmem = pl.BlockSpec(memory_space=pltpu.VMEM)
    return pl.pallas_call(
        functools.partial(decode_local_kernel, section),
        in_specs=[vmem] * 3 + [pl.BlockSpec(memory_space=pl.ANY), HBM, HBM],
        out_shape=[pltpu.VMEM((senders, count, width), BF16), matrices(3, width)],
        scratch_shapes=[pltpu.SemaphoreType.DMA((3,))],
        compiler_params=LIMIT,
        name="decode_local",
    )(near(target), near(table), edges, after, weights["node_first"], weights["node_second"])


def decode_kernel(section, places, split, *refs):
    pre_ref, second, layers, grid_ref, edges_ref = refs[:5]
    remote = refs[5 : 5 + len(places)]
    gain_ref, node_bias_ref, node_gain_ref, out_ref, table, ready, sent = refs[5 + len(places) :]
    place_remote(table, remote, places, 0)
    count = grid_ref.shape[0]
    block = math_block(count, 512)
    copies = []
    for index, start in enumerate(range(0, count, block)):
        part = slice(start, start + block)
        summed = None
        for sender in range(edges_ref.shape[1]):
            ids = column(edges_ref[0, sender : sender + 1, part])
            pre = pre_ref[sender, part].astype(F32) + dot(one_hot(ids, table.shape[0], split), table[...])
            message = normed(dot(silu(pre), second[0])).astype(BF16).astype(F32)
            summed = message if summed is None else summed + message
        rows = grid_ref[part]
        summed = (summed * row_of(gain_ref, section)).astype(BF16)
        inner = dot(rows, layers[1]) + dot(summed, layers[2]) + row_of(node_bias_ref, section)
        update = normed(dot(silu(inner), layers[0])) * row_of(node_gain_ref, section)
        ready[part] = (rows.astype(F32) + update).astype(BF16)
        copies.append(pltpu.make_async_copy(ready.at[part], out_ref.at[part], sent.at[index]))
        copies[-1].start()
    for copy in copies:
        copy.wait()


def decode_part(prepared, grid_rows, edges, remote, places, weights, section, split):
    count, width = grid_rows.shape
    table_rows = sum(r.shape[0] * r.shape[1] for r in remote)
    vmem = pl.BlockSpec(memory_space=pltpu.VMEM)
    return pl.pallas_call(
        functools.partial(decode_kernel, section, places, split),
        in_specs=[vmem] * (8 + len(remote)),
        out_specs=pl.BlockSpec(memory_space=pl.ANY),
        out_shape=jax.ShapeDtypeStruct((count, width), BF16),
        scratch_shapes=[
            pltpu.VMEM((table_rows, width), BF16),
            pltpu.VMEM((count, width), BF16),
            pltpu.SemaphoreType.DMA((count // math_block(count, 512),)),
        ],
        compiler_params=LIMIT,
        name="decode_part",
    )(
        *[near(value) for value in prepared], grid_rows, edges, *remote,
        weights["edge_gain"], weights["node_bias"], weights["node_gain"],
    )


def move(value, target):
    bands, sectors = lax.axis_size("aa"), lax.axis_size("ba")
    pairs = []
    for i in range(bands):
        for j in range(sectors):
            place = target(i, j)
            if place is None:
                continue
            band, sector = place
            pairs.append((i * sectors + j, band % bands * sectors + sector % sectors))
    return lax.ppermute(value, AXES, pairs)


def join_kernel(up_ref, down_ref, right_ref, left_ref, after_ref, right_out, left_out):
    for index, (own, out) in enumerate(((right_ref, right_out), (left_ref, left_out))):
        out[0] = own[0]
        out[1] = up_ref[index]
        out[2] = down_ref[index]


def halo(up, down, right, left, after):
    from_up = move(up, lambda i, j: (i + 1, j))
    from_down = move(down, lambda i, j: (i - 1, j))
    joined = jax.ShapeDtypeStruct((3,) + right.shape[1:], BF16)
    right, left = pl.pallas_call(
        join_kernel,
        in_specs=[pl.BlockSpec(memory_space=pltpu.VMEM)] * 4 + [pl.BlockSpec(memory_space=pl.ANY)],
        out_shape=[joined, joined],
        compiler_params=LIMIT,
        name="join",
    )(from_up, from_down, right, left, after)
    from_left = move(right, lambda i, j: (i, j + 1))
    from_right = move(left, lambda i, j: (i, j - 1))
    blocks = [from_up[2:3], from_down[2:3], from_left, from_right]
    return blocks, ((1,), (6,), (3, 0, 5), (4, 2, 7)), right


def per_device(
    grid_nodes, mesh_nodes, owned_nodes, grid_rim, mesh_rim, long_send, g2m_edges, short_edges,
    long_edges, m2g_edges, edge_first, edge_second, edge_bias, edge_gain, node_first, node_second,
    node_bias, node_gain,
):
    weights = dict(
        edge_bias=edge_bias, edge_gain=edge_gain, node_bias=node_bias, node_gain=node_gain,
        edge_first=stay(edge_first), edge_second=stay(edge_second),
        node_first=stay(node_first), node_second=stay(node_second),
    )
    width = grid_nodes.shape[1]
    slots = mesh_nodes.shape[0]
    depth = mesh_rim.shape[2]
    peers, listed = long_send.shape[1:]

    long_lists = long_send.reshape(1, peers * listed)
    rim_sends = send_shapes(depth, width)
    remote, joined, tile, kept = grid_halo(grid_nodes, grid_rim, mesh_nodes, g2m_edges, weights, 0)
    prepared = encode_local(tile, kept, joined, weights, 0)
    mesh_one, proj, *sends = encode(prepared, kept, remote, mesh_rim, depth, grid_nodes.shape[0])

    target, inner = receivers(mesh_one, weights, 1)
    remote, places, joined = halo(*sends, target)
    prepared = target, inner, layers(joined, weights, 1)
    mesh_two, proj, sent = round_part(
        short_edges, proj, prepared, mesh_one, remote, places, long_lists, owned_nodes,
        [jax.ShapeDtypeStruct((peers * listed, width), BF16)], weights, 1,
    )

    sent = sent.reshape(peers, listed, width)
    arrived = lax.all_to_all(sent, AXES, split_axis=0, concat_axis=0, tiled=True)
    prepared = prepare(mesh_two, weights, 2)
    mesh_out, proj, *sends = round_part(
        long_edges, proj, prepared, mesh_two, [arrived.reshape(1, peers * listed, width)], ((0,),),
        mesh_rim, owned_nodes, rim_sends, weights, 2,
    )

    target, second = grid_receivers(grid_nodes, weights, 3)
    remote, places, joined = halo(*sends, target)
    pre, stack = decode_local(target, proj, m2g_edges, joined, weights, 3)
    grid_out = decode_part(
        (pre, second, stack), grid_nodes, m2g_edges, remote, places, weights, 3, slots
    )
    return grid_out, mesh_out


def solution(mesh):
    rows = P(AXES, None)
    lists = P(AXES, None, None)
    in_specs = (rows, rows, P(AXES)) + (lists,) * 7 + (P(),) * 8
    return jax.shard_map(
        per_device, mesh=mesh, in_specs=in_specs, out_specs=(rows, rows), check_vma=False
    )
```

```python
import functools

import jax
import jax.numpy as jnp
from jax import lax
from jax.experimental import pallas as pl
from jax.experimental.pallas import tpu as pltpu
from jax.sharding import PartitionSpec as P

EPSILON = 1e-05
AXES = ("aa", "ba")
LANES = 128
BF16 = jnp.bfloat16
F32 = jnp.float32
LIMIT = pltpu.CompilerParams(vmem_limit_bytes=20 * 1024 * 1024)

UP_LISTS = (7, 5, 6)
DOWN_LISTS = (2, 0, 1)
RIGHT_LIST = 4
LEFT_LIST = 3
SEND_ORDER = UP_LISTS + DOWN_LISTS + (RIGHT_LIST, LEFT_LIST)


def dot(left, right):
    return jnp.dot(left, right, preferred_element_type=F32)


def math_block(total, most):
    block = most
    while total % block:
        block -= LANES
    return block


def round_up(value, unit):
    return -(-value // unit) * unit


def column(row):
    tall = jnp.broadcast_to(row, (LANES, row.shape[1]))
    return jnp.transpose(tall).astype(jnp.int16)


def one_hot(ids, width, base=0):
    lane = lax.broadcasted_iota(jnp.int16, ids.shape, 1)
    parts = [
        jnp.where(ids == lane + jnp.int16(base + start), BF16(1), BF16(0))
        for start in range(0, width, LANES)
    ]
    return parts[0] if len(parts) == 1 else jnp.concatenate(parts, 1)


def silu(value):
    half = (0.5 * value).astype(BF16)
    return half + half * jnp.tanh(half)


def centred(weight):
    weight = weight.astype(F32)
    return (weight - jnp.mean(weight, axis=-1, keepdims=True)).astype(BF16)


def normed(value):
    spread = jnp.mean(value * value, axis=-1, keepdims=True)
    return value * lax.rsqrt(spread + EPSILON)


def whole(shape):
    return pl.BlockSpec(shape, lambda *_: (0,) * len(shape))


def cost(macs, moved):
    return pl.CostEstimate(flops=2 * macs, bytes_accessed=moved, transcendentals=0)


HBM = pl.BlockSpec(memory_space=pltpu.HBM)
SMEM = pl.BlockSpec(memory_space=pltpu.SMEM)


def stay(stack):
    return pltpu.with_memory_space_constraint(stack, pltpu.HBM)


def near(value):
    return pltpu.with_memory_space_constraint(value, pltpu.VMEM)


def held(value, section):
    return pltpu.with_memory_space_constraint(value, place_of(section))


def place_of(section):
    return pltpu.HBM if section == 2 else pltpu.VMEM


def fetch(sources, buffers, arrived):
    copies = [
        pltpu.make_async_copy(source, buffers.at[i], arrived.at[i]) for i, source in enumerate(sources)
    ]
    for copy in copies:
        copy.start()
    return copies


def fetch_scratch(count, width):
    return [pltpu.VMEM((count, width, width), BF16), pltpu.SemaphoreType.DMA((count,))]


def matrices(count, width):
    return pltpu.VMEM((count, width, width), BF16)


def fill(ref, value):
    rows = value.shape[0]
    ref[:rows] = value
    if ref.shape[0] > rows:
        ref[rows:] = jnp.zeros((ref.shape[0] - rows, ref.shape[1]), ref.dtype)


def clear_tail(ref, rows):
    ref[rows:] = jnp.zeros((ref.shape[0] - rows, ref.shape[1]), ref.dtype)


def row_of(ref, index):
    return ref[index : index + 1]


def added(pre, targets, second, slots):
    hidden = silu(pre)
    message = normed(dot(hidden, second)).astype(BF16)
    member = lax.broadcasted_iota(jnp.int32, (slots, targets.shape[1]), 0) == targets
    return dot(member.astype(BF16), message)


def updated(rows, total, inner, first, second, gain):
    inner = inner + dot(total.astype(BF16), first)
    update = normed(dot(silu(inner), second)) * gain
    return (rows.astype(F32) + update).astype(BF16)


def side_base():
    return jnp.where(lax.axis_index("aa") % 2 == 0, 5, 0)


def send_shapes(depth, width):
    return [jax.ShapeDtypeStruct((n, depth, width), BF16) for n in (3, 3, 1, 1)]


def list_rows(proj_out, lists_ref, sends):
    if len(lists_ref.shape) == 3:
        ids = jnp.concatenate([column(lists_ref[0, m : m + 1]) for m in SEND_ORDER], 0)
    else:
        ids = column(lists_ref[...])
    listed = ids.shape[0]
    size = math_block(listed, 256)
    made = []
    for start in range(0, listed, size):
        picked = one_hot(ids[start : start + size], proj_out.shape[0])
        made.append(dot(picked, proj_out[...]).astype(BF16))
    made = made[0] if len(made) == 1 else jnp.concatenate(made, 0)
    place = 0
    for ref in sends:
        if len(ref.shape) == 2:
            ref[...] = made
            continue
        depth = ref.shape[1]
        for index in range(ref.shape[0]):
            ref[index] = made[place : place + depth]
            place += depth


def pick_pair_kernel(rows_hbm, rim_hbm, pair_out, rows, rim, rows_here, rim_here):
    depth = rim.shape[2]
    parts = rows_here.shape[0]
    size = rows.shape[0] // parts
    copies = [pltpu.make_async_copy(rim_hbm, rim, rim_here.at[0])]
    for part in range(parts):
        span = pl.ds(part * size, size)
        copies.append(pltpu.make_async_copy(rows_hbm.at[span], rows.at[span], rows_here.at[part]))
    for copy in copies:
        copy.start()
    pair = side_base()
    copies[0].wait()
    ids = [column(rim[0, pl.ds(pair + offset, 1), :]) for offset in (2, 0, 1)]
    picked = [None] * len(ids)
    for part in range(parts):
        copies[part + 1].wait()
        values = rows[part * size : (part + 1) * size]
        for index, listed in enumerate(ids):
            found = dot(one_hot(listed, size, part * size), values)
            picked[index] = found if part == 0 else picked[index] + found
    for index, found in enumerate(picked):
        pair_out[index * depth : (index + 1) * depth] = found.astype(BF16)


def pick_pair(rows, rim):
    count, width = rows.shape
    parts = count // 256 if count % 256 == 0 else 1
    return pl.pallas_call(
        pick_pair_kernel,
        in_specs=[HBM, HBM],
        out_shape=[
            pltpu.VMEM((3 * rim.shape[2], width), BF16),
            pltpu.VMEM((count, width), BF16),
            pltpu.VMEM(rim.shape, jnp.int32),
        ],
        scratch_shapes=[pltpu.SemaphoreType.DMA((parts,)), pltpu.SemaphoreType.DMA((1,))],
        compiler_params=LIMIT,
        name="pick_pair",
    )(stay(rows), stay(rim))


def pick_outer_kernel(rows_ref, rim_ref, after_ref, *outs):
    outer = 5 - side_base()
    for out, offset in zip(outs, (2, 0, 1)):
        ids = column(rim_ref[0, pl.ds(outer + offset, 1), :])
        out[...] = dot(one_hot(ids, rows_ref.shape[0]), rows_ref[...]).astype(BF16)


def pick_outer(rows, rim, after):
    vmem = pl.BlockSpec(memory_space=pltpu.VMEM)
    return pl.pallas_call(
        pick_outer_kernel,
        in_specs=[vmem, vmem, pl.BlockSpec(memory_space=pl.ANY)],
        out_shape=[pltpu.VMEM((rim.shape[2], rows.shape[1]), BF16)] * 3,
        compiler_params=LIMIT,
        name="pick_outer",
    )(near(rows), near(rim), after)


def pick_rest_kernel(section, rows_ref, rim_ref, edge_first, node_first, mesh_hbm, edges_hbm, *refs):
    vectors, refs = refs[:4], refs[4:]
    outs, (stack, mesh, edges, rows_of, arrived, mesh_here, edges_here, vectors_here) = refs[:2], refs[2:]
    copies = fetch(
        [edge_first.at[section, 1], edge_first.at[section, 0], node_first.at[section, 0]], stack, arrived
    )
    copies.append(pltpu.make_async_copy(mesh_hbm, mesh, mesh_here.at[0]))
    copies.append(pltpu.make_async_copy(edges_hbm, edges, edges_here.at[0]))
    for index, vector in enumerate(vectors):
        copies.append(
            pltpu.make_async_copy(
                vector.at[pl.ds(section, 1)], rows_of.at[pl.ds(index, 1)], vectors_here.at[index]
            )
        )
    for copy in copies[3:]:
        copy.start()
    for out, chosen in zip(outs, (RIGHT_LIST, LEFT_LIST)):
        ids = column(rim_ref[0, pl.ds(chosen, 1), :])
        out[...] = dot(one_hot(ids, rows_ref.shape[0]), rows_ref[...]).astype(BF16)
    for copy in copies:
        copy.wait()


def pick_rest(rows, rim, mesh_rows, edges, weights, section):
    width = rows.shape[1]
    vmem = pl.BlockSpec(memory_space=pltpu.VMEM)
    return pl.pallas_call(
        functools.partial(pick_rest_kernel, section),
        in_specs=[vmem] * 2 + [HBM] * 8,
        out_shape=[pltpu.VMEM((rim.shape[2], width), BF16)] * 2
        + [
            matrices(3, width),
            pltpu.VMEM(mesh_rows.shape, BF16),
            pltpu.VMEM(edges.shape, edges.dtype),
            pltpu.VMEM((4, width), F32),
        ],
        scratch_shapes=[pltpu.SemaphoreType.DMA((n,)) for n in (3, 1, 1, 4)],
        compiler_params=LIMIT,
        name="pick_rest",
    )(
        near(rows), near(rim), weights["edge_first"], weights["node_first"], stay(mesh_rows), stay(edges),
        stay(weights["edge_bias"]), stay(weights["node_bias"]), stay(weights["edge_gain"]),
        stay(weights["node_gain"]),
    )


def pair_join_kernel(pair_ref, right_ref, left_ref, right_out, left_out):
    depth = right_ref.shape[0]
    for index, (own, out) in enumerate(((right_ref, right_out), (left_ref, left_out))):
        out[:depth] = own[...]
        out[depth:] = pair_ref[index * depth : (index + 1) * depth]


def pair_join(pair, right, left):
    depth, width = right.shape
    return pl.pallas_call(
        pair_join_kernel,
        out_shape=[pltpu.VMEM((2 * depth, width), BF16)] * 2,
        compiler_params=LIMIT,
        name="pair_join",
    )(pair, right, left)


def grid_halo(rows, rim, mesh_rows, edges, weights, section):
    pair, rows, rim = pick_pair(rows, rim)
    pair = move(pair, lambda i, j: (i ^ 1, j))
    right, left, *kept = pick_rest(rows, rim, mesh_rows, edges, weights, section)
    right, left = pair_join(pair, right, left)
    outer = pick_outer(rows, rim, right)
    bands = lax.axis_size("aa")
    other = lambda i: i + 1 if i % 2 else i - 1
    inside = lambda i: 0 <= other(i) < bands
    remote = [
        pair,
        move(right, lambda i, j: (i, j + 1)),
        move(left, lambda i, j: (i, j - 1)),
        move(outer[0], lambda i, j: (other(i), j + 1) if inside(i) else None),
        move(outer[1], lambda i, j: (other(i), j - 1) if inside(i) else None),
        move(outer[2], lambda i, j: (other(i), j)),
    ]
    return remote, right, rows, kept


def encode_local_kernel(
    section, grid_ref, stack, mesh_ref, edges_ref, vectors, after_ref,
    edge_first, edge_second, node_first, node_second, pre_out, inner_out, later, table, target, arrived,
):
    copies = fetch(
        [
            edge_first.at[section, 0], edge_second.at[section], node_first.at[section, 1],
            node_second.at[section], edge_first.at[section + 1, 0],
        ],
        later, arrived,
    )
    rows = mesh_ref[...]
    fill(target, (dot(rows, stack[0]) + row_of(vectors, 0)).astype(BF16))
    fill(table, dot(grid_ref[...], stack[1]).astype(BF16))
    inner_out[...] = dot(rows, stack[2]) + row_of(vectors, 1)
    edges = edges_ref.shape[2]
    block = math_block(edges, 1024)
    for start in range(0, edges, block):
        part = slice(start, start + block)
        senders = column(edges_ref[0, 0:1, part])
        targets = column(edges_ref[0, 1:2, part])
        pre_out[part] = dot(one_hot(senders, table.shape[0]), table[...]) + dot(
            one_hot(targets, target.shape[0]), target[...]
        )
    for copy in copies:
        copy.wait()
    later[1] = centred(later[1])
    later[3] = centred(later[3])


def encode_local(grid_rows, kept, after, weights, section):
    stack, mesh_rows, edges, vectors = [near(value) for value in kept]
    total = edges.shape[2]
    count, width = grid_rows.shape
    slots = mesh_rows.shape[0]
    vmem = pl.BlockSpec(memory_space=pltpu.VMEM)
    return pl.pallas_call(
        functools.partial(encode_local_kernel, section),
        in_specs=[vmem] * 5 + [pl.BlockSpec(memory_space=pl.ANY)] + [HBM] * 4,
        out_shape=[
            pltpu.VMEM((total, width), F32),
            pltpu.VMEM((slots, width), F32),
            matrices(5, width),
        ],
        scratch_shapes=[
            pltpu.VMEM((round_up(count, LANES), width), BF16),
            pltpu.VMEM((round_up(slots, LANES), width), BF16),
            pltpu.SemaphoreType.DMA((5,)),
        ],
        compiler_params=LIMIT,
        name="encode_local",
    )(
        near(grid_rows), stack, mesh_rows, edges, vectors, after,
        weights["edge_first"], weights["edge_second"], weights["node_first"], weights["node_second"],
    )


def encode_kernel(count, *refs):
    pre_ref, edges_ref, stack, inner_ref, mesh_ref = refs[:5]
    pair_ref, right_ref, left_ref, outer_right, outer_left, outer_ref = refs[5:11]
    vectors, lists_ref = refs[11:13]
    mesh_out, proj_out, up, down, right, left, table = refs[13:]
    slots = mesh_ref.shape[0]
    depth = outer_ref.shape[0]
    pair = side_base()
    outer = 5 - pair
    for ref, start, direction in (
        (pair_ref, 2 * depth, pair + 1),
        (right_ref, 0, 3),
        (right_ref, depth, pair),
        (left_ref, 0, 4),
        (left_ref, depth, pair + 2),
        (outer_right, 0, outer),
        (outer_left, 0, outer + 2),
        (outer_ref, 0, outer + 1),
    ):
        place = pl.multiple_of(direction * depth, LANES)
        table[pl.ds(place, depth)] = dot(ref[start : start + depth], stack[0]).astype(BF16)
    edges = pre_ref.shape[0]
    block = math_block(edges, 1024)
    summed = None
    for start in range(0, edges, block):
        part = slice(start, start + block)
        senders = column(edges_ref[0, 0:1, part] - count)
        pre = pre_ref[part] + dot(one_hot(senders, table.shape[0]), table[...])
        made = added(pre, edges_ref[0, 1:2, part], stack[1], slots)
        summed = made if summed is None else summed + made
    summed = summed * row_of(vectors, 2)
    fresh = updated(mesh_ref[...], summed, inner_ref[...], stack[2], stack[3], row_of(vectors, 3))
    mesh_out[...] = fresh
    fill(proj_out, dot(fresh, stack[4]).astype(BF16))
    list_rows(proj_out, lists_ref, (up, down, right, left))


def encode(prepared, kept, remote, lists, depth, count):
    pre, inner, stack = [near(value) for value in prepared]
    mesh_rows, edges, vectors = [near(value) for value in kept[1:]]
    slots, width = mesh_rows.shape
    return pl.pallas_call(
        functools.partial(encode_kernel, count),
        out_shape=[
            pltpu.VMEM((slots, width), BF16),
            pltpu.VMEM((round_up(slots, LANES), width), BF16),
        ]
        + send_shapes(depth, width),
        scratch_shapes=[pltpu.VMEM((8 * remote[-1].shape[0], width), BF16)],
        compiler_params=LIMIT,
        name="encode",
    )(pre, edges, stack, inner, mesh_rows, *remote, vectors, lists)


def prepare_kernel(
    section, mesh_ref, bias_ref, node_bias_ref, edge_first, edge_second, node_first, node_second,
    target_out, inner_out, later, own, arrived, later_arrived,
):
    copies = fetch([edge_first.at[section, 1], node_first.at[section, 0]], own, arrived)
    copies += fetch(
        [
            edge_second.at[section], node_second.at[section], node_first.at[section, 1],
            edge_first.at[section + 1, 0],
        ],
        later, later_arrived,
    )
    rows = mesh_ref[...]
    copies[0].wait()
    fill(target_out, (dot(rows, own[0]) + row_of(bias_ref, section)).astype(BF16))
    copies[1].wait()
    inner_out[...] = dot(rows, own[1]) + row_of(node_bias_ref, section)
    for copy in copies[2:]:
        copy.wait()
    later[0] = centred(later[0])
    later[1] = centred(later[1])


def prepare(mesh_rows, weights, section):
    slots, width = mesh_rows.shape
    vmem = pl.BlockSpec(memory_space=pltpu.VMEM)
    return pl.pallas_call(
        functools.partial(prepare_kernel, section),
        in_specs=[vmem] * 3 + [HBM] * 4,
        out_shape=[
            place_of(section)((round_up(slots, LANES), width), BF16),
            place_of(section)((slots, width), F32),
            matrices(4, width),
        ],
        scratch_shapes=fetch_scratch(2, width) + [pltpu.SemaphoreType.DMA((4,))],
        compiler_params=LIMIT,
        name="prepare",
    )(
        held(mesh_rows, section), weights["edge_bias"], weights["node_bias"],
        weights["edge_first"], weights["edge_second"], weights["node_first"], weights["node_second"],
    )


def receivers_kernel(section, mesh_ref, bias_ref, node_bias_ref, edge_first, node_first, target_out, inner_out, own, arrived):
    copies = fetch([edge_first.at[section, 1], node_first.at[section, 0]], own, arrived)
    rows = mesh_ref[...]
    copies[0].wait()
    fill(target_out, (dot(rows, own[0]) + row_of(bias_ref, section)).astype(BF16))
    copies[1].wait()
    inner_out[...] = dot(rows, own[1]) + row_of(node_bias_ref, section)


def receivers(mesh_rows, weights, section):
    slots, width = mesh_rows.shape
    vmem = pl.BlockSpec(memory_space=pltpu.VMEM)
    return pl.pallas_call(
        functools.partial(receivers_kernel, section),
        in_specs=[vmem] * 3 + [HBM] * 2,
        out_shape=[pltpu.VMEM((round_up(slots, LANES), width), BF16), pltpu.VMEM((slots, width), F32)],
        scratch_shapes=fetch_scratch(2, width),
        compiler_params=LIMIT,
        name="receivers",
    )(near(mesh_rows), weights["edge_bias"], weights["node_bias"], weights["edge_first"], weights["node_first"])


def layers_kernel(section, after_ref, edge_first, edge_second, node_first, node_second, later, arrived):
    copies = fetch(
        [
            edge_second.at[section], node_second.at[section], node_first.at[section, 1],
            edge_first.at[section + 1, 0],
        ],
        later, arrived,
    )
    for index in (0, 1):
        copies[index].wait()
        later[index] = centred(later[index])
    for copy in copies[2:]:
        copy.wait()


def layers(after, weights, section):
    width = after.shape[-1]
    return pl.pallas_call(
        functools.partial(layers_kernel, section),
        in_specs=[pl.BlockSpec(memory_space=pl.ANY)] + [HBM] * 4,
        out_shape=matrices(4, width),
        scratch_shapes=[pltpu.SemaphoreType.DMA((4,))],
        compiler_params=LIMIT,
        name="layers",
    )(after, weights["edge_first"], weights["edge_second"], weights["node_first"], weights["node_second"])


def place_remote(table, remote, places, base):
    for ref, slots in zip(remote, places):
        depth = ref.shape[1]
        for index, slot in enumerate(slots):
            place = base + slot * depth
            table[place : place + depth] = ref[index]


def round_kernel(section, places, last, *refs):
    edges_ref, local_ref, target, inner_ref, stack, mesh_ref = refs[:6]
    remote = refs[6 : 6 + len(places)]
    gain_ref, node_gain_ref, lists_ref, owned_ref = refs[6 + len(places) : 10 + len(places)]
    rest = refs[10 + len(places) :]
    slots, padded = mesh_ref.shape[0], local_ref.shape[0]
    if last:
        table, target_here, inner_here, mesh_here, here = rest[-5:]
        rest = rest[:-5]
        copies = [
            pltpu.make_async_copy(local_ref, table.at[pl.ds(0, padded)], here.at[0]),
            pltpu.make_async_copy(target, target_here, here.at[1]),
            pltpu.make_async_copy(inner_ref, inner_here, here.at[2]),
            pltpu.make_async_copy(mesh_ref, mesh_here, here.at[3]),
        ]
        for copy in copies[:2]:
            copy.start()
        target, inner_ref, mesh_ref = target_here, inner_here, mesh_here
    else:
        table = rest[-1]
        rest = rest[:-1]
        table[:padded] = local_ref[...]
    mesh_out, proj_out = rest[:2]
    sends = rest[2:]
    place_remote(table, remote, places, padded)
    waiting = copies if last else []
    edges = edges_ref.shape[2]
    block = math_block(edges, 1536)
    summed = None
    for start in range(0, edges, block):
        senders = edges_ref[0, 0:1, start : start + block]
        targets = edges_ref[0, 1:2, start : start + block]
        senders = column(senders)
        pre = dot(one_hot(senders, table.shape[0] - padded, slots), table[padded:])
        for copy in waiting[:2]:
            copy.wait()
        for copy in waiting[2:]:
            copy.start()
        waiting = []
        own = jnp.where(senders < slots, senders, jnp.int16(-1))
        pre = pre + dot(one_hot(own, padded), table[:padded])
        pre = pre + dot(one_hot(column(targets), padded), target[...])
        part = added(pre, targets, stack[0], slots)
        summed = part if summed is None else summed + part
    summed = summed * row_of(gain_ref, section)
    for copy in copies[2:] if last else []:
        copy.wait()
    fresh = updated(mesh_ref[...], summed, inner_ref[...], stack[2], stack[1], row_of(node_gain_ref, section))
    if last:
        alive = lax.broadcasted_iota(jnp.int32, fresh.shape, 0) < owned_ref[0]
        mesh_out[...] = jnp.where(alive, fresh, jnp.zeros_like(fresh))
    else:
        mesh_out[...] = fresh
    fill(proj_out, dot(fresh, stack[3]).astype(BF16))
    list_rows(proj_out, lists_ref, sends)


def round_part(edges, local, prepared, mesh_rows, remote, places, lists, owned, sends, weights, section):
    slots, width = mesh_rows.shape
    last = section == 2
    padded = local.shape[0]
    table_rows = padded + sum(r.shape[0] * r.shape[1] for r in remote)
    space = place_of(section + 1)
    out_shape = [
        jax.ShapeDtypeStruct((slots, width), BF16) if last else space((slots, width), BF16),
        space((padded, width), BF16),
    ]
    scratch = [pltpu.VMEM((table_rows, width), BF16)]
    if last:
        scratch += [pltpu.VMEM(value.shape, value.dtype) for value in (*prepared[:2], mesh_rows)]
        scratch.append(pltpu.SemaphoreType.DMA((4,)))
    vmem = pl.BlockSpec(memory_space=pltpu.VMEM)
    return pl.pallas_call(
        functools.partial(round_kernel, section, places, last),
        in_specs=[vmem] + [HBM if last else vmem] * 3 + [vmem] + [HBM if last else vmem]
        + [vmem] * (3 + len(remote))
        + [SMEM],
        out_shape=out_shape + sends,
        scratch_shapes=scratch,
        compiler_params=LIMIT,
        name="round_part",
    )(
        edges, held(local, section), *[held(value, section) for value in prepared[:2]], near(prepared[2]),
        held(mesh_rows, section), *remote,
        weights["edge_gain"], weights["node_gain"], lists, owned,
    )


def grid_receivers_kernel(section, grid_ref, bias_ref, edge_first, edge_second, target_out, later, own, arrived, later_arrived):
    copies = fetch([edge_first.at[section, 1]], own, arrived)
    copies += fetch([edge_second.at[section]], later, later_arrived)
    copies[0].wait()
    target_out[...] = (dot(grid_ref[...], own[0]) + row_of(bias_ref, section)).astype(BF16)
    copies[1].wait()
    later[0] = centred(later[0])


def grid_receivers(grid_rows, weights, section):
    vmem = pl.BlockSpec(memory_space=pltpu.VMEM)
    width = grid_rows.shape[1]
    return pl.pallas_call(
        functools.partial(grid_receivers_kernel, section),
        in_specs=[vmem] * 2 + [HBM] * 2,
        out_shape=[pltpu.VMEM(grid_rows.shape, BF16), matrices(1, width)],
        scratch_shapes=fetch_scratch(1, width) + [pltpu.SemaphoreType.DMA((1,))],
        compiler_params=LIMIT,
        name="grid_receivers",
    )(grid_rows, weights["edge_bias"], weights["edge_first"], weights["edge_second"])


def decode_local_kernel(
    section, target_ref, table_ref, edges_ref, after_ref, node_first, node_second, pre_ref, later, arrived
):
    copies = fetch(
        [node_second.at[section], node_first.at[section, 0], node_first.at[section, 1]], later, arrived
    )
    count = target_ref.shape[0]
    block = math_block(count, 512)
    for start in range(0, count, block):
        target = target_ref[start : start + block].astype(F32)
        for sender in range(edges_ref.shape[1]):
            ids = column(edges_ref[0, sender : sender + 1, start : start + block])
            pre = dot(one_hot(ids, table_ref.shape[0]), table_ref[...]) + target
            pre_ref[sender, start : start + block] = pre.astype(BF16)
    copies[0].wait()
    later[0] = centred(later[0])
    for copy in copies[1:]:
        copy.wait()


def decode_local(target, table, edges, after, weights, section):
    count, width = target.shape
    senders = edges.shape[1]
    vmem = pl.BlockSpec(memory_space=pltpu.VMEM)
    return pl.pallas_call(
        functools.partial(decode_local_kernel, section),
        in_specs=[vmem] * 3 + [pl.BlockSpec(memory_space=pl.ANY), HBM, HBM],
        out_shape=[pltpu.VMEM((senders, count, width), BF16), matrices(3, width)],
        scratch_shapes=[pltpu.SemaphoreType.DMA((3,))],
        compiler_params=LIMIT,
        name="decode_local",
    )(near(target), near(table), edges, after, weights["node_first"], weights["node_second"])


def decode_kernel(section, places, split, *refs):
    pre_ref, second, layers, grid_ref, edges_ref = refs[:5]
    remote = refs[5 : 5 + len(places)]
    gain_ref, node_bias_ref, node_gain_ref, out_ref, table, ready, sent = refs[5 + len(places) :]
    place_remote(table, remote, places, 0)
    count = grid_ref.shape[0]
    block = math_block(count, 512)
    copies = []
    for index, start in enumerate(range(0, count, block)):
        part = slice(start, start + block)
        summed = None
        for sender in range(edges_ref.shape[1]):
            ids = column(edges_ref[0, sender : sender + 1, part])
            pre = pre_ref[sender, part].astype(F32) + dot(one_hot(ids, table.shape[0], split), table[...])
            message = normed(dot(silu(pre), second[0])).astype(BF16).astype(F32)
            summed = message if summed is None else summed + message
        rows = grid_ref[part]
        summed = (summed * row_of(gain_ref, section)).astype(BF16)
        inner = dot(rows, layers[1]) + dot(summed, layers[2]) + row_of(node_bias_ref, section)
        update = normed(dot(silu(inner), layers[0])) * row_of(node_gain_ref, section)
        ready[part] = (rows.astype(F32) + update).astype(BF16)
        copies.append(pltpu.make_async_copy(ready.at[part], out_ref.at[part], sent.at[index]))
        copies[-1].start()
    for copy in copies:
        copy.wait()


def decode_part(prepared, grid_rows, edges, remote, places, weights, section, split):
    count, width = grid_rows.shape
    table_rows = sum(r.shape[0] * r.shape[1] for r in remote)
    vmem = pl.BlockSpec(memory_space=pltpu.VMEM)
    return pl.pallas_call(
        functools.partial(decode_kernel, section, places, split),
        in_specs=[vmem] * (8 + len(remote)),
        out_specs=pl.BlockSpec(memory_space=pl.ANY),
        out_shape=jax.ShapeDtypeStruct((count, width), BF16),
        scratch_shapes=[
            pltpu.VMEM((table_rows, width), BF16),
            pltpu.VMEM((count, width), BF16),
            pltpu.SemaphoreType.DMA((count // math_block(count, 512),)),
        ],
        compiler_params=LIMIT,
        name="decode_part",
    )(
        *[near(value) for value in prepared], grid_rows, edges, *remote,
        weights["edge_gain"], weights["node_bias"], weights["node_gain"],
    )


def move(value, target):
    bands, sectors = lax.axis_size("aa"), lax.axis_size("ba")
    pairs = []
    for i in range(bands):
        for j in range(sectors):
            place = target(i, j)
            if place is None:
                continue
            band, sector = place
            pairs.append((i * sectors + j, band % bands * sectors + sector % sectors))
    return lax.ppermute(value, AXES, pairs)


def join_kernel(up_ref, down_ref, right_ref, left_ref, after_ref, right_out, left_out):
    for index, (own, out) in enumerate(((right_ref, right_out), (left_ref, left_out))):
        out[0] = own[0]
        out[1] = up_ref[index]
        out[2] = down_ref[index]


def halo(up, down, right, left, after):
    from_up = move(up, lambda i, j: (i + 1, j))
    from_down = move(down, lambda i, j: (i - 1, j))
    joined = jax.ShapeDtypeStruct((3,) + right.shape[1:], BF16)
    right, left = pl.pallas_call(
        join_kernel,
        in_specs=[pl.BlockSpec(memory_space=pltpu.VMEM)] * 4 + [pl.BlockSpec(memory_space=pl.ANY)],
        out_shape=[joined, joined],
        compiler_params=LIMIT,
        name="join",
    )(from_up, from_down, right, left, after)
    from_left = move(right, lambda i, j: (i, j + 1))
    from_right = move(left, lambda i, j: (i, j - 1))
    blocks = [from_up[2:3], from_down[2:3], from_left, from_right]
    return blocks, ((1,), (6,), (3, 0, 5), (4, 2, 7)), right


def per_device(
    grid_nodes, mesh_nodes, owned_nodes, grid_rim, mesh_rim, long_send, g2m_edges, short_edges,
    long_edges, m2g_edges, edge_first, edge_second, edge_bias, edge_gain, node_first, node_second,
    node_bias, node_gain,
):
    weights = dict(
        edge_bias=edge_bias, edge_gain=edge_gain, node_bias=node_bias, node_gain=node_gain,
        edge_first=stay(edge_first), edge_second=stay(edge_second),
        node_first=stay(node_first), node_second=stay(node_second),
    )
    width = grid_nodes.shape[1]
    slots = mesh_nodes.shape[0]
    depth = mesh_rim.shape[2]
    peers, listed = long_send.shape[1:]

    long_lists = long_send.reshape(1, peers * listed)
    rim_sends = send_shapes(depth, width)
    remote, joined, tile, kept = grid_halo(grid_nodes, grid_rim, mesh_nodes, g2m_edges, weights, 0)
    prepared = encode_local(tile, kept, joined, weights, 0)
    mesh_one, proj, *sends = encode(prepared, kept, remote, mesh_rim, depth, grid_nodes.shape[0])

    target, inner = receivers(mesh_one, weights, 1)
    remote, places, joined = halo(*sends, target)
    prepared = target, inner, layers(joined, weights, 1)
    mesh_two, proj, sent = round_part(
        short_edges, proj, prepared, mesh_one, remote, places, long_lists, owned_nodes,
        [jax.ShapeDtypeStruct((peers * listed, width), BF16)], weights, 1,
    )

    sent = sent.reshape(peers, listed, width)
    arrived = lax.all_to_all(sent, AXES, split_axis=0, concat_axis=0, tiled=True)
    prepared = prepare(mesh_two, weights, 2)
    mesh_out, proj, *sends = round_part(
        long_edges, proj, prepared, mesh_two, [arrived.reshape(1, peers * listed, width)], ((0,),),
        mesh_rim, owned_nodes, rim_sends, weights, 2,
    )

    target, second = grid_receivers(grid_nodes, weights, 3)
    remote, places, joined = halo(*sends, target)
    pre, stack = decode_local(target, proj, m2g_edges, joined, weights, 3)
    grid_out = decode_part(
        (pre, second, stack), grid_nodes, m2g_edges, remote, places, weights, 3, slots
    )
    return grid_out, mesh_out


def solution(mesh):
    rows = P(AXES, None)
    lists = P(AXES, None, None)
    in_specs = (rows, rows, P(AXES)) + (lists,) * 7 + (P(),) * 8
    return jax.shard_map(
        per_device, mesh=mesh, in_specs=in_specs, out_specs=(rows, rows), check_vma=False
    )
```
